128 devices in a mesh: req: 8 (over z, core), mlp: 16 (over x, y).
Axes of the slice: x: 4, y: 4, z: 4, core: 2. Of those that a mesh axis runs over, the one named last changes fastest.
Arguments:
- queries: bfloat16 [384, 7168], P(('req', 'mlp')), may hold values from -36 to 36
- keys_new: bfloat16 [384, 7168], P(('req', 'mlp')), may hold values from -6 to 6
- values_new: bfloat16 [384, 7168], P(('req', 'mlp')), may hold values from -6 to 6
- resid: bfloat16 [384, 7168], P(('req', 'mlp')), may hold values from -3 to 3
- tree_mask: int32 [24, 16, 16], P('req'), may hold values from 0 to 1, as said below
- tree_size: int32 [24], P('req'), may hold values from 8 to 16, as said below
- accepted: int32 [24, 16], P('req'), may hold values from -1 to 15, as said below
- dest_slot: int32 [24], P('req'), may hold values from 0 to 15, as said below
- page_table: int32 [24, 384], P('req'), may hold values from -1 to 383, as said below
- key_cache: bfloat16 [3072, 16, 7168], P(('req', 'mlp')), may hold values from -6 to 6
- value_cache: bfloat16 [3072, 16, 7168], P(('req', 'mlp')), may hold values from -6 to 6
- w_out: bfloat16 [7168, 7168], P(('req', 'mlp')), may hold values from -0.0625 to 0.0625
- w_up: bfloat16 [7168, 28672], P(None, ('req', 'mlp')), may hold values from -0.0625 to 0.0625
- w_down: bfloat16 [28672, 7168], P(('req', 'mlp')), may hold values from -0.03125 to 0.03125
- ln_gain: float32 [7168], replicated, may hold values from 0.1 to 1.9
Outputs:
- mixed: bfloat16 [384, 7168], P(('req', 'mlp'))
- new_keys: bfloat16 [128, 16, 7168], P(('req', 'mlp'))
- new_values: bfloat16 [128, 16, 7168], P(('req', 'mlp'))
The draws below stay inside these ranges and needn't reach their ends.
Inputs may be any that keep to these rules, and one draw needn't show every extreme that they name: `tree_mask`: entry [r, i, j] is 1 where slot j is slot i or one of its ancestors in request r's draft tree, else 0; every slot's parent has a lower index, so slot 0 is the root. `tree_size`: draft slots at or beyond a request's size are padding. `accepted`: row r lists in increasing order the slots of one path from the root of request r's tree to a slot below tree_size[r], then -1. `dest_slot`: the new pages of one group's 3 requests are distinct. `page_table`: row r lists the pages of its group's pool that hold request r's cache, then -1; no page belongs to two requests, every request has 16 pages or more, and in some groups one request holds every page that the others leave.
All inputs are finite; a program needn't handle non-finite values.
Results may differ from the reference program's by a relative error of at most 0.017.
Values may be sent and summed in bfloat16 or wider, within the bound.
No kernel may reach another device: no remote copies, remote signals or barrier semaphores. Data moves between devices by JAX's collectives and lax.ppermute only.
A program may use at most 128 MiB of HBM per device.

```python
import math
import jax
import jax.numpy as jnp
from jax import lax

D = 7168
H = 56
HD = 128
FF = 28672
PAGE = 16
TREE = 16
RG = 3
SHORTP = 16
GROUPS = 8
SLOTS = 16
REQUESTS = 24
TOKENS = 384
GPOOL = 384
POOL = 3072
NEWPAGES = 128


def tree_shapes(key):
    base_key = jax.random.fold_in(key, 7)
    parent_key, size_key, node_key = jax.random.split(base_key, 3)
    slot_ids = jnp.arange(TREE, dtype=jnp.int32)
    raw_ints = jax.random.randint(parent_key, (REQUESTS, TREE), 0, 1 << 20)
    parents = raw_ints % jnp.maximum(slot_ids, 1)[None, :]
    identity = (slot_ids[:, None] == slot_ids[None, :]).astype(jnp.int32)
    ancestry = jnp.zeros((REQUESTS, TREE, TREE), jnp.int32)
    ancestry = ancestry.at[:, 0, :].set(identity[0])
    for slot_index in range(1, TREE):
        picker = jnp.broadcast_to(parents[:, slot_index][:, None, None], (REQUESTS, 1, TREE))
        parent_row = jnp.take_along_axis(ancestry, picker, axis=1)[:, 0, :]
        ancestry = ancestry.at[:, slot_index, :].set(jnp.maximum(parent_row, identity[slot_index]))
    tree_sizes = jax.random.randint(size_key, (REQUESTS,), TREE // 2, TREE + 1).astype(jnp.int32)
    tree_sizes = tree_sizes.at[0].set(TREE).at[1].set(TREE // 2)
    nodes = jax.random.randint(node_key, (REQUESTS,), 0, 1 << 20).astype(jnp.int32) % tree_sizes
    nodes = nodes.at[0].set(TREE - 1)
    return (ancestry, tree_sizes, nodes)


def draw_tree_mask(key, part):
    ancestry, tree_sizes, nodes = tree_shapes(key)
    return ancestry


def draw_tree_size(key, part):
    ancestry, tree_sizes, nodes = tree_shapes(key)
    return tree_sizes


def draw_accepted(key, part):
    ancestry, tree_sizes, nodes = tree_shapes(key)
    picker = jnp.broadcast_to(nodes[:, None, None], (REQUESTS, 1, TREE))
    path_row = jnp.take_along_axis(ancestry, picker, axis=1)[:, 0, :]
    depth = jnp.sum(path_row, axis=1)
    slot_ids = jnp.arange(TREE, dtype=jnp.int32)
    ranked = jnp.argsort(jnp.where(path_row == 1, slot_ids[None, :], TREE + slot_ids[None, :]), axis=1, stable=True).astype(jnp.int32)
    positions = jnp.arange(PAGE, dtype=jnp.int32)
    chosen = ranked[:, jnp.minimum(positions, TREE - 1)]
    return jnp.where(positions[None, :] < depth[:, None], chosen, -1).astype(jnp.int32)


def draw_dest_slot(key, part):
    base_key = jax.random.fold_in(key, 13)
    order_key, swap_key = jax.random.split(base_key, 2)
    slot_ids = jnp.arange(SLOTS, dtype=jnp.int32)
    shuffled = jnp.argsort(jax.random.randint(order_key, (GROUPS, SLOTS), 0, 1 << 20) * SLOTS + slot_ids[None, :], axis=1, stable=True).astype(jnp.int32)
    chosen = jax.random.randint(swap_key, (GROUPS,), 0, RG).astype(jnp.int32)
    holder = jnp.argmax(shuffled == SLOTS - 1, axis=1).astype(jnp.int32)
    held = jnp.take_along_axis(shuffled, chosen[:, None], axis=1)
    swapped = jnp.where(slot_ids[None, :] == holder[:, None], held, jnp.where(slot_ids[None, :] == chosen[:, None], SLOTS - 1, shuffled))
    return swapped[:, :RG].reshape(REQUESTS).astype(jnp.int32)


def draw_page_table(key, part):
    base_key = jax.random.fold_in(key, 11)
    group_key, long_key, pool_key = jax.random.split(base_key, 3)
    group_ids = jnp.arange(GROUPS, dtype=jnp.int32)
    group_order = jnp.argsort(jax.random.randint(group_key, (GROUPS,), 0, 1 << 20) * GROUPS + group_ids, stable=True)
    long_count = max(1, 3 * GROUPS // 8)
    has_long = jnp.zeros((GROUPS,), jnp.int32).at[group_order[:long_count]].set(1)
    long_member = jax.random.randint(long_key, (GROUPS,), 0, RG).astype(jnp.int32)
    member_ids = jnp.arange(RG, dtype=jnp.int32)
    long_pages = GPOOL - (RG - 1) * SHORTP
    is_long = (member_ids[None, :] == long_member[:, None]) & (has_long[:, None] == 1)
    counts = jnp.where(is_long, long_pages, SHORTP).astype(jnp.int32)
    offsets = jnp.cumsum(counts, axis=1) - counts
    pool_ids = jnp.arange(GPOOL, dtype=jnp.int32)
    shuffled = jnp.argsort(jax.random.randint(pool_key, (GROUPS, GPOOL), 0, 1 << 20) * GPOOL + pool_ids[None, :], axis=1, stable=True).astype(jnp.int32)
    spots = jnp.minimum(offsets[:, :, None] + pool_ids[None, None, :], GPOOL - 1)
    spread_pool = jnp.broadcast_to(shuffled[:, None, :], (GROUPS, RG, GPOOL))
    entries = jnp.take_along_axis(spread_pool, spots, axis=2)
    table = jnp.where(pool_ids[None, None, :] < counts[:, :, None], entries, -1)
    return table.reshape(REQUESTS, GPOOL).astype(jnp.int32)


def draw_keys_new(key, part):
    draw_key = jax.random.fold_in(key, 31)
    return jnp.clip(jax.random.normal(draw_key, (TOKENS, D)), -6.0, 6.0).astype(jnp.bfloat16)


def draw_queries(key, part):
    draw_key = jax.random.fold_in(key, 37)
    return jnp.clip(2.0 * jax.random.normal(draw_key, (TOKENS, D)), -12.0, 12.0).astype(jnp.bfloat16)


def levels(stream_key, extent, pieces, smallest, high):
    def one(dim, blocks):
        heights = jax.random.uniform(jax.random.fold_in(jax.random.fold_in(stream_key, 6), dim), (blocks,), jnp.float32, smallest / len(pieces), high / len(pieces))
        return jnp.repeat(jnp.exp(heights), extent[dim] // blocks).reshape((-1,) + (1,) * (len(extent) - dim - 1))

    level = one(*pieces[0])
    for cut in pieces[1:]:
        level = level * one(*cut)
    return level


def bell_draw(stream_key, extent, deviation, limit, pieces=(), kind=jnp.bfloat16):
    array = deviation * jax.random.normal(stream_key, extent, jnp.float32)
    if pieces:
        array = array * levels(stream_key, extent, pieces, -0.22, 0.18)
    return jnp.clip(array, -limit, limit).astype(kind)


def setup_inputs(seed: int = 0) -> dict:
    splits = jax.random.split(jax.random.key(seed), 16)
    queries = draw_queries(jax.random.fold_in(splits[15], 71), 0)
    keys_new = draw_keys_new(jax.random.fold_in(splits[15], 71), 0)
    values_new = bell_draw(splits[2], (TOKENS, D), 1.0, 6.0, ((0, 128),))
    resid = bell_draw(splits[3], (TOKENS, D), 0.5, 3.0, ((0, 128),))
    tree_mask = draw_tree_mask(jax.random.fold_in(splits[15], 71), 0)
    tree_size = draw_tree_size(jax.random.fold_in(splits[15], 71), 0)
    accepted = draw_accepted(jax.random.fold_in(splits[15], 71), 0)
    dest_slot = draw_dest_slot(jax.random.fold_in(splits[15], 71), 0)
    page_table = draw_page_table(jax.random.fold_in(splits[15], 71), 0)
    key_cache = bell_draw(splits[9], (POOL, PAGE, D), 1.0, 6.0, ((0, 128),))
    value_cache = bell_draw(splits[10], (POOL, PAGE, D), 1.0, 6.0, ((0, 128),))
    w_out = bell_draw(splits[11], (D, D), D ** -0.5, 0.0625, ((0, 128),))
    w_up = bell_draw(splits[12], (D, FF), D ** -0.5, 0.0625, ((1, 128),))
    w_down = bell_draw(splits[13], (FF, D), FF ** -0.5, 0.03125, ((0, 128),))
    ln_gain = jnp.clip(1.0 + 0.18 * jax.random.normal(splits[14], (D,), jnp.float32), 0.1, 1.9)
    return {"queries": queries, "keys_new": keys_new, "values_new": values_new, "resid": resid, "tree_mask": tree_mask, "tree_size": tree_size, "accepted": accepted, "dest_slot": dest_slot, "page_table": page_table, "key_cache": key_cache, "value_cache": value_cache, "w_out": w_out, "w_up": w_up, "w_down": w_down, "ln_gain": ln_gain}


def reference(queries, keys_new, values_new, resid, tree_mask, tree_size, accepted, dest_slot, page_table, key_cache, value_cache, w_out, w_up, w_down, ln_gain):
    group_rows = RG * TREE
    scaling = 1.0 / math.sqrt(HD)

    def group_attention(group):
        offset = (group * group_rows).astype(jnp.int32)
        first_req = (group * RG).astype(jnp.int32)
        first_page = (group * GPOOL).astype(jnp.int32)
        query_rows = lax.dynamic_slice_in_dim(queries, offset, group_rows, 0).astype(jnp.float32).reshape(group_rows, H, HD)
        draft_keys = lax.dynamic_slice_in_dim(keys_new, offset, group_rows, 0).astype(jnp.float32).reshape(group_rows, H, HD)
        draft_vals = lax.dynamic_slice_in_dim(values_new, offset, group_rows, 0).astype(jnp.float32).reshape(group_rows, H, HD)
        page_rows = lax.dynamic_slice_in_dim(page_table, first_req, RG, 0)
        tree_masks = lax.dynamic_slice_in_dim(tree_mask, first_req, RG, 0)
        tree_sizes = lax.dynamic_slice_in_dim(tree_size, first_req, RG, 0)
        pool_keys = lax.dynamic_slice_in_dim(key_cache, first_page, GPOOL, 0).astype(jnp.float32).reshape(GPOOL * PAGE, H, HD)
        pool_vals = lax.dynamic_slice_in_dim(value_cache, first_page, GPOOL, 0).astype(jnp.float32).reshape(GPOOL * PAGE, H, HD)
        page_ids = jnp.arange(GPOOL, dtype=jnp.int32)
        owners = jnp.any(page_rows[:, :, None] == page_ids[None, None, :], axis=1)
        owner_tokens = jnp.repeat(owners, PAGE, axis=1)
        row_req = jnp.arange(group_rows, dtype=jnp.int32) // TREE
        req_ids = jnp.arange(RG, dtype=jnp.int32)
        pool_ok = jnp.any((row_req[:, None, None] == req_ids[None, :, None]) & owner_tokens[None], axis=1)
        key_slot = jnp.arange(group_rows, dtype=jnp.int32) % TREE
        draft_ok = (row_req[:, None] == row_req[None, :]) & (jnp.tile(tree_masks.reshape(group_rows, TREE), (1, RG)) == 1) & (key_slot[None, :] < jnp.repeat(tree_sizes, TREE)[None, :])
        pool_scores = jnp.einsum('qhd,khd->hqk', query_rows, pool_keys) * scaling
        pool_scores = jnp.where(pool_ok[None], pool_scores, -jnp.inf)
        draft_scores = jnp.einsum('qhd,khd->hqk', query_rows, draft_keys) * scaling
        draft_scores = jnp.where(draft_ok[None], draft_scores, -jnp.inf)
        row_max = jnp.maximum(lax.optimization_barrier(jnp.max(pool_scores, axis=2)), lax.optimization_barrier(jnp.max(draft_scores, axis=2)))
        pool_weights = jnp.exp(pool_scores - row_max[:, :, None])
        draft_weights = jnp.exp(draft_scores - row_max[:, :, None])
        total = lax.optimization_barrier(jnp.sum(pool_weights, axis=2)) + lax.optimization_barrier(jnp.sum(draft_weights, axis=2))
        pool_half = pool_weights.astype(jnp.bfloat16).astype(jnp.float32)
        draft_half = draft_weights.astype(jnp.bfloat16).astype(jnp.float32)
        weighted = jnp.einsum('hqk,khd->qhd', pool_half, pool_vals) + jnp.einsum('hqk,khd->qhd', draft_half, draft_vals)
        attended = weighted / jnp.transpose(total)[:, :, None]
        return attended.reshape(group_rows, D).astype(jnp.bfloat16)
    attended = lax.map(group_attention, jnp.arange(GROUPS, dtype=jnp.int32)).reshape(TOKENS, D)
    hidden = resid.astype(jnp.float32) + jnp.dot(attended, w_out, preferred_element_type=jnp.float32)
    row_mean = lax.optimization_barrier(jnp.mean(hidden, axis=1, keepdims=True))
    centered = hidden - row_mean
    spread = lax.optimization_barrier(jnp.mean(centered * centered, axis=1, keepdims=True))
    normed = (centered * lax.rsqrt(spread + 1e-05) * ln_gain).astype(jnp.bfloat16)
    activation = jnp.maximum(jnp.dot(normed, w_up, preferred_element_type=jnp.float32), 0.0).astype(jnp.bfloat16)
    mixed = (hidden + jnp.dot(activation, w_down, preferred_element_type=jnp.float32)).astype(jnp.bfloat16)
    valid_rows = accepted >= 0
    source_rows = jnp.arange(REQUESTS, dtype=jnp.int32)[:, None] * TREE + jnp.maximum(accepted, 0)
    targets = jnp.arange(REQUESTS, dtype=jnp.int32) // RG * SLOTS + dest_slot
    key_pages = jnp.where(valid_rows[:, :, None], keys_new[source_rows], jnp.zeros((), jnp.bfloat16))
    value_pages = jnp.where(valid_rows[:, :, None], values_new[source_rows], jnp.zeros((), jnp.bfloat16))
    new_keys = jnp.zeros((NEWPAGES, PAGE, D), jnp.bfloat16).at[targets].set(key_pages)
    new_values = jnp.zeros((NEWPAGES, PAGE, D), jnp.bfloat16).at[targets].set(value_pages)
    return (mixed, new_keys, new_values)
```

```python
import math

import jax
import jax.numpy as jnp
from jax import lax
from jax.experimental import pallas as pl
from jax.experimental.pallas import tpu as pltpu
from jax.sharding import Mesh, PartitionSpec as P

HD = 128
NEG = -(2.0**100)
F32 = jnp.float32
BF16 = jnp.bfloat16
ALL = ("z", "c", "x", "y")
REQ = ("z", "c")
MLP = ("x", "y")
CHIPS = ("z", "x", "y")
DN = (((1,), (1,)), ((), ()))


def attend_kernel(heads, scaling, q, k, v, dk, dv, pool_mask, draft_mask, out):
    pm = pool_mask[...]
    dm = draft_mask[...]
    rows = q.shape[0]
    keys = k.shape[0] * k.shape[1]
    kk = k[...].reshape(keys, k.shape[2])
    vv = v[...].reshape(keys, v.shape[2])
    lane = lax.broadcasted_iota(jnp.int32, (rows, HD), 1)
    stats = jnp.zeros((rows, HD), F32)
    for h in range(heads):
        cols = slice(h * HD, (h + 1) * HD)
        qh = q[:, cols]
        s = lax.dot_general(qh, kk[:, cols], DN, preferred_element_type=F32) * scaling
        sd = lax.dot_general(qh, dk[:, cols], DN, preferred_element_type=F32) * scaling
        s = jnp.where(pm > 0, s, NEG)
        sd = jnp.where(dm > 0, sd, NEG)
        top = jnp.maximum(jnp.max(s, axis=1, keepdims=True), jnp.max(sd, axis=1, keepdims=True))
        top = top.astype(BF16).astype(F32)
        p = jnp.exp(s - top) * pm
        pd = jnp.exp(sd - top) * dm
        total = jnp.sum(p, axis=1, keepdims=True) + jnp.sum(pd, axis=1, keepdims=True)
        high = total.astype(BF16).astype(F32)
        stats = jnp.where(lane == h, top, stats)
        stats = jnp.where(lane == 8 + h, high, stats)
        stats = jnp.where(lane == 16 + h, total - high, stats)
        w = jnp.dot(p.astype(BF16), vv[:, cols], preferred_element_type=F32)
        w = w + jnp.dot(pd.astype(BF16), dv[:, cols], preferred_element_type=F32)
        out[:, cols] = w.astype(BF16)
    out[:, heads * HD :] = stats.astype(BF16)


def attend(q, key_cache, value_cache, dk, dv, pool_mask, draft_mask):
    rows, width = q.shape
    pages, page_len, _ = key_cache.shape
    heads = 7
    steps = width // (heads * HD)
    wide = heads * HD
    col = lambda i: (0, i)
    col3 = lambda i: (0, 0, i)
    fixed = lambda i: (0, 0)

    def body(*refs):
        attend_kernel(heads, 1.0 / math.sqrt(HD), *refs)

    return pl.pallas_call(
        body,
        grid=(steps,),
        in_specs=[
            pl.BlockSpec((rows, wide), col),
            pl.BlockSpec((pages, page_len, wide), col3),
            pl.BlockSpec((pages, page_len, wide), col3),
            pl.BlockSpec((dk.shape[0], wide), col),
            pl.BlockSpec((dv.shape[0], wide), col),
            pl.BlockSpec(pool_mask.shape, fixed),
            pl.BlockSpec(draft_mask.shape, fixed),
        ],
        out_specs=pl.BlockSpec((rows, wide + HD), col),
        out_shape=jax.ShapeDtypeStruct((rows, steps * (wide + HD)), BF16),
        compiler_params=pltpu.CompilerParams(vmem_limit_bytes=40 * 1024 * 1024),
        cost_estimate=pl.CostEstimate(
            flops=4 * rows * pages * page_len * width,
            bytes_accessed=4 * pages * page_len * width,
            transcendentals=rows * pages * page_len * width // HD,
        ),
    )(q, key_cache, value_cache, dk, dv, pool_mask, draft_mask)


def pair(x):
    return lax.ppermute(x, "c", [(0, 1), (1, 0)])


def spread(x, axes, count):
    return lax.all_to_all(
        jnp.broadcast_to(x[None], (count,) + x.shape), axes, split_axis=0, concat_axis=0
    )


def exchange(x, axes):
    return lax.all_to_all(x, axes, split_axis=0, concat_axis=0)


def local(
    queries,
    keys_new,
    values_new,
    resid,
    tree_mask,
    tree_size,
    accepted,
    dest_slot,
    page_table,
    key_cache,
    value_cache,
    w_out,
    w_up,
    w_down,
    ln_gain,
):
    zs, cs, xs, ys = (lax.axis_size(a) for a in ALL)
    members = xs * ys
    groups = zs * cs
    z = lax.axis_index("z")
    c = lax.axis_index("c")
    member = lax.axis_index(MLP)
    rows_dev, width = queries.shape
    requests, tree_len = tree_mask.shape[:2]
    group_rows = requests * tree_len
    pages_dev, page_len, _ = key_cache.shape
    tokens = group_rows * groups
    heads = width // HD
    half = width // cs
    chunk = half // zs
    block = tokens // members

    k_dev = w_out.shape[0]
    wo = w_out.reshape(k_dev, cs, zs, chunk)
    wo_parts = []
    for d in range(zs):
        piece = lax.dynamic_index_in_dim(wo, (z + d) % zs, 2, keepdims=False)
        if d:
            piece = lax.ppermute(piece, "z", [(i, (i + d) % zs) for i in range(zs)])
        wo_parts.append(piece)

    up_own = lax.dynamic_slice_in_dim(w_up, c * half, half, 0)
    up_pair = pair(lax.dynamic_slice_in_dim(w_up, (1 - c) * half, half, 0))
    down_own = lax.dynamic_slice_in_dim(w_down, c * half, half, 1)
    down_pair = pair(lax.dynamic_slice_in_dim(w_down, (1 - c) * half, half, 1))
    gain = lax.dynamic_slice_in_dim(ln_gain, c * half + z * chunk, chunk, 0)

    res = exchange(
        resid.reshape(rows_dev, cs, zs, chunk).transpose(2, 1, 0, 3).reshape(groups, rows_dev, chunk),
        REQ,
    ).reshape(block, chunk)

    group_q = spread(queries, MLP, members).reshape(group_rows, width)

    page_ids = member * pages_dev + jnp.arange(pages_dev, dtype=jnp.int32)
    owners = jnp.any(page_table[:, :, None] == page_ids[None, None, :], axis=1)
    pool_mask = jnp.repeat(jnp.repeat(owners, page_len, axis=1), tree_len, axis=0).astype(F32)
    draft_pad = 8
    slot_ids = member * rows_dev + jnp.arange(draft_pad, dtype=jnp.int32)
    row_ids = jnp.arange(group_rows, dtype=jnp.int32)
    tree_cols = jnp.tile(tree_mask.reshape(group_rows, tree_len), (1, requests))
    live = jnp.repeat(tree_size, tree_len) > (row_ids % tree_len)
    tree_ok = (
        (tree_cols == 1)
        & live[None, :]
        & ((row_ids // tree_len)[:, None] == (row_ids // tree_len)[None, :])
    ).astype(F32)
    pick = (row_ids[:, None] == slot_ids[None, :]) & (
        jnp.arange(draft_pad, dtype=jnp.int32) < rows_dev
    )[None, :]
    draft_mask = jnp.dot(tree_ok, pick.astype(F32))
    pad = ((0, draft_pad - rows_dev), (0, 0))
    parts = attend(
        group_q,
        key_cache,
        value_cache,
        jnp.pad(keys_new, pad),
        jnp.pad(values_new, pad),
        pool_mask,
        draft_mask,
    )

    parts = exchange(parts.reshape(members, rows_dev, parts.shape[1]), MLP)
    parts = parts.reshape(members, rows_dev, heads // 7, 8, HD).astype(F32)
    st = parts[:, :, :, 7]
    tops, highs, lows = st[..., 0:7], st[..., 8:15], st[..., 16:23]
    scale = jnp.exp(tops - jnp.max(tops, axis=0, keepdims=True))
    total = jnp.sum(scale * (highs + lows), axis=0)
    weighted = jnp.sum(scale[..., None] * parts[:, :, :, :7], axis=0)
    attended = (weighted / total[..., None]).astype(BF16).reshape(rows_dev, width)

    feats = (
        attended.reshape(rows_dev, zs, cs, members, k_dev)
        .transpose(2, 3, 0, 1, 4)
        .reshape(1, cs * members, rows_dev, zs * k_dev)
    )
    feats = jnp.broadcast_to(feats, (zs,) + feats.shape[1:]).reshape(
        groups * members, rows_dev, zs * k_dev
    )
    feats = exchange(feats, ALL)
    feats = (
        feats.reshape(groups, members, rows_dev, zs * k_dev)
        .transpose(1, 0, 2, 3)
        .reshape(tokens, zs * k_dev)
    )
    wo_all = jnp.concatenate([jnp.stack(wo_parts[::-1]), jnp.stack(wo_parts[::-1])])
    wo_all = lax.dynamic_slice_in_dim(wo_all, zs - 1 - z, zs, 0)
    wo_all = wo_all.reshape(zs * k_dev, cs, chunk)
    wo_own = lax.dynamic_index_in_dim(wo_all, c, 1, keepdims=False)
    wo_pair = lax.dynamic_index_in_dim(wo_all, 1 - c, 1, keepdims=False)
    sent = pair(jnp.dot(feats, wo_pair, preferred_element_type=F32).astype(BF16))
    part = jnp.dot(feats, wo_own, preferred_element_type=F32) + sent.astype(F32)
    part = exchange(part.astype(BF16).reshape(members, block, chunk), MLP)
    hidden = res.astype(F32) + jnp.sum(part.astype(F32), axis=0)

    mean = jnp.mean(hidden, axis=1)
    dev = jnp.sum(jnp.square(hidden - mean[:, None]), axis=1)
    stat = jnp.stack([mean, dev])
    stat = spread(jnp.pad(stat, ((0, 6), (0, 128 - block))), REQ, groups)[:, :2, :block]
    row_mean = jnp.mean(stat[:, 0], axis=0)
    spread_sum = jnp.sum(stat[:, 1] + chunk * jnp.square(stat[:, 0] - row_mean[None]), axis=0)
    inv = lax.rsqrt(spread_sum / width + 1e-05)
    normed = ((hidden - row_mean[:, None]) * inv[:, None] * gain[None, :]).astype(BF16)

    rows = spread(normed, CHIPS, zs * members).reshape(zs, tokens, chunk)

    def up(weight):
        out = None
        for i in range(zs):
            term = jnp.dot(
                rows[i], weight[i * chunk : (i + 1) * chunk], preferred_element_type=F32
            )
            out = term if out is None else out + term
        return out

    other = pair(up(up_pair))
    act = jnp.maximum(up(up_own) + other, 0.0).astype(BF16)
    act_pair = pair(act)
    down = []
    for i in range(zs):
        cols = slice(i * chunk, (i + 1) * chunk)
        down.append(
            (
                jnp.dot(act, down_own[:, cols], preferred_element_type=F32)
                + jnp.dot(act_pair, down_pair[:, cols], preferred_element_type=F32)
            )
            .astype(BF16)
            .reshape(members, block, chunk)
        )
    down = exchange(jnp.stack(down).reshape(zs * members, block, chunk), CHIPS)
    mixed = (hidden + jnp.sum(down.astype(F32), axis=0)).astype(BF16)
    mixed = exchange(mixed.reshape(groups, rows_dev, chunk), REQ)
    mixed = mixed.reshape(zs, cs, rows_dev, chunk).transpose(2, 1, 0, 3).reshape(rows_dev, width)

    both = lax.all_gather(
        jnp.concatenate([keys_new, values_new], axis=1), MLP, axis=0, tiled=True
    )
    valid = (accepted >= 0) & (dest_slot == member)[:, None]
    target = jnp.arange(requests, dtype=jnp.int32)[:, None] * tree_len + jnp.maximum(accepted, 0)
    chooser = jnp.any((target[:, :, None] == row_ids[None, None, :]) & valid[:, :, None], axis=0)
    picked = jnp.dot(chooser.astype(BF16), both, preferred_element_type=F32).astype(BF16)
    return (mixed, picked[:, :width][None], picked[:, width:][None])


def solution(mesh):
    groups, members = mesh.devices.shape
    side = math.isqrt(members)
    fine = Mesh(mesh.devices.reshape(groups // 2, 2, side, side), ALL)
    rows = P(ALL, None)
    pages = P(ALL, None, None)
    in_specs = (
        rows,
        rows,
        rows,
        rows,
        P(REQ, None, None),
        P(REQ),
        P(REQ, None),
        P(REQ),
        P(REQ, None),
        pages,
        pages,
        rows,
        P(None, ALL),
        rows,
        P(),
    )
    return jax.shard_map(
        local, mesh=fine, in_specs=in_specs, out_specs=(rows, pages, pages), check_vma=False
    )
```

```python
import math

import jax
import jax.numpy as jnp
from jax import lax
from jax.experimental import pallas as pl
from jax.experimental.pallas import tpu as pltpu
from jax.sharding import Mesh, PartitionSpec as P

HD = 128
NEG = -(2.0**100)
F32 = jnp.float32
BF16 = jnp.bfloat16
ALL = ("z", "c", "x", "y")
REQ = ("z", "c")
MLP = ("x", "y")
DN = (((1,), (1,)), ((), ()))


def attend_kernel(heads, scaling, q, k, v, dk, dv, pool_mask, draft_mask, out):
    pm = pool_mask[...]
    dm = draft_mask[...]
    rows = q.shape[0]
    keys = k.shape[0] * k.shape[1]
    kk = k[...].reshape(keys, k.shape[2])
    vv = v[...].reshape(keys, v.shape[2])
    lane = lax.broadcasted_iota(jnp.int32, (rows, HD), 1)
    stats = jnp.zeros((rows, HD), F32)
    for h in range(heads):
        cols = slice(h * HD, (h + 1) * HD)
        qh = q[:, cols]
        s = lax.dot_general(qh, kk[:, cols], DN, preferred_element_type=F32) * scaling
        sd = lax.dot_general(qh, dk[:, cols], DN, preferred_element_type=F32) * scaling
        s = jnp.where(pm > 0, s, NEG)
        sd = jnp.where(dm > 0, sd, NEG)
        top = jnp.maximum(jnp.max(s, axis=1, keepdims=True), jnp.max(sd, axis=1, keepdims=True))
        top = top.astype(BF16).astype(F32)
        p = jnp.exp(s - top) * pm
        pd = jnp.exp(sd - top) * dm
        total = jnp.sum(p, axis=1, keepdims=True) + jnp.sum(pd, axis=1, keepdims=True)
        high = total.astype(BF16).astype(F32)
        stats = jnp.where(lane == h, top, stats)
        stats = jnp.where(lane == 8 + h, high, stats)
        stats = jnp.where(lane == 16 + h, total - high, stats)
        w = jnp.dot(p.astype(BF16), vv[:, cols], preferred_element_type=F32)
        w = w + jnp.dot(pd.astype(BF16), dv[:, cols], preferred_element_type=F32)
        out[:, cols] = w.astype(BF16)
    out[:, heads * HD :] = stats.astype(BF16)


def attend(q, key_cache, value_cache, dk, dv, pool_mask, draft_mask):
    rows, width = q.shape
    pages, page_len, _ = key_cache.shape
    heads = 7
    steps = width // (heads * HD)
    wide = heads * HD
    col = lambda i: (0, i)
    col3 = lambda i: (0, 0, i)
    fixed = lambda i: (0, 0)

    def body(*refs):
        attend_kernel(heads, 1.0 / math.sqrt(HD), *refs)

    return pl.pallas_call(
        body,
        grid=(steps,),
        in_specs=[
            pl.BlockSpec((rows, wide), col),
            pl.BlockSpec((pages, page_len, wide), col3),
            pl.BlockSpec((pages, page_len, wide), col3),
            pl.BlockSpec((dk.shape[0], wide), col),
            pl.BlockSpec((dv.shape[0], wide), col),
            pl.BlockSpec(pool_mask.shape, fixed),
            pl.BlockSpec(draft_mask.shape, fixed),
        ],
        out_specs=pl.BlockSpec((rows, wide + HD), col),
        out_shape=jax.ShapeDtypeStruct((rows, steps * (wide + HD)), BF16),
        compiler_params=pltpu.CompilerParams(vmem_limit_bytes=40 * 1024 * 1024),
        cost_estimate=pl.CostEstimate(
            flops=4 * rows * pages * page_len * width,
            bytes_accessed=4 * pages * page_len * width,
            transcendentals=rows * pages * page_len * width // HD,
        ),
    )(q, key_cache, value_cache, dk, dv, pool_mask, draft_mask)


def pair(x):
    return lax.ppermute(x, "c", [(0, 1), (1, 0)])


def shift(x, step, size):
    return lax.ppermute(x, "z", [(i, (i + step) % size) for i in range(size)])


def after(x, first):
    return lax.optimization_barrier((x, first))[0]


def up_kernel(n, *refs):
    g = refs[0][...]
    for d in range(n):
        for e in range(2):
            w = lax.dot_general(g, refs[1 + d][e], DN, preferred_element_type=F32)
            if e:
                refs[n + 2][d] = w.astype(BF16)
            else:
                refs[n + 1][d] = w


def up_project(normed, weights):
    n = len(weights)
    rows = normed.shape[0]
    units = weights[0].shape[1]
    return pl.pallas_call(
        lambda *refs: up_kernel(n, *refs),
        out_shape=(
            jax.ShapeDtypeStruct((n, rows, units), F32),
            jax.ShapeDtypeStruct((n, rows, units), BF16),
        ),
        compiler_params=pltpu.CompilerParams(vmem_limit_bytes=40 * 1024 * 1024),
        cost_estimate=pl.CostEstimate(
            flops=4 * n * rows * normed.shape[1] * units,
            bytes_accessed=4 * n * normed.shape[1] * units,
            transcendentals=0,
        ),
    )(normed, *weights)


def down_kernel(n, *refs):
    total = None
    for d in range(n):
        for e in range(2):
            term = jnp.dot(refs[e * n + d][...], refs[2 * n + d][e], preferred_element_type=F32)
            total = term if total is None else total + term
    refs[3 * n][...] = total.astype(BF16)


def down_project(own, other, weights):
    n = len(weights)
    rows, units = own[0].shape
    width = weights[0].shape[2]
    return pl.pallas_call(
        lambda *refs: down_kernel(n, *refs),
        out_shape=jax.ShapeDtypeStruct((rows, width), BF16),
        compiler_params=pltpu.CompilerParams(vmem_limit_bytes=40 * 1024 * 1024),
        cost_estimate=pl.CostEstimate(
            flops=4 * n * rows * width * units,
            bytes_accessed=4 * n * width * units,
            transcendentals=0,
        ),
    )(*own, *other, *weights)


def spread(x, axes, count):
    return lax.all_to_all(
        jnp.broadcast_to(x[None], (count,) + x.shape), axes, split_axis=0, concat_axis=0
    )


def exchange(x, axes):
    return lax.all_to_all(x, axes, split_axis=0, concat_axis=0)


def local(
    queries,
    keys_new,
    values_new,
    resid,
    tree_mask,
    tree_size,
    accepted,
    dest_slot,
    page_table,
    key_cache,
    value_cache,
    w_out,
    w_up,
    w_down,
    ln_gain,
):
    zs, cs, xs, ys = (lax.axis_size(a) for a in ALL)
    members = xs * ys
    groups = zs * cs
    z = lax.axis_index("z")
    c = lax.axis_index("c")
    member = lax.axis_index(MLP)
    rows_dev, width = queries.shape
    requests, tree_len = tree_mask.shape[:2]
    group_rows = requests * tree_len
    pages_dev, page_len, _ = key_cache.shape
    tokens = group_rows * groups
    heads = width // HD
    half = width // cs
    chunk = half // zs
    block = tokens // members

    group_q = spread(queries, MLP, members).reshape(group_rows, width)

    def piece(w, core, d):
        return lax.dynamic_slice_in_dim(w, core * half + ((z + d) % zs) * chunk, chunk, 1)

    k_dev = w_out.shape[0]
    wo = after(w_out, group_q)
    wo_parts = []
    for d in range(zs):
        part = jnp.stack([piece(wo, c, d), piece(wo, 1 - c, d)])
        wo_parts.append(shift(part, d, zs) if d else part)
    wo_parts = jnp.concatenate(wo_parts, axis=1)

    both = spread(
        after(jnp.concatenate([keys_new, values_new], axis=1), group_q), MLP, members
    ).reshape(group_rows, 2 * width)

    page_ids = member * pages_dev + jnp.arange(pages_dev, dtype=jnp.int32)
    owners = jnp.any(page_table[:, :, None] == page_ids[None, None, :], axis=1)
    pool_mask = jnp.repeat(jnp.repeat(owners, page_len, axis=1), tree_len, axis=0).astype(F32)
    draft_pad = 8
    slot_ids = member * rows_dev + jnp.arange(draft_pad, dtype=jnp.int32)
    row_ids = jnp.arange(group_rows, dtype=jnp.int32)
    tree_cols = jnp.tile(tree_mask.reshape(group_rows, tree_len), (1, requests))
    live = jnp.repeat(tree_size, tree_len) > (row_ids % tree_len)
    tree_ok = (
        (tree_cols == 1)
        & live[None, :]
        & ((row_ids // tree_len)[:, None] == (row_ids // tree_len)[None, :])
    ).astype(F32)
    pick = (row_ids[:, None] == slot_ids[None, :]) & (
        jnp.arange(draft_pad, dtype=jnp.int32) < rows_dev
    )[None, :]
    draft_mask = jnp.dot(tree_ok, pick.astype(F32))
    pad = ((0, draft_pad - rows_dev), (0, 0))
    parts = attend(
        group_q,
        key_cache,
        value_cache,
        jnp.pad(keys_new, pad),
        jnp.pad(values_new, pad),
        pool_mask,
        draft_mask,
    )

    res = after(resid, parts)
    res = jnp.stack(
        [
            lax.dynamic_slice_in_dim(res, c * half, half, 1),
            pair(lax.dynamic_slice_in_dim(res, (1 - c) * half, half, 1)),
        ]
    ).reshape(cs * rows_dev, half)
    res_parts = []
    for d in range(zs):
        part = lax.dynamic_slice_in_dim(res, ((z + d) % zs) * chunk, chunk, 1)
        res_parts.append(shift(part, d, zs) if d else part)
    res = jnp.concatenate(res_parts, axis=0)
    at = jnp.arange(block, dtype=jnp.int32)
    source = ((z - at // (cs * rows_dev)) % zs) * cs + (c + at // rows_dev) % cs
    order = at[:, None] == (source * rows_dev + at % rows_dev)[None, :]
    res = jnp.dot(order.astype(BF16), res, preferred_element_type=F32)

    weights = []
    for w in (w_up.T, w_down):
        w = after(w, parts)
        other = pair(lax.dynamic_slice_in_dim(w, (1 - c) * half, half, 1))
        split = []
        for d in range(zs):
            at = ((z + d) % zs) * chunk
            part = jnp.stack([piece(w, c, d), lax.dynamic_slice_in_dim(other, at, chunk, 1)])
            split.append(shift(part, d, zs) if d else part)
        weights.append(split)

    parts = exchange(parts.reshape(members, rows_dev, parts.shape[1]), MLP)
    parts = parts.reshape(members, rows_dev, heads // 7, 8, HD).astype(F32)
    st = parts[:, :, :, 7]
    tops, highs, lows = st[..., 0:7], st[..., 8:15], st[..., 16:23]
    scale = jnp.exp(tops - jnp.max(tops, axis=0, keepdims=True))
    total = jnp.sum(scale * (highs + lows), axis=0)
    weighted = jnp.sum(scale[..., None] * parts[:, :, :, :7], axis=0)
    attended = (weighted / total[..., None]).astype(BF16).reshape(rows_dev, width)

    feats = attended.reshape(rows_dev, zs, cs, members, k_dev).transpose(1, 2, 3, 0, 4)
    feats = jnp.stack(
        [
            jnp.concatenate([feats[(to - d) % zs] for d in range(zs)], axis=3)
            for to in range(zs)
        ]
    ).reshape(groups * members, rows_dev, zs * k_dev)
    feats = exchange(feats, ALL)
    feats = (
        feats.reshape(groups, members, rows_dev, zs * k_dev)
        .transpose(1, 0, 2, 3)
        .reshape(tokens, zs * k_dev)
    )
    wo_own, wo_pair = wo_parts[0], wo_parts[1]
    sent = pair(jnp.dot(feats, wo_pair, preferred_element_type=F32).astype(BF16))
    part = jnp.dot(feats, wo_own, preferred_element_type=F32) + sent.astype(F32)
    part = exchange(part.astype(BF16).reshape(members, block, chunk), MLP)
    hidden = res + jnp.sum(part.astype(F32), axis=0)

    gain = lax.dynamic_slice_in_dim(ln_gain, c * half + z * chunk, chunk, 0)

    mean = jnp.mean(hidden, axis=1)
    dev = jnp.sum(jnp.square(hidden - mean[:, None]), axis=1)
    stat = jnp.stack([mean, dev])
    stat = spread(jnp.pad(stat, ((0, 6), (0, 128 - block))), REQ, groups)[:, :2, :block]
    row_mean = jnp.mean(stat[:, 0], axis=0)
    spread_sum = jnp.sum(stat[:, 1] + chunk * jnp.square(stat[:, 0] - row_mean[None]), axis=0)
    inv = lax.rsqrt(spread_sum / width + 1e-05)
    normed = ((hidden - row_mean[:, None]) * inv[:, None] * gain[None, :]).astype(BF16)

    rows = spread(normed, MLP, members).reshape(tokens, chunk)
    mine, theirs = up_project(rows, weights[0])
    theirs = pair(theirs)
    act = None
    for d in range(zs):
        term = mine[d] + theirs[d].astype(F32)
        if d:
            term = shift(term.astype(BF16), -d, zs).astype(F32)
        act = term if act is None else act + term
    act = jnp.maximum(act, 0.0).astype(BF16)
    acts = [shift(act, d, zs) if d else act for d in range(zs)]
    down = down_project(acts, [pair(a) for a in acts], weights[1])
    down = exchange(down.reshape(members, block, chunk), MLP)
    mixed = (hidden + jnp.sum(down.astype(F32), axis=0)).astype(BF16)
    mixed = exchange(mixed.reshape(groups, rows_dev, chunk), REQ)
    mixed = mixed.reshape(zs, cs, rows_dev, chunk).transpose(2, 1, 0, 3).reshape(rows_dev, width)

    valid = (accepted >= 0) & (dest_slot == member)[:, None]
    target = jnp.arange(requests, dtype=jnp.int32)[:, None] * tree_len + jnp.maximum(accepted, 0)
    chooser = jnp.any((target[:, :, None] == row_ids[None, None, :]) & valid[:, :, None], axis=0)
    picked = jnp.dot(chooser.astype(BF16), both, preferred_element_type=F32).astype(BF16)
    return (mixed, picked[:, :width][None], picked[:, width:][None])


def solution(mesh):
    groups, members = mesh.devices.shape
    side = math.isqrt(members)
    fine = Mesh(mesh.devices.reshape(groups // 2, 2, side, side), ALL)
    rows = P(ALL, None)
    pages = P(ALL, None, None)
    in_specs = (
        rows,
        rows,
        rows,
        rows,
        P(REQ, None, None),
        P(REQ),
        P(REQ, None),
        P(REQ),
        P(REQ, None),
        pages,
        pages,
        rows,
        P(None, ALL),
        rows,
        P(),
    )
    return jax.shard_map(
        local, mesh=fine, in_specs=in_specs, out_specs=(rows, pages, pages), check_vma=False
    )
```

```python
import math

import jax
import jax.numpy as jnp
from jax import lax
from jax.experimental import pallas as pl
from jax.experimental.pallas import tpu as pltpu
from jax.sharding import Mesh, PartitionSpec as P

HD = 128
NEG = -(2.0**100)
F32 = jnp.float32
BF16 = jnp.bfloat16
ALL = ("z", "c", "x", "y")
REQ = ("z", "c")
MLP = ("x", "y")
CHIPS = ("z", "x", "y")
DN = (((1,), (1,)), ((), ()))


def attend_kernel(heads, scaling, q, k, v, dk, dv, pool_mask, draft_mask, out):
    pm = pool_mask[...]
    dm = draft_mask[...]
    rows = q.shape[0]
    keys = k.shape[0] * k.shape[1]
    kk = k[...].reshape(keys, k.shape[2])
    vv = v[...].reshape(keys, v.shape[2])
    lane = lax.broadcasted_iota(jnp.int32, (rows, HD), 1)
    stats = jnp.zeros((rows, HD), F32)
    for h in range(heads):
        cols = slice(h * HD, (h + 1) * HD)
        qh = q[:, cols]
        s = lax.dot_general(qh, kk[:, cols], DN, preferred_element_type=F32) * scaling
        sd = lax.dot_general(qh, dk[:, cols], DN, preferred_element_type=F32) * scaling
        s = jnp.where(pm > 0, s, NEG)
        sd = jnp.where(dm > 0, sd, NEG)
        top = jnp.maximum(jnp.max(s, axis=1, keepdims=True), jnp.max(sd, axis=1, keepdims=True))
        top = top.astype(BF16).astype(F32)
        p = jnp.exp(s - top) * pm
        pd = jnp.exp(sd - top) * dm
        total = jnp.sum(p, axis=1, keepdims=True) + jnp.sum(pd, axis=1, keepdims=True)
        high = total.astype(BF16).astype(F32)
        stats = jnp.where(lane == h, top, stats)
        stats = jnp.where(lane == 8 + h, high, stats)
        stats = jnp.where(lane == 16 + h, total - high, stats)
        w = jnp.dot(p.astype(BF16), vv[:, cols], preferred_element_type=F32)
        w = w + jnp.dot(pd.astype(BF16), dv[:, cols], preferred_element_type=F32)
        out[:, cols] = w.astype(BF16)
    out[:, heads * HD :] = stats.astype(BF16)


def attend(q, key_cache, value_cache, dk, dv, pool_mask, draft_mask):
    rows, width = q.shape
    pages, page_len, _ = key_cache.shape
    heads = 7
    steps = width // (heads * HD)
    wide = heads * HD
    col = lambda i: (0, i)
    col3 = lambda i: (0, 0, i)
    fixed = lambda i: (0, 0)

    def body(*refs):
        attend_kernel(heads, 1.0 / math.sqrt(HD), *refs)

    return pl.pallas_call(
        body,
        grid=(steps,),
        in_specs=[
            pl.BlockSpec((rows, wide), col),
            pl.BlockSpec((pages, page_len, wide), col3),
            pl.BlockSpec((pages, page_len, wide), col3),
            pl.BlockSpec((dk.shape[0], wide), col),
            pl.BlockSpec((dv.shape[0], wide), col),
            pl.BlockSpec(pool_mask.shape, fixed),
            pl.BlockSpec(draft_mask.shape, fixed),
        ],
        out_specs=pl.BlockSpec((rows, wide + HD), col),
        out_shape=jax.ShapeDtypeStruct((rows, steps * (wide + HD)), BF16),
        compiler_params=pltpu.CompilerParams(vmem_limit_bytes=58 * 1024 * 1024),
        cost_estimate=pl.CostEstimate(
            flops=4 * rows * pages * page_len * width,
            bytes_accessed=4 * pages * page_len * width,
            transcendentals=rows * pages * page_len * width // HD,
        ),
    )(q, key_cache, value_cache, dk, dv, pool_mask, draft_mask)


def pair(x):
    return lax.ppermute(x, "c", [(0, 1), (1, 0)])


def shift(x, step, size):
    return lax.ppermute(x, "z", [(i, (i + step) % size) for i in range(size)])


def after(x, first):
    return lax.optimization_barrier((x, first))[0]


def gain_kernel(gain, own, other, out):
    high = gain[...].astype(BF16).astype(F32)
    row = lax.broadcasted_iota(jnp.int32, (8, gain.shape[1]), 0)
    low = gain[...] - high
    both = jnp.where(row == 0, high, jnp.where(row == 1, low, 0.0)).astype(BF16)
    for e, w in enumerate((own, other)):
        out[e] = lax.dot_general(both, w[...], DN, preferred_element_type=F32)


def hidden_kernel(parts, res, gain, hidden_out, row_out):
    hidden = res[...] + jnp.sum(parts[...].astype(F32), axis=0)
    hidden_out[...] = hidden
    rows, chunk = hidden.shape
    mean = jnp.mean(hidden, axis=1, keepdims=True)
    centered = hidden - mean
    dev = jnp.sum(centered * centered, axis=1, keepdims=True)
    row_out[:, :chunk] = (centered * gain[...]).astype(BF16)
    lane = lax.broadcasted_iota(jnp.int32, (rows, HD), 1)
    stats = jnp.zeros((rows, HD), F32)
    at = 0
    for value in (mean, dev):
        for _ in range(3):
            high = value.astype(BF16).astype(F32)
            stats = jnp.where(lane == at, high, stats)
            value = value - high
            at += 1
    row_out[:, chunk:] = stats.astype(BF16)


def up_kernel(place, rows, own, other, gain_own, gain_other, mine, theirs, stats_out):
    step = pl.program_id(0)
    chunk = own.shape[1]
    g = rows[0, :, :chunk]
    st = rows[0, :, chunk:].astype(F32)
    mean = st[:, 0:1] + st[:, 1:2] + st[:, 2:3]
    dev = st[:, 3:4] + st[:, 4:5] + st[:, 5:6]
    lane = lax.broadcasted_iota(jnp.int32, st.shape, 1)
    stats = jnp.where(lane == step, mean, 0.0) + jnp.where(lane == 8, dev, 0.0)

    @pl.when(step == 0)
    def _():
        mine[...] = jnp.zeros_like(mine)
        theirs[...] = jnp.zeros_like(theirs)
        stats_out[...] = jnp.zeros_like(stats_out)

    stats_out[...] += stats
    for w, gw, out in ((own, gain_own, mine), (other, gain_other, theirs)):
        term = lax.dot_general(g, w[...], DN, preferred_element_type=F32)
        out[...] += term + mean * (gw[0, 0:1, :] + gw[0, 1:2, :])


def act_kernel(width, mine, theirs, stats, stats_pair, gain_own, gain_pair, out):
    n = gain_own.shape[0]
    a = stats[...]
    b = stats_pair[...]
    lane = lax.broadcasted_iota(jnp.int32, a.shape, 1)
    chunk = width // (2 * n)
    mean = (
        jnp.sum(jnp.where(lane < n, a, 0.0), axis=1, keepdims=True)
        + jnp.sum(jnp.where(lane < n, b, 0.0), axis=1, keepdims=True)
    ) / (2 * n)

    def spread_of(v):
        part = jnp.where(lane < n, chunk * jnp.square(v - mean), jnp.where(lane == 8, v, 0.0))
        return jnp.sum(part, axis=1, keepdims=True)

    inv = lax.rsqrt((spread_of(a) + spread_of(b)) / width + 1e-05)
    gw = jnp.zeros((1, out.shape[1]), F32)
    for k in range(n):
        for ref in (gain_own, gain_pair):
            gw = gw + ref[k, 0:1, :] + ref[k, 1:2, :]
    pre = inv * (mine[...] + theirs[...] - mean * gw)
    out[...] = jnp.maximum(pre, 0.0).astype(BF16)


def down_kernel(place, act, act_pair, own, other, out):
    out[0] = (
        jnp.dot(act[...], own[...], preferred_element_type=F32)
        + jnp.dot(act_pair[...], other[...], preferred_element_type=F32)
    ).astype(BF16)


def finish_kernel(parts, hidden, out, total):
    step = pl.program_id(0)

    @pl.when(step == 0)
    def _():
        total[...] = hidden[...]

    total[...] += jnp.sum(parts[...].astype(F32), axis=0)

    @pl.when(step == pl.num_programs(0) - 1)
    def _():
        out[...] = total[...].astype(BF16)


def params():
    return pltpu.CompilerParams(vmem_limit_bytes=32 * 1024 * 1024)


def own_spec(units, chunk, n):
    return pl.BlockSpec((units, chunk), lambda i, place: (0, place[0] * n + i))


def other_spec(units, chunk):
    return pl.BlockSpec((units, chunk), lambda i, place: (0, i))


def gain_products(place, gain, own, other, n, chunk):
    units = own.shape[0]

    def body(place, gain, own, other, out):
        gain_kernel(gain, own, other, out.at[0])

    return pl.pallas_call(
        body,
        grid_spec=pltpu.PrefetchScalarGridSpec(
            num_scalar_prefetch=1,
            grid=(n,),
            in_specs=[
                pl.BlockSpec((1, chunk), lambda i, place: (0, place[0] * n + i)),
                own_spec(units, chunk, n),
                other_spec(units, chunk),
            ],
            out_specs=pl.BlockSpec((1, 2, 8, units), lambda i, place: (i, 0, 0, 0)),
        ),
        out_shape=jax.ShapeDtypeStruct((n, 2, 8, units), F32),
        compiler_params=params(),
    )(place, gain, own, other)


def up_project(place, rows, own, other, gain_own, gain_other):
    n, tokens, wide = rows.shape
    units = own.shape[0]
    chunk = wide - HD
    fixed = lambda i, place: (0, 0)
    turn = lambda i, place: (i, 0, 0)
    return pl.pallas_call(
        up_kernel,
        grid_spec=pltpu.PrefetchScalarGridSpec(
            num_scalar_prefetch=1,
            grid=(n,),
            in_specs=[
                pl.BlockSpec((1, tokens, wide), turn),
                own_spec(units, chunk, n),
                other_spec(units, chunk),
                pl.BlockSpec((1, 8, units), turn),
                pl.BlockSpec((1, 8, units), turn),
            ],
            out_specs=[
                pl.BlockSpec((tokens, units), fixed),
                pl.BlockSpec((tokens, units), fixed),
                pl.BlockSpec((tokens, HD), fixed),
            ],
        ),
        out_shape=(
            jax.ShapeDtypeStruct((tokens, units), F32),
            jax.ShapeDtypeStruct((tokens, units), F32),
            jax.ShapeDtypeStruct((tokens, HD), F32),
        ),
        compiler_params=params(),
    )(place, rows, own, other, gain_own, gain_other)


def down_project(place, act, act_pair, own, other, n, chunk):
    tokens, units = act.shape
    fixed = lambda i, place: (0, 0)
    return pl.pallas_call(
        down_kernel,
        grid_spec=pltpu.PrefetchScalarGridSpec(
            num_scalar_prefetch=1,
            grid=(n,),
            in_specs=[
                pl.BlockSpec((tokens, units), fixed),
                pl.BlockSpec((tokens, units), fixed),
                own_spec(units, chunk, n),
                other_spec(units, chunk),
            ],
            out_specs=pl.BlockSpec((1, tokens, chunk), lambda i, place: (i, 0, 0)),
        ),
        out_shape=jax.ShapeDtypeStruct((n, tokens, chunk), BF16),
        compiler_params=params(),
    )(place, act, act_pair, own, other)


def finish(parts, hidden):
    count, block, chunk = parts.shape
    per = count // 4
    return pl.pallas_call(
        finish_kernel,
        grid=(4,),
        in_specs=[
            pl.BlockSpec((per, block, chunk), lambda i: (i, 0, 0)),
            pl.BlockSpec((block, chunk), lambda i: (0, 0)),
        ],
        out_specs=pl.BlockSpec((block, chunk), lambda i: (0, 0)),
        out_shape=jax.ShapeDtypeStruct((block, chunk), BF16),
        scratch_shapes=[pltpu.VMEM((block, chunk), F32)],
        compiler_params=params(),
    )(parts, hidden)


def spread(x, axes, count):
    return lax.all_to_all(
        jnp.broadcast_to(x[None], (count,) + x.shape), axes, split_axis=0, concat_axis=0
    )


def exchange(x, axes):
    return lax.all_to_all(x, axes, split_axis=0, concat_axis=0)


def local(
    queries,
    keys_new,
    values_new,
    resid,
    tree_mask,
    tree_size,
    accepted,
    dest_slot,
    page_table,
    key_cache,
    value_cache,
    w_out,
    w_up,
    w_down,
    ln_gain,
):
    zs, cs, xs, ys = (lax.axis_size(a) for a in ALL)
    members = xs * ys
    groups = zs * cs
    z = lax.axis_index("z")
    c = lax.axis_index("c")
    member = lax.axis_index(MLP)
    rows_dev, width = queries.shape
    requests, tree_len = tree_mask.shape[:2]
    group_rows = requests * tree_len
    pages_dev, page_len, _ = key_cache.shape
    tokens = group_rows * groups
    heads = width // HD
    half = width // cs
    chunk = half // zs
    block = tokens // members

    group_q = spread(queries, MLP, members).reshape(group_rows, width)

    def piece(w, core, d):
        return lax.dynamic_slice_in_dim(w, core * half + ((z + d) % zs) * chunk, chunk, 1)

    k_dev = w_out.shape[0]
    wo = after(w_out, group_q)
    wo_parts = []
    for d in range(zs):
        part = jnp.stack([piece(wo, c, d), piece(wo, 1 - c, d)])
        wo_parts.append(shift(part, d, zs) if d else part)
    wo_parts = jnp.concatenate(wo_parts, axis=1)

    both = spread(
        after(jnp.concatenate([keys_new, values_new], axis=1), group_q), MLP, members
    ).reshape(group_rows, 2 * width)

    page_ids = member * pages_dev + jnp.arange(pages_dev, dtype=jnp.int32)
    owners = jnp.any(page_table[:, :, None] == page_ids[None, None, :], axis=1)
    pool_mask = jnp.repeat(jnp.repeat(owners, page_len, axis=1), tree_len, axis=0).astype(F32)
    draft_pad = 8
    slot_ids = member * rows_dev + jnp.arange(draft_pad, dtype=jnp.int32)
    row_ids = jnp.arange(group_rows, dtype=jnp.int32)
    tree_cols = jnp.tile(tree_mask.reshape(group_rows, tree_len), (1, requests))
    live = jnp.repeat(tree_size, tree_len) > (row_ids % tree_len)
    tree_ok = (
        (tree_cols == 1)
        & live[None, :]
        & ((row_ids // tree_len)[:, None] == (row_ids // tree_len)[None, :])
    ).astype(F32)
    pick = (row_ids[:, None] == slot_ids[None, :]) & (
        jnp.arange(draft_pad, dtype=jnp.int32) < rows_dev
    )[None, :]
    draft_mask = jnp.dot(tree_ok, pick.astype(F32))
    pad = ((0, draft_pad - rows_dev), (0, 0))
    parts = attend(
        group_q,
        key_cache,
        value_cache,
        jnp.pad(keys_new, pad),
        jnp.pad(values_new, pad),
        pool_mask,
        draft_mask,
    )

    parts, both = lax.optimization_barrier((parts, both))

    res = after(resid, parts)
    res = jnp.stack(
        [
            lax.dynamic_slice_in_dim(res, c * half, half, 1),
            pair(lax.dynamic_slice_in_dim(res, (1 - c) * half, half, 1)),
        ]
    ).reshape(cs * rows_dev, half)
    res_parts = []
    for d in range(zs):
        part = lax.dynamic_slice_in_dim(res, ((z + d) % zs) * chunk, chunk, 1)
        res_parts.append(shift(part, d, zs) if d else part)
    res = jnp.concatenate(res_parts, axis=0)
    at = jnp.arange(block, dtype=jnp.int32)
    source = ((z - at // (cs * rows_dev)) % zs) * cs + (c + at // rows_dev) % cs
    order = at[:, None] == (source * rows_dev + at % rows_dev)[None, :]
    res = jnp.dot(order.astype(BF16), res, preferred_element_type=F32)

    place = c.reshape(1).astype(jnp.int32)
    up_w = w_up.T
    up_other = pair(lax.dynamic_slice_in_dim(after(up_w, parts), (1 - c) * half, half, 1))
    down_other = pair(lax.dynamic_slice_in_dim(after(w_down, parts), (1 - c) * half, half, 1))
    gw = gain_products(place, ln_gain[None], up_w, up_other, zs, chunk)
    gain_own = gw[:, 0]
    gain_other = gw[:, 1]
    gain_pair = pair(gain_other)

    parts = exchange(parts.reshape(members, rows_dev, parts.shape[1]), MLP)
    parts = parts.reshape(members, rows_dev, heads // 7, 8, HD).astype(F32)
    st = parts[:, :, :, 7]
    tops, highs, lows = st[..., 0:7], st[..., 8:15], st[..., 16:23]
    scale = jnp.exp(tops - jnp.max(tops, axis=0, keepdims=True))
    total = jnp.sum(scale * (highs + lows), axis=0)
    weighted = jnp.sum(scale[..., None] * parts[:, :, :, :7], axis=0)
    attended = (weighted / total[..., None]).astype(BF16).reshape(rows_dev, width)

    feats = attended.reshape(rows_dev, zs, cs, members, k_dev).transpose(1, 2, 3, 0, 4)
    feats = jnp.stack(
        [
            jnp.concatenate([feats[(to - d) % zs] for d in range(zs)], axis=3)
            for to in range(zs)
        ]
    ).reshape(groups * members, rows_dev, zs * k_dev)
    feats = exchange(feats, ALL)
    feats = (
        feats.reshape(groups, members, rows_dev, zs * k_dev)
        .transpose(1, 0, 2, 3)
        .reshape(tokens, zs * k_dev)
    )
    wo_own, wo_pair = wo_parts[0], wo_parts[1]
    sent = pair(jnp.dot(feats, wo_pair, preferred_element_type=F32).astype(BF16))
    part = jnp.dot(feats, wo_own, preferred_element_type=F32) + sent.astype(F32)
    part = exchange(part.astype(BF16).reshape(members, block, chunk), MLP)
    gain = lax.dynamic_slice_in_dim(ln_gain, c * half + z * chunk, chunk, 0)

    hidden, row = pl.pallas_call(
        hidden_kernel,
        out_shape=(
            jax.ShapeDtypeStruct((block, chunk), F32),
            jax.ShapeDtypeStruct((block, chunk + HD), BF16),
        ),
        compiler_params=params(),
    )(part, res, gain[None])
    rows = spread(row, CHIPS, zs * members).reshape(zs, tokens, chunk + HD)
    mine, theirs, stats = up_project(place, rows, up_w, up_other, gain_own, gain_other)
    act = pl.pallas_call(
        lambda *refs: act_kernel(width, *refs),
        out_shape=jax.ShapeDtypeStruct(mine.shape, BF16),
        compiler_params=params(),
    )(mine, pair(theirs), stats, pair(stats), gain_own, gain_pair)
    down = down_project(place, act, pair(act), w_down, down_other, zs, chunk)
    down = exchange(down.reshape(zs * members, block, chunk), CHIPS)
    mixed = finish(down, hidden)
    mixed = exchange(mixed.reshape(groups, rows_dev, chunk), REQ)
    mixed = mixed.reshape(zs, cs, rows_dev, chunk).transpose(2, 1, 0, 3).reshape(rows_dev, width)

    valid = (accepted >= 0) & (dest_slot == member)[:, None]
    target = jnp.arange(requests, dtype=jnp.int32)[:, None] * tree_len + jnp.maximum(accepted, 0)
    chooser = jnp.any((target[:, :, None] == row_ids[None, None, :]) & valid[:, :, None], axis=0)
    picked = jnp.dot(chooser.astype(BF16), both, preferred_element_type=F32).astype(BF16)
    return (mixed, picked[:, :width][None], picked[:, width:][None])


def solution(mesh):
    groups, members = mesh.devices.shape
    side = math.isqrt(members)
    fine = Mesh(mesh.devices.reshape(groups // 2, 2, side, side), ALL)
    rows = P(ALL, None)
    pages = P(ALL, None, None)
    in_specs = (
        rows,
        rows,
        rows,
        rows,
        P(REQ, None, None),
        P(REQ),
        P(REQ, None),
        P(REQ),
        P(REQ, None),
        pages,
        pages,
        rows,
        P(None, ALL),
        rows,
        P(),
    )
    return jax.shard_map(
        local, mesh=fine, in_specs=in_specs, out_specs=(rows, pages, pages), check_vma=False
    )
```

```python
import math

import jax
import jax.numpy as jnp
from jax import lax
from jax.experimental import pallas as pl
from jax.experimental.pallas import tpu as pltpu
from jax.sharding import Mesh, PartitionSpec as P

HD = 128
NEG = -(2.0**100)
F32 = jnp.float32
BF16 = jnp.bfloat16
ALL = ("z", "c", "x", "u", "v")
REQ = ("z", "c")
MLP = ("x", "u", "v")
HEADS = ("x", "u")
CHIPS = ("z", "x", "u", "v")
DN = (((1,), (1,)), ((), ()))


def attend_kernel(heads, scaling, q, k, v, dk, dv, mask, out):
    rows = q.shape[0]
    keys = k.shape[0] * k.shape[1]
    kk = jnp.concatenate([k[...].reshape(keys, k.shape[2]), dk[...]], axis=0)
    vv = jnp.concatenate([v[...].reshape(keys, v.shape[2]), dv[...]], axis=0)
    m = mask[...]
    span = [slice(h * HD, (h + 1) * HD) for h in range(heads)]
    scores = [
        jnp.where(
            m > 0,
            lax.dot_general(q[:, cols], kk[:, cols], DN, preferred_element_type=F32) * scaling,
            NEG,
        )
        for cols in span
    ]
    tops = [jnp.max(s, axis=1, keepdims=True).astype(BF16).astype(F32) for s in scores]
    weights = [jnp.exp(s - top) * m for s, top in zip(scores, tops)]
    totals = [jnp.sum(p, axis=1, keepdims=True) for p in weights]
    half = out.shape[1]
    lane = lax.broadcasted_iota(jnp.int32, (rows, HD), 1)
    stats = jnp.zeros((rows, HD), F32)
    for h, cols in enumerate(span):
        w = jnp.dot(weights[h].astype(BF16), vv[:, cols], preferred_element_type=F32)
        for i in range(rows // half):
            out[i, :, cols] = w[i * half : (i + 1) * half].astype(BF16)
        high = totals[h].astype(BF16).astype(F32)
        stats = jnp.where(lane == h, tops[h], stats)
        stats = jnp.where(lane == 8 + h, high, stats)
        stats = jnp.where(lane == 16 + h, totals[h] - high, stats)
    for i in range(rows // half):
        out[i, :, heads * HD :] = stats[i * half : (i + 1) * half].astype(BF16)


def attend(q, key_cache, value_cache, dk, dv, mask, steps, split):
    rows, width = q.shape
    pages, page_len, _ = key_cache.shape
    wide = width // steps
    heads = wide // HD
    col = lambda i: (0, i)
    col3 = lambda i: (0, 0, i)

    def body(*refs):
        attend_kernel(heads, 1.0 / math.sqrt(HD), *refs)

    return pl.pallas_call(
        body,
        grid=(steps,),
        in_specs=[
            pl.BlockSpec((rows, wide), col),
            pl.BlockSpec((pages, page_len, wide), col3),
            pl.BlockSpec((pages, page_len, wide), col3),
            pl.BlockSpec((dk.shape[0], wide), col),
            pl.BlockSpec((dv.shape[0], wide), col),
            pl.BlockSpec(mask.shape, lambda i: (0, 0)),
        ],
        out_specs=pl.BlockSpec((split, rows // split, wide + HD), lambda i: (i, 0, 0)),
        out_shape=jax.ShapeDtypeStruct((steps * split, rows // split, wide + HD), BF16),
        compiler_params=pltpu.CompilerParams(vmem_limit_bytes=58 * 1024 * 1024),
        cost_estimate=pl.CostEstimate(
            flops=4 * rows * pages * page_len * width,
            bytes_accessed=4 * pages * page_len * width,
            transcendentals=rows * pages * page_len * width // HD,
        ),
    )(q, key_cache, value_cache, dk, dv, mask)


def combine_kernel(heads, parts, out):
    count, rows, _ = parts.shape
    st = parts[:, :, heads * HD :].astype(F32).reshape(count * rows, HD)
    sums = pltpu.roll(st, HD - 8, 1) + pltpu.roll(st, HD - 16, 1)
    st = st.reshape(count, rows, HD)
    scale = jnp.exp(st - jnp.max(st, axis=0, keepdims=True))
    total = jnp.sum(scale * sums.reshape(count, rows, HD), axis=0)
    for h in range(heads):
        cols = slice(h * HD, (h + 1) * HD)
        acc = jnp.zeros((rows, HD), F32)
        for i in range(count):
            acc = acc + scale[i, :, h : h + 1] * parts[i, :, cols].astype(F32)
        out[:, cols] = (acc / total[:, h : h + 1]).astype(BF16)


def pair(x):
    return lax.ppermute(x, "c", [(0, 1), (1, 0)])


def shift(x, step, size, axes="z"):
    return lax.ppermute(x, axes, [(i, (i + step) % size) for i in range(size)])


def move(x, count, to):
    return lax.ppermute(x, ALL, [(i, to(i)) for i in range(count)])


def after(x, first):
    return lax.optimization_barrier((x, first))[0]


def gain_kernel(gain, own, other, out):
    high = gain[...].astype(BF16).astype(F32)
    row = lax.broadcasted_iota(jnp.int32, (8, gain.shape[1]), 0)
    low = gain[...] - high
    both = jnp.where(row == 0, high, jnp.where(row == 1, low, 0.0)).astype(BF16)
    for e, w in enumerate((own, other)):
        out[e] = lax.dot_general(both, w[...], DN, preferred_element_type=F32)


def hidden_kernel(parts, res, gain, hidden_out, row_out):
    hidden = res[...] + jnp.sum(parts[...].astype(F32), axis=0)
    hidden_out[...] = hidden
    rows, chunk = hidden.shape
    mean = jnp.mean(hidden, axis=1, keepdims=True)
    centered = hidden - mean
    dev = jnp.sum(centered * centered, axis=1, keepdims=True)
    row_out[:, :chunk] = (centered * gain[...]).astype(BF16)
    lane = lax.broadcasted_iota(jnp.int32, (rows, HD), 1)
    stats = jnp.zeros((rows, HD), F32)
    at = 0
    for value in (mean, dev):
        for _ in range(3):
            high = value.astype(BF16).astype(F32)
            stats = jnp.where(lane == at, high, stats)
            value = value - high
            at += 1
    row_out[:, chunk:] = stats.astype(BF16)


def up_kernel(place, rows, own, other, gain_own, gain_other, mine, theirs, stats_out):
    step = pl.program_id(0)
    chunk = own.shape[1]
    g = rows[0, :, :chunk]
    st = rows[0, :, chunk:].astype(F32)
    mean = st[:, 0:1] + st[:, 1:2] + st[:, 2:3]
    dev = st[:, 3:4] + st[:, 4:5] + st[:, 5:6]
    lane = lax.broadcasted_iota(jnp.int32, st.shape, 1)
    stats = jnp.where(lane == step, mean, 0.0) + jnp.where(lane == 8, dev, 0.0)

    @pl.when(step == 0)
    def _():
        mine[...] = jnp.zeros_like(mine)
        theirs[...] = jnp.zeros_like(theirs)
        stats_out[...] = jnp.zeros_like(stats_out)

    stats_out[...] += stats
    for w, gw, out in ((own, gain_own, mine), (other, gain_other, theirs)):
        term = lax.dot_general(g, w[...], DN, preferred_element_type=F32)
        out[...] += term + mean * (gw[0, 0:1, :] + gw[0, 1:2, :])


def act_kernel(width, mine, theirs, stats, stats_pair, gain_own, gain_pair, out):
    n = gain_own.shape[0]
    a = stats[...]
    b = stats_pair[...]
    lane = lax.broadcasted_iota(jnp.int32, a.shape, 1)
    chunk = width // (2 * n)
    mean = (
        jnp.sum(jnp.where(lane < n, a, 0.0), axis=1, keepdims=True)
        + jnp.sum(jnp.where(lane < n, b, 0.0), axis=1, keepdims=True)
    ) / (2 * n)

    def spread_of(v):
        part = jnp.where(lane < n, chunk * jnp.square(v - mean), jnp.where(lane == 8, v, 0.0))
        return jnp.sum(part, axis=1, keepdims=True)

    inv = lax.rsqrt((spread_of(a) + spread_of(b)) / width + 1e-05)
    gw = jnp.zeros((1, out.shape[1]), F32)
    for k in range(n):
        for ref in (gain_own, gain_pair):
            gw = gw + ref[k, 0:1, :] + ref[k, 1:2, :]
    pre = inv * (mine[...] + theirs[...] - mean * gw)
    out[...] = jnp.maximum(pre, 0.0).astype(BF16)


def down_kernel(place, act, act_pair, own, other, out):
    out[0] = (
        jnp.dot(act[...], own[...], preferred_element_type=F32)
        + jnp.dot(act_pair[...], other[...], preferred_element_type=F32)
    ).astype(BF16)


def finish_kernel(parts, hidden, out, total):
    step = pl.program_id(0)

    @pl.when(step == 0)
    def _():
        total[...] = hidden[...]

    total[...] += jnp.sum(parts[...].astype(F32), axis=0)

    @pl.when(step == pl.num_programs(0) - 1)
    def _():
        out[...] = total[...].astype(BF16)


def params():
    return pltpu.CompilerParams(vmem_limit_bytes=32 * 1024 * 1024)


def own_spec(units, chunk, n):
    return pl.BlockSpec((units, chunk), lambda i, place: (0, place[0] * n + i))


def other_spec(units, chunk):
    return pl.BlockSpec((units, chunk), lambda i, place: (0, i))


def gain_products(place, gain, own, other, n, chunk):
    units = own.shape[0]

    def body(place, gain, own, other, out):
        gain_kernel(gain, own, other, out.at[0])

    return pl.pallas_call(
        body,
        grid_spec=pltpu.PrefetchScalarGridSpec(
            num_scalar_prefetch=1,
            grid=(n,),
            in_specs=[
                pl.BlockSpec((1, chunk), lambda i, place: (0, place[0] * n + i)),
                own_spec(units, chunk, n),
                other_spec(units, chunk),
            ],
            out_specs=pl.BlockSpec((1, 2, 8, units), lambda i, place: (i, 0, 0, 0)),
        ),
        out_shape=jax.ShapeDtypeStruct((n, 2, 8, units), F32),
        compiler_params=params(),
    )(place, gain, own, other)


def up_project(place, rows, own, other, gain_own, gain_other):
    n, tokens, wide = rows.shape
    units = own.shape[0]
    chunk = wide - HD
    fixed = lambda i, place: (0, 0)
    turn = lambda i, place: (i, 0, 0)
    return pl.pallas_call(
        up_kernel,
        grid_spec=pltpu.PrefetchScalarGridSpec(
            num_scalar_prefetch=1,
            grid=(n,),
            in_specs=[
                pl.BlockSpec((1, tokens, wide), turn),
                own_spec(units, chunk, n),
                other_spec(units, chunk),
                pl.BlockSpec((1, 8, units), turn),
                pl.BlockSpec((1, 8, units), turn),
            ],
            out_specs=[
                pl.BlockSpec((tokens, units), fixed),
                pl.BlockSpec((tokens, units), fixed),
                pl.BlockSpec((tokens, HD), fixed),
            ],
        ),
        out_shape=(
            jax.ShapeDtypeStruct((tokens, units), F32),
            jax.ShapeDtypeStruct((tokens, units), F32),
            jax.ShapeDtypeStruct((tokens, HD), F32),
        ),
        compiler_params=params(),
    )(place, rows, own, other, gain_own, gain_other)


def down_project(place, act, act_pair, own, other, n, chunk):
    tokens, units = act.shape
    fixed = lambda i, place: (0, 0)
    return pl.pallas_call(
        down_kernel,
        grid_spec=pltpu.PrefetchScalarGridSpec(
            num_scalar_prefetch=1,
            grid=(n,),
            in_specs=[
                pl.BlockSpec((tokens, units), fixed),
                pl.BlockSpec((tokens, units), fixed),
                own_spec(units, chunk, n),
                other_spec(units, chunk),
            ],
            out_specs=pl.BlockSpec((1, tokens, chunk), lambda i, place: (i, 0, 0)),
        ),
        out_shape=jax.ShapeDtypeStruct((n, tokens, chunk), BF16),
        compiler_params=params(),
    )(place, act, act_pair, own, other)


def finish(parts, hidden):
    count, block, chunk = parts.shape
    per = count // 4
    return pl.pallas_call(
        finish_kernel,
        grid=(4,),
        in_specs=[
            pl.BlockSpec((per, block, chunk), lambda i: (i, 0, 0)),
            pl.BlockSpec((block, chunk), lambda i: (0, 0)),
        ],
        out_specs=pl.BlockSpec((block, chunk), lambda i: (0, 0)),
        out_shape=jax.ShapeDtypeStruct((block, chunk), BF16),
        scratch_shapes=[pltpu.VMEM((block, chunk), F32)],
        compiler_params=params(),
    )(parts, hidden)


def spread(x, axes, count):
    return lax.all_to_all(
        jnp.broadcast_to(x[None], (count,) + x.shape), axes, split_axis=0, concat_axis=0
    )


def exchange(x, axes):
    return lax.all_to_all(x, axes, split_axis=0, concat_axis=0)


def local(
    queries,
    keys_new,
    values_new,
    resid,
    tree_mask,
    tree_size,
    accepted,
    dest_slot,
    page_table,
    key_cache,
    value_cache,
    w_out,
    w_up,
    w_down,
    ln_gain,
):
    zs, cs, xs, us, vs = (lax.axis_size(a) for a in ALL)
    ys = us * vs
    members = xs * ys
    groups = zs * cs
    hosts = xs * us
    z = lax.axis_index("z")
    c = lax.axis_index("c")
    v = lax.axis_index("v")
    member = lax.axis_index(MLP)
    rows_dev, width = queries.shape
    requests, tree_len = tree_mask.shape[:2]
    group_rows = requests * tree_len
    pages_dev, page_len, _ = key_cache.shape
    tokens = group_rows * groups
    heads = width // HD
    half = width // cs
    chunk = half // zs
    block = tokens // members

    wide_q = jnp.broadcast_to(queries[None], (members,) + queries.shape)
    group_q = exchange(wide_q, MLP).reshape(group_rows, width)

    def piece(w, d):
        return lax.dynamic_slice_in_dim(w, ((z + d) % zs) * chunk, chunk, w.ndim - 1)

    def regroup(x):
        x = jnp.stack(
            [
                lax.dynamic_slice_in_dim(x, c * half, half, 1),
                pair(lax.dynamic_slice_in_dim(x, (1 - c) * half, half, 1)),
            ]
        )
        got = [shift(piece(x, d), d, zs) if d else piece(x, 0) for d in range(zs)]
        got = jnp.concatenate(got)
        at = [((z - k // cs) % zs) * cs + (c + k) % cs for k in range(groups)]
        return jnp.stack([lax.dynamic_index_in_dim(got, i, 0, keepdims=False) for i in at])

    k_dev = w_out.shape[0]
    lanes = groups * members

    def to_host(i):
        r, a, b = i // members, i % members // vs, i % vs
        return a * members + r * vs + b

    def to_other(i):
        return to_host(i) // vs * vs + (vs - 1 - i % vs)

    wo = after(w_out, wide_q)
    wo_same, wo_other = move(wo, lanes, to_host), move(wo, lanes, to_other)

    def to_block(i):
        r, s, k = i // members, i % members // groups, i % groups
        return k * members + r * vs + s

    def from_block(i):
        k, r, s = i // members, i % members // vs, i % vs
        return r * members + s * groups + k

    res = regroup(move(after(resid, wide_q), lanes, to_block)).reshape(block, chunk)
    res = res.astype(F32)

    both = after(jnp.concatenate([keys_new, values_new], axis=1), wide_q)
    both = jnp.stack([shift(both, d, xs, "x") if d else both for d in range(xs)])

    page_ids = member * pages_dev + jnp.arange(pages_dev, dtype=jnp.int32)
    owners = jnp.any(page_table[:, :, None] == page_ids[None, None, :], axis=1)
    pool_mask = jnp.repeat(jnp.repeat(owners, page_len, axis=1), tree_len, axis=0).astype(F32)
    draft_pad = 16
    slot_ids = member * rows_dev + jnp.arange(draft_pad, dtype=jnp.int32)
    row_ids = jnp.arange(group_rows, dtype=jnp.int32)
    tree_cols = jnp.tile(tree_mask.reshape(group_rows, tree_len), (1, requests))
    live = jnp.repeat(tree_size, tree_len) > (row_ids % tree_len)
    tree_ok = (
        (tree_cols == 1)
        & live[None, :]
        & ((row_ids // tree_len)[:, None] == (row_ids // tree_len)[None, :])
    ).astype(F32)
    pick = (row_ids[:, None] == slot_ids[None, :]) & (
        jnp.arange(draft_pad, dtype=jnp.int32) < rows_dev
    )[None, :]
    draft_mask = jnp.dot(tree_ok, pick.astype(F32))
    pad = ((0, draft_pad - rows_dev), (0, 0))
    parts = attend(
        group_q,
        key_cache,
        value_cache,
        jnp.pad(keys_new, pad),
        jnp.pad(values_new, pad),
        jnp.concatenate([pool_mask, draft_mask], axis=1),
        hosts,
        vs,
    )

    parts, wo_same, wo_other, res, both = lax.optimization_barrier(
        (parts, wo_same, wo_other, res, both)
    )
    wo = jnp.where(v == 0, jnp.stack([wo_same, wo_other]), jnp.stack([wo_other, wo_same]))
    wo = regroup(wo.reshape(vs * k_dev, width)).reshape(groups * vs * k_dev, chunk)

    both = jnp.stack([shift(both, d, ys, ("u", "v")) if d else both for d in range(ys)])

    place = c.reshape(1).astype(jnp.int32)
    up_w = w_up.T
    up_other = pair(lax.dynamic_slice_in_dim(after(up_w, parts), (1 - c) * half, half, 1))
    down_other = pair(lax.dynamic_slice_in_dim(after(w_down, parts), (1 - c) * half, half, 1))
    gw = gain_products(place, ln_gain[None], up_w, up_other, zs, chunk)
    gain_own = gw[:, 0]
    gain_other = gw[:, 1]
    gain_pair = pair(gain_other)

    parts = exchange(parts, MLP)
    attended = pl.pallas_call(
        lambda *refs: combine_kernel(heads // hosts, *refs),
        out_shape=jax.ShapeDtypeStruct((block, width // hosts), BF16),
        compiler_params=params(),
    )(parts)

    feats = spread(attended, REQ, groups).reshape(groups * block, width // hosts)
    part = jnp.dot(feats, wo, preferred_element_type=F32).astype(BF16)
    part = exchange(part.reshape(groups, block, chunk), HEADS)
    gain = lax.dynamic_slice_in_dim(ln_gain, c * half + z * chunk, chunk, 0)

    hidden, row = pl.pallas_call(
        hidden_kernel,
        out_shape=(
            jax.ShapeDtypeStruct((block, chunk), F32),
            jax.ShapeDtypeStruct((block, chunk + HD), BF16),
        ),
        compiler_params=params(),
    )(part, res, gain[None])
    row, both = lax.optimization_barrier((row, both))
    rows = spread(row, CHIPS, zs * members).reshape(zs, tokens, chunk + HD)
    mine, theirs, stats = up_project(place, rows, up_w, up_other, gain_own, gain_other)
    act = pl.pallas_call(
        lambda *refs: act_kernel(width, *refs),
        out_shape=jax.ShapeDtypeStruct(mine.shape, BF16),
        compiler_params=params(),
    )(mine, pair(theirs), stats, pair(stats), gain_own, gain_pair)
    down = down_project(place, act, pair(act), w_down, down_other, zs, chunk)
    down = exchange(down.reshape(zs * members, block, chunk), CHIPS)
    mixed = finish(down, hidden)
    mixed = exchange(mixed.reshape(groups, rows_dev, chunk), REQ)
    mixed = mixed.reshape(zs, cs, rows_dev, chunk).transpose(2, 1, 0, 3).reshape(rows_dev, width)
    mixed = move(mixed, lanes, from_block)

    valid = (accepted >= 0) & (dest_slot == member)[:, None]
    target = jnp.arange(requests, dtype=jnp.int32)[:, None] * tree_len + jnp.maximum(accepted, 0)
    x = lax.axis_index("x")
    y = lax.axis_index(("u", "v"))
    at = jnp.arange(group_rows, dtype=jnp.int32)
    near = at // rows_dev
    slots = (((x - near % xs) % xs) * ys + (y - near // xs) % ys) * rows_dev + at % rows_dev
    chooser = jnp.any((target[:, :, None] == slots[None, None, :]) & valid[:, :, None], axis=0)
    both = both.reshape(group_rows, 2 * width)
    picked = jnp.dot(chooser.astype(BF16), both, preferred_element_type=F32).astype(BF16)
    return (mixed, picked[:, :width][None], picked[:, width:][None])


def solution(mesh):
    groups, members = mesh.devices.shape
    side = math.isqrt(members)
    fine = Mesh(mesh.devices.reshape(groups // 2, 2, side, side // 2, 2), ALL)
    rows = P(ALL, None)
    pages = P(ALL, None, None)
    in_specs = (
        rows,
        rows,
        rows,
        rows,
        P(REQ, None, None),
        P(REQ),
        P(REQ, None),
        P(REQ),
        P(REQ, None),
        pages,
        pages,
        rows,
        P(None, ALL),
        rows,
        P(),
    )
    return jax.shard_map(
        local, mesh=fine, in_specs=in_specs, out_specs=(rows, pages, pages), check_vma=False
    )
```

```python
import math

import jax
import jax.numpy as jnp
from jax import lax
from jax.experimental import pallas as pl
from jax.experimental.pallas import tpu as pltpu
from jax.sharding import Mesh, PartitionSpec as P

HD = 128
NEG = -(2.0**100)
F32 = jnp.float32
BF16 = jnp.bfloat16
ALL = ("z", "c", "x", "y")
REQ = ("z", "c")
MLP = ("x", "y")
DN = (((1,), (1,)), ((), ()))


def attend_kernel(heads, scaling, q, k, v, dk, dv, mask, out):
    rows = q.shape[0]
    keys = k.shape[0] * k.shape[1]
    kk = jnp.concatenate([k[...].reshape(keys, k.shape[2]), dk[...]], axis=0)
    vv = jnp.concatenate([v[...].reshape(keys, v.shape[2]), dv[...]], axis=0)
    m = mask[...]
    span = [slice(h * HD, (h + 1) * HD) for h in range(heads)]
    scores = [
        jnp.where(
            m > 0,
            lax.dot_general(q[:, cols], kk[:, cols], DN, preferred_element_type=F32) * scaling,
            NEG,
        )
        for cols in span
    ]
    tops = [jnp.max(s, axis=1, keepdims=True).astype(BF16).astype(F32) for s in scores]
    weights = [jnp.exp(s - top) * m for s, top in zip(scores, tops)]
    totals = [jnp.sum(p, axis=1, keepdims=True) for p in weights]
    lane = lax.broadcasted_iota(jnp.int32, (rows, HD), 1)
    stats = jnp.zeros((rows, HD), F32)
    for h, cols in enumerate(span):
        w = jnp.dot(weights[h].astype(BF16), vv[:, cols], preferred_element_type=F32)
        out[:, cols] = w.astype(BF16)
        high = totals[h].astype(BF16).astype(F32)
        stats = jnp.where(lane == h, tops[h], stats)
        stats = jnp.where(lane == 8 + h, high, stats)
        stats = jnp.where(lane == 16 + h, totals[h] - high, stats)
    out[:, heads * HD :] = stats.astype(BF16)


def attend(q, key_cache, value_cache, dk, dv, mask, steps):
    rows, width = q.shape
    pages, page_len, _ = key_cache.shape
    wide = width // steps
    heads = wide // HD
    col = lambda i: (0, i)
    col3 = lambda i: (0, 0, i)

    def body(*refs):
        attend_kernel(heads, 1.0 / math.sqrt(HD), *refs)

    return pl.pallas_call(
        body,
        grid=(steps,),
        in_specs=[
            pl.BlockSpec((rows, wide), col),
            pl.BlockSpec((pages, page_len, wide), col3),
            pl.BlockSpec((pages, page_len, wide), col3),
            pl.BlockSpec((dk.shape[0], wide), col),
            pl.BlockSpec((dv.shape[0], wide), col),
            pl.BlockSpec(mask.shape, lambda i: (0, 0)),
        ],
        out_specs=pl.BlockSpec((rows, wide + HD), col),
        out_shape=jax.ShapeDtypeStruct((rows, steps * (wide + HD)), BF16),
        compiler_params=pltpu.CompilerParams(vmem_limit_bytes=58 * 1024 * 1024),
        cost_estimate=pl.CostEstimate(
            flops=4 * rows * pages * page_len * width,
            bytes_accessed=4 * pages * page_len * width,
            transcendentals=rows * pages * page_len * width // HD,
        ),
    )(q, key_cache, value_cache, dk, dv, mask)


def pair(x):
    return lax.ppermute(x, "c", [(0, 1), (1, 0)])


def shift(x, step, size):
    return lax.ppermute(x, "z", [(i, (i + step) % size) for i in range(size)])


def after(x, first):
    return lax.optimization_barrier((x, first))[0]


def gain_kernel(place, gain, weight, out):
    high = gain[...].astype(BF16).astype(F32)
    row = lax.broadcasted_iota(jnp.int32, (8, gain.shape[1]), 0)
    both = jnp.where(row == 0, high, jnp.where(row == 1, gain[...] - high, 0.0)).astype(BF16)
    got = lax.dot_general(both, weight[...], DN, preferred_element_type=F32)
    out[0] = jnp.broadcast_to(got[0:1] + got[1:2], got.shape)


def hidden_kernel(parts, res, gain, hidden_out, row_out):
    hidden = res[...] + jnp.sum(parts[...].astype(F32), axis=0)
    hidden_out[...] = hidden
    rows, chunk = hidden.shape
    mean = jnp.mean(hidden, axis=1, keepdims=True)
    centered = hidden - mean
    dev = jnp.sum(centered * centered, axis=1, keepdims=True)
    row_out[:, :chunk] = (centered * gain[...]).astype(BF16)
    lane = lax.broadcasted_iota(jnp.int32, (rows, HD), 1)
    stats = jnp.zeros((rows, HD), F32)
    at = 0
    for value in (mean, dev):
        for _ in range(3):
            high = value.astype(BF16).astype(F32)
            stats = jnp.where(lane == at, high, stats)
            value = value - high
            at += 1
    row_out[:, chunk:] = stats.astype(BF16)


def up_kernel(n, *refs):
    rows = refs[0]
    chunk = refs[1].shape[2]
    g = rows[:, :chunk]
    st = rows[:, chunk:].astype(F32)
    lane = lax.broadcasted_iota(jnp.int32, st.shape, 1)
    st = jnp.where(lane < 6, st, 0.0)
    none = jnp.zeros_like(st)
    for d in range(n):
        for e in range(2):
            w = refs[1 + d][e]
            wide = refs[n + 1].shape[2]
            w = jnp.concatenate([w, jnp.zeros((wide - w.shape[0], chunk), BF16)], axis=0)
            got = lax.dot_general(g, w, DN, preferred_element_type=F32)
            beside = jnp.concatenate([none, pltpu.roll(st, 96 if e else 102, 1)], axis=1)
            refs[n + 1 + e][d] = (got + beside).astype(refs[n + 1 + e].dtype)


def act_kernel(width, units, n, *refs):
    terms = [refs[d][...].astype(F32) for d in range(n)]
    gain = refs[n]
    out = refs[n + 1]
    chunk = width // (2 * n)
    pre = terms[0]
    for d in range(1, n):
        pre = pre + terms[d]
    pre = pre[:, :units]
    means, devs = [], []
    for t in terms:
        for at in (units + 6, units):
            means.append(t[:, at : at + 1] + t[:, at + 1 : at + 2] + t[:, at + 2 : at + 3])
            devs.append(t[:, at + 3 : at + 4] + t[:, at + 4 : at + 5] + t[:, at + 5 : at + 6])
    mean = sum(means[1:], means[0]) / (2 * n)
    var = sum(devs[1:], devs[0])
    for k, value in enumerate(means):
        off = value - mean
        var = var + chunk * off * off
        pre = pre + off * gain[k, 0:1, :]
    out[...] = jnp.maximum(lax.rsqrt(var / width + 1e-05) * pre, 0.0).astype(BF16)


def down_kernel(n, *refs):
    total = None
    for d in range(n):
        for e in range(2):
            term = jnp.dot(refs[e * n + d][...], refs[2 * n + d][e], preferred_element_type=F32)
            total = term if total is None else total + term
    refs[3 * n][...] = total.astype(BF16)


def finish_kernel(parts, hidden, out, total):
    step = pl.program_id(0)

    @pl.when(step == 0)
    def _():
        total[...] = hidden[...]

    total[...] += jnp.sum(parts[...].astype(F32), axis=0)

    @pl.when(step == pl.num_programs(0) - 1)
    def _():
        out[...] = total[...].astype(BF16)


def params():
    return pltpu.CompilerParams(vmem_limit_bytes=32 * 1024 * 1024)


def gain_products(order, gain, weight, chunk):
    units = weight.shape[0]
    n = order.shape[0]
    return pl.pallas_call(
        gain_kernel,
        grid_spec=pltpu.PrefetchScalarGridSpec(
            num_scalar_prefetch=1,
            grid=(n,),
            in_specs=[
                pl.BlockSpec((1, chunk), lambda i, order: (0, order[i])),
                pl.BlockSpec((units, chunk), lambda i, order: (0, order[i])),
            ],
            out_specs=pl.BlockSpec((1, 8, units), lambda i, order: (i, 0, 0)),
        ),
        out_shape=jax.ShapeDtypeStruct((n, 8, units), F32),
        compiler_params=params(),
    )(order, gain, weight)


def up_project(rows, weights):
    n = len(weights)
    tokens = rows.shape[0]
    return pl.pallas_call(
        lambda *refs: up_kernel(n, *refs),
        out_shape=(
            jax.ShapeDtypeStruct((n, tokens, 256), F32),
            jax.ShapeDtypeStruct((n, tokens, 256), BF16),
        ),
        compiler_params=params(),
    )(rows, *weights)


def down_project(own, other, weights):
    n = len(weights)
    return pl.pallas_call(
        lambda *refs: down_kernel(n, *refs),
        out_shape=jax.ShapeDtypeStruct((own[0].shape[0], weights[0].shape[2]), BF16),
        compiler_params=params(),
    )(*own, *other, *weights)


def finish(parts, hidden):
    count, block, chunk = parts.shape
    per = count // 4
    return pl.pallas_call(
        finish_kernel,
        grid=(4,),
        in_specs=[
            pl.BlockSpec((per, block, chunk), lambda i: (i, 0, 0)),
            pl.BlockSpec((block, chunk), lambda i: (0, 0)),
        ],
        out_specs=pl.BlockSpec((block, chunk), lambda i: (0, 0)),
        out_shape=jax.ShapeDtypeStruct((block, chunk), BF16),
        scratch_shapes=[pltpu.VMEM((block, chunk), F32)],
        compiler_params=params(),
    )(parts, hidden)


def spread(x, axes, count):
    return lax.all_to_all(
        jnp.broadcast_to(x[None], (count,) + x.shape), axes, split_axis=0, concat_axis=0
    )


def exchange(x, axes):
    return lax.all_to_all(x, axes, split_axis=0, concat_axis=0)


def local(
    queries,
    keys_new,
    values_new,
    resid,
    tree_mask,
    tree_size,
    accepted,
    dest_slot,
    page_table,
    key_cache,
    value_cache,
    w_out,
    w_up,
    w_down,
    ln_gain,
):
    zs, cs, xs, ys = (lax.axis_size(a) for a in ALL)
    members = xs * ys
    groups = zs * cs
    z = lax.axis_index("z")
    c = lax.axis_index("c")
    member = lax.axis_index(MLP)
    rows_dev, width = queries.shape
    requests, tree_len = tree_mask.shape[:2]
    group_rows = requests * tree_len
    pages_dev, page_len, _ = key_cache.shape
    tokens = group_rows * groups
    heads = width // HD
    half = width // cs
    chunk = half // zs
    block = tokens // members

    wide_q = jnp.broadcast_to(queries[None], (members,) + queries.shape)
    group_q = exchange(wide_q, MLP).reshape(group_rows, width)

    def piece(w, core, d):
        return lax.dynamic_slice_in_dim(w, core * half + ((z + d) % zs) * chunk, chunk, 1)

    k_dev = w_out.shape[0]
    wo = after(w_out, wide_q)
    wo_parts = []
    for d in range(zs):
        part = jnp.stack([piece(wo, c, d), piece(wo, 1 - c, d)])
        wo_parts.append(shift(part, d, zs) if d else part)
    wo_parts = jnp.concatenate(wo_parts, axis=1)

    def swap(w):
        return pair(lax.dynamic_slice_in_dim(w, (1 - c) * half, half, 1))

    def reshard(w, other):
        split = []
        for d in range(zs):
            at = ((z + d) % zs) * chunk
            part = jnp.stack([piece(w, c, d), lax.dynamic_slice_in_dim(other, at, chunk, 1)])
            split.append(shift(part, d, zs) if d else part)
        return split

    up_w = w_up.T
    up_w = after(up_w, wide_q)
    ups = reshard(up_w, swap(up_w))
    order = jnp.stack(
        [(c + e) % cs * zs + (z + d) % zs for d in range(zs) for e in range(cs)]
    ).astype(jnp.int32)
    gain_up = gain_products(order, ln_gain[None], up_w, chunk)

    page_ids = member * pages_dev + jnp.arange(pages_dev, dtype=jnp.int32)
    owners = jnp.any(page_table[:, :, None] == page_ids[None, None, :], axis=1)
    pool_mask = jnp.repeat(jnp.repeat(owners, page_len, axis=1), tree_len, axis=0).astype(F32)
    draft_pad = 16
    slot_ids = member * rows_dev + jnp.arange(draft_pad, dtype=jnp.int32)
    row_ids = jnp.arange(group_rows, dtype=jnp.int32)
    tree_cols = jnp.tile(tree_mask.reshape(group_rows, tree_len), (1, requests))
    live = jnp.repeat(tree_size, tree_len) > (row_ids % tree_len)
    tree_ok = (
        (tree_cols == 1)
        & live[None, :]
        & ((row_ids // tree_len)[:, None] == (row_ids // tree_len)[None, :])
    ).astype(F32)
    pick = (row_ids[:, None] == slot_ids[None, :]) & (
        jnp.arange(draft_pad, dtype=jnp.int32) < rows_dev
    )[None, :]
    draft_mask = jnp.dot(tree_ok, pick.astype(F32))
    pad = ((0, draft_pad - rows_dev), (0, 0))
    parts = attend(
        group_q,
        key_cache,
        value_cache,
        jnp.pad(keys_new, pad),
        jnp.pad(values_new, pad),
        jnp.concatenate([pool_mask, draft_mask], axis=1),
        heads // 7,
    )

    parts, ups[1], ups[3], wo_parts = lax.optimization_barrier((parts, ups[1], ups[3], wo_parts))
    down_other = swap(after(w_down, parts))

    res = after(resid, parts)
    res = jnp.stack(
        [
            lax.dynamic_slice_in_dim(res, c * half, half, 1),
            pair(lax.dynamic_slice_in_dim(res, (1 - c) * half, half, 1)),
        ]
    ).reshape(cs * rows_dev, half)
    res_parts = []
    for d in range(zs):
        part = lax.dynamic_slice_in_dim(res, ((z + d) % zs) * chunk, chunk, 1)
        res_parts.append(shift(part, d, zs) if d else part)
    res = jnp.concatenate(res_parts, axis=0)
    at = jnp.arange(block, dtype=jnp.int32)
    source = ((z - at // (cs * rows_dev)) % zs) * cs + (c + at // rows_dev) % cs
    order = at[:, None] == (source * rows_dev + at % rows_dev)[None, :]
    res = jnp.dot(order.astype(BF16), res, preferred_element_type=F32)

    parts = exchange(parts.reshape(members, rows_dev, parts.shape[1]), MLP)
    parts = parts.reshape(members, rows_dev, heads // 7, 8, HD).astype(F32)
    st = parts[:, :, :, 7]
    tops, highs, lows = st[..., 0:7], st[..., 8:15], st[..., 16:23]
    scale = jnp.exp(tops - jnp.max(tops, axis=0, keepdims=True))
    total = jnp.sum(scale * (highs + lows), axis=0)
    weighted = jnp.sum(scale[..., None] * parts[:, :, :, :7], axis=0)
    attended = (weighted / total[..., None]).astype(BF16).reshape(rows_dev, width)

    feats = attended.reshape(rows_dev, zs, cs, members, k_dev).transpose(1, 2, 3, 0, 4)
    feats = jnp.stack(
        [
            jnp.concatenate([feats[(to - d) % zs] for d in range(zs)], axis=3)
            for to in range(zs)
        ]
    ).reshape(groups * members, rows_dev, zs * k_dev)
    feats, ups[2], down_other = lax.optimization_barrier((feats, ups[2], down_other))
    feats = exchange(feats, ALL)
    downs = reshard(*after((w_down, down_other), feats))
    feats = (
        feats.reshape(groups, members, rows_dev, zs * k_dev)
        .transpose(1, 0, 2, 3)
        .reshape(tokens, zs * k_dev)
    )
    wo_own, wo_pair = wo_parts[0], wo_parts[1]
    sent = pair(jnp.dot(feats, wo_pair, preferred_element_type=F32).astype(BF16))
    part = jnp.dot(feats, wo_own, preferred_element_type=F32) + sent.astype(F32)
    part = exchange(part.astype(BF16).reshape(members, block, chunk), MLP)
    gain = lax.dynamic_slice_in_dim(ln_gain, c * half + z * chunk, chunk, 0)

    hidden, row = pl.pallas_call(
        hidden_kernel,
        out_shape=(
            jax.ShapeDtypeStruct((block, chunk), F32),
            jax.ShapeDtypeStruct((block, chunk + HD), BF16),
        ),
        compiler_params=params(),
    )(part, res, gain[None])
    row, downs[1], downs[3] = lax.optimization_barrier((row, downs[1], downs[3]))
    rows = spread(row, MLP, members).reshape(tokens, chunk + HD)
    rows, downs[2] = lax.optimization_barrier((rows, downs[2]))

    both = jnp.broadcast_to(
        jnp.concatenate([keys_new, values_new], axis=1)[None], (members, rows_dev, 2 * width)
    )
    both = exchange(after(both, rows), MLP).reshape(group_rows, 2 * width)

    mine, theirs = up_project(rows, ups)
    theirs = pair(theirs)
    terms = []
    for d in range(zs):
        term = mine[d] + theirs[d].astype(F32)
        terms.append(shift(term.astype(BF16), -d, zs) if d else term)
    units = w_down.shape[0]
    act = pl.pallas_call(
        lambda *refs: act_kernel(width, units, zs, *refs),
        out_shape=jax.ShapeDtypeStruct((tokens, units), BF16),
        compiler_params=params(),
    )(*terms, gain_up)
    acts = [shift(act, d, zs) if d else act for d in range(zs)]
    down = down_project(acts, [pair(a) for a in acts], downs)
    down, both = lax.optimization_barrier((down, both))
    down = exchange(down.reshape(members, block, chunk), MLP)
    mixed = finish(down, hidden)
    mixed = exchange(mixed.reshape(groups, rows_dev, chunk), REQ)
    mixed = mixed.reshape(zs, cs, rows_dev, chunk).transpose(2, 1, 0, 3).reshape(rows_dev, width)

    valid = (accepted >= 0) & (dest_slot == member)[:, None]
    target = jnp.arange(requests, dtype=jnp.int32)[:, None] * tree_len + jnp.maximum(accepted, 0)
    chooser = jnp.any((target[:, :, None] == row_ids[None, None, :]) & valid[:, :, None], axis=0)
    picked = jnp.dot(chooser.astype(BF16), both, preferred_element_type=F32).astype(BF16)
    return (mixed, picked[:, :width][None], picked[:, width:][None])


def solution(mesh):
    groups, members = mesh.devices.shape
    side = math.isqrt(members)
    fine = Mesh(mesh.devices.reshape(groups // 2, 2, side, side), ALL)
    rows = P(ALL, None)
    pages = P(ALL, None, None)
    in_specs = (
        rows,
        rows,
        rows,
        rows,
        P(REQ, None, None),
        P(REQ),
        P(REQ, None),
        P(REQ),
        P(REQ, None),
        pages,
        pages,
        rows,
        P(None, ALL),
        rows,
        P(),
    )
    return jax.shard_map(
        local, mesh=fine, in_specs=in_specs, out_specs=(rows, pages, pages), check_vma=False
    )
```

```python
import math

import jax
import jax.numpy as jnp
from jax import lax
from jax.experimental import pallas as pl
from jax.experimental.pallas import tpu as pltpu
from jax.sharding import Mesh, PartitionSpec as P

HD = 128
NEG = -(2.0**100)
F32 = jnp.float32
BF16 = jnp.bfloat16
ALL = ("z", "c", "x", "y")
REQ = ("z", "c")
MLP = ("x", "y")
DN = (((1,), (1,)), ((), ()))


def attend_kernel(heads, scaling, q, k, v, dk, dv, mask, out):
    rows = q.shape[0]
    keys = k.shape[0] * k.shape[1]
    kk = jnp.concatenate([k[...].reshape(keys, k.shape[2]), dk[...]], axis=0)
    vv = jnp.concatenate([v[...].reshape(keys, v.shape[2]), dv[...]], axis=0)
    m = mask[...]
    span = [slice(h * HD, (h + 1) * HD) for h in range(heads)]
    scores = [
        jnp.where(
            m > 0,
            lax.dot_general(q[:, cols], kk[:, cols], DN, preferred_element_type=F32) * scaling,
            NEG,
        )
        for cols in span
    ]
    tops = [jnp.max(s, axis=1, keepdims=True).astype(BF16).astype(F32) for s in scores]
    weights = [jnp.exp(s - top) * m for s, top in zip(scores, tops)]
    totals = [jnp.sum(p, axis=1, keepdims=True) for p in weights]
    lane = lax.broadcasted_iota(jnp.int32, (rows, HD), 1)
    stats = jnp.zeros((rows, HD), F32)
    for h, cols in enumerate(span):
        w = jnp.dot(weights[h].astype(BF16), vv[:, cols], preferred_element_type=F32)
        out[:, cols] = w.astype(BF16)
        high = totals[h].astype(BF16).astype(F32)
        stats = jnp.where(lane == h, tops[h], stats)
        stats = jnp.where(lane == 8 + h, high, stats)
        stats = jnp.where(lane == 16 + h, totals[h] - high, stats)
    out[:, heads * HD :] = stats.astype(BF16)


def attend(q, key_cache, value_cache, dk, dv, mask, steps):
    rows, width = q.shape
    pages, page_len, _ = key_cache.shape
    wide = width // steps
    heads = wide // HD
    col = lambda i: (0, i)
    col3 = lambda i: (0, 0, i)

    def body(*refs):
        attend_kernel(heads, 1.0 / math.sqrt(HD), *refs)

    return pl.pallas_call(
        body,
        grid=(steps,),
        in_specs=[
            pl.BlockSpec((rows, wide), col),
            pl.BlockSpec((pages, page_len, wide), col3),
            pl.BlockSpec((pages, page_len, wide), col3),
            pl.BlockSpec((dk.shape[0], wide), col),
            pl.BlockSpec((dv.shape[0], wide), col),
            pl.BlockSpec(mask.shape, lambda i: (0, 0)),
        ],
        out_specs=pl.BlockSpec((rows, wide + HD), col),
        out_shape=jax.ShapeDtypeStruct((rows, steps * (wide + HD)), BF16),
        compiler_params=pltpu.CompilerParams(vmem_limit_bytes=58 * 1024 * 1024),
        cost_estimate=pl.CostEstimate(
            flops=4 * rows * pages * page_len * width,
            bytes_accessed=4 * pages * page_len * width,
            transcendentals=rows * pages * page_len * width // HD,
        ),
    )(q, key_cache, value_cache, dk, dv, mask)


def pair(x):
    return lax.ppermute(x, "c", [(0, 1), (1, 0)])


def shift(x, step, size):
    return lax.ppermute(x, "z", [(i, (i + step) % size) for i in range(size)])


def after(x, first):
    return lax.optimization_barrier((x, first))[0]


def gain_kernel(place, gain, weight, out):
    high = gain[...].astype(BF16).astype(F32)
    row = lax.broadcasted_iota(jnp.int32, (8, gain.shape[1]), 0)
    both = jnp.where(row == 0, high, jnp.where(row == 1, gain[...] - high, 0.0)).astype(BF16)
    got = lax.dot_general(both, weight[...], DN, preferred_element_type=F32)
    out[0] = jnp.broadcast_to(got[0:1] + got[1:2], got.shape)


def hidden_kernel(parts, res, gain, hidden_out, row_out):
    hidden = res[...] + jnp.sum(parts[...].astype(F32), axis=0)
    hidden_out[...] = hidden
    rows, chunk = hidden.shape
    mean = jnp.mean(hidden, axis=1, keepdims=True)
    centered = hidden - mean
    dev = jnp.sum(centered * centered, axis=1, keepdims=True)
    row_out[:, :chunk] = (centered * gain[...]).astype(BF16)
    lane = lax.broadcasted_iota(jnp.int32, (rows, HD), 1)
    stats = jnp.zeros((rows, HD), F32)
    at = 0
    for value in (mean, dev):
        for _ in range(3):
            high = value.astype(BF16).astype(F32)
            stats = jnp.where(lane == at, high, stats)
            value = value - high
            at += 1
    row_out[:, chunk:] = stats.astype(BF16)


def fetch(sources, buffer, sems):
    copies = []
    for d, source in enumerate(sources):
        copies.append(pltpu.make_async_copy(source, buffer.at[d], sems.at[d]))
        copies[-1].start()
    return copies


def up_kernel(n, *refs):
    rows = refs[0]
    outs = refs[n + 1 : n + 3]
    buffer = refs[n + 3]
    copies = fetch(refs[1 : n + 1], buffer, refs[n + 4])
    chunk = buffer.shape[3]
    wide = outs[0].shape[2]
    g = rows[:, :chunk]
    st = rows[:, chunk:].astype(F32)
    lane = lax.broadcasted_iota(jnp.int32, st.shape, 1)
    st = jnp.where(lane < 6, st, 0.0)
    none = jnp.zeros_like(st)
    beside = [jnp.concatenate([none, pltpu.roll(st, by, 1)], axis=1) for by in (102, 96)]
    for d in range(n):
        copies[d].wait()
        for e in range(2):
            w = buffer[d, e]
            w = jnp.concatenate([w, jnp.zeros((wide - w.shape[0], chunk), BF16)], axis=0)
            got = lax.dot_general(g, w, DN, preferred_element_type=F32)
            outs[e][d] = (got + beside[e]).astype(BF16)


def act_kernel(width, units, n, *refs):
    terms = [refs[d][...].astype(F32) for d in range(n)]
    gain = refs[n]
    out = refs[n + 1]
    chunk = width // (2 * n)
    pre = terms[0]
    for d in range(1, n):
        pre = pre + terms[d]
    pre = pre[:, :units]
    means, devs = [], []
    for t in terms:
        for at in (units + 6, units):
            means.append(t[:, at : at + 1] + t[:, at + 1 : at + 2] + t[:, at + 2 : at + 3])
            devs.append(t[:, at + 3 : at + 4] + t[:, at + 4 : at + 5] + t[:, at + 5 : at + 6])
    mean = sum(means[1:], means[0]) / (2 * n)
    var = sum(devs[1:], devs[0])
    for k, value in enumerate(means):
        off = value - mean
        var = var + chunk * off * off
        pre = pre + off * gain[k, 0:1, :]
    out[...] = jnp.maximum(lax.rsqrt(var / width + 1e-05) * pre, 0.0).astype(BF16)


def down_kernel(n, *refs):
    buffer = refs[3 * n + 1]
    copies = fetch(refs[2 * n : 3 * n], buffer, refs[3 * n + 2])
    total = None
    for d in range(n):
        copies[d].wait()
        for e in range(2):
            term = jnp.dot(refs[e * n + d][...], buffer[d, e], preferred_element_type=F32)
            total = term if total is None else total + term
    refs[3 * n][...] = total.astype(BF16)


def finish_kernel(parts, hidden, out, total):
    step = pl.program_id(0)

    @pl.when(step == 0)
    def _():
        total[...] = hidden[...]

    total[...] += jnp.sum(parts[...].astype(F32), axis=0)

    @pl.when(step == pl.num_programs(0) - 1)
    def _():
        out[...] = total[...].astype(BF16)


def params(mib=32):
    return pltpu.CompilerParams(vmem_limit_bytes=mib * 1024 * 1024)


def cut_kernel(n, spots, a, b, *outs):
    for d in range(n):

        @pl.when(pl.program_id(0) == d)
        def _():
            outs[d][0] = a[...]
            outs[d][1] = b[...]


def cut(spots, a, b, n, chunk):
    rows = a.shape[0]
    whole = pl.BlockSpec((2, rows, chunk), lambda i, spots: (0, 0, 0))
    return pl.pallas_call(
        lambda *refs: cut_kernel(n, *refs),
        grid_spec=pltpu.PrefetchScalarGridSpec(
            num_scalar_prefetch=1,
            grid=(n,),
            in_specs=[
                pl.BlockSpec((rows, chunk), lambda i, spots: (0, spots[i])),
                pl.BlockSpec((rows, chunk), lambda i, spots: (0, spots[n + i])),
            ],
            out_specs=[whole] * n,
        ),
        out_shape=[jax.ShapeDtypeStruct((2, rows, chunk), BF16)] * n,
        compiler_params=params(),
    )(spots, a, b)


def gain_products(order, gain, weight, chunk):
    units = weight.shape[0]
    n = order.shape[0]
    return pl.pallas_call(
        gain_kernel,
        grid_spec=pltpu.PrefetchScalarGridSpec(
            num_scalar_prefetch=1,
            grid=(n,),
            in_specs=[
                pl.BlockSpec((1, chunk), lambda i, order: (0, order[i])),
                pl.BlockSpec((units, chunk), lambda i, order: (0, order[i])),
            ],
            out_specs=pl.BlockSpec((1, 8, units), lambda i, order: (i, 0, 0)),
        ),
        out_shape=jax.ShapeDtypeStruct((n, 8, units), F32),
        compiler_params=params(),
    )(order, gain, weight)


def weight_specs(weights):
    n = len(weights)
    return (
        [pl.BlockSpec(memory_space=pltpu.HBM)] * n,
        [pltpu.VMEM((n,) + weights[0].shape, BF16), pltpu.SemaphoreType.DMA((n,))],
    )


def up_project(rows, weights):
    n = len(weights)
    tokens = rows.shape[0]
    specs, scratch = weight_specs(weights)
    return pl.pallas_call(
        lambda *refs: up_kernel(n, *refs),
        in_specs=[pl.BlockSpec(memory_space=pltpu.VMEM)] + specs,
        out_shape=[jax.ShapeDtypeStruct((n, tokens, 256), BF16)] * 2,
        scratch_shapes=scratch,
        compiler_params=params(24),
    )(rows, *weights)


def down_project(own, other, weights):
    n = len(weights)
    specs, scratch = weight_specs(weights)
    return pl.pallas_call(
        lambda *refs: down_kernel(n, *refs),
        in_specs=[pl.BlockSpec(memory_space=pltpu.VMEM)] * (2 * n) + specs,
        out_shape=jax.ShapeDtypeStruct((own[0].shape[0], weights[0].shape[2]), BF16),
        scratch_shapes=scratch,
        compiler_params=params(24),
    )(*own, *other, *weights)


def finish(parts, hidden):
    count, block, chunk = parts.shape
    per = count // 4
    return pl.pallas_call(
        finish_kernel,
        grid=(4,),
        in_specs=[
            pl.BlockSpec((per, block, chunk), lambda i: (i, 0, 0)),
            pl.BlockSpec((block, chunk), lambda i: (0, 0)),
        ],
        out_specs=pl.BlockSpec((block, chunk), lambda i: (0, 0)),
        out_shape=jax.ShapeDtypeStruct((block, chunk), BF16),
        scratch_shapes=[pltpu.VMEM((block, chunk), F32)],
        compiler_params=params(),
    )(parts, hidden)


def spread(x, axes, count):
    return lax.all_to_all(
        jnp.broadcast_to(x[None], (count,) + x.shape), axes, split_axis=0, concat_axis=0
    )


def exchange(x, axes):
    return lax.all_to_all(x, axes, split_axis=0, concat_axis=0)


def local(
    queries,
    keys_new,
    values_new,
    resid,
    tree_mask,
    tree_size,
    accepted,
    dest_slot,
    page_table,
    key_cache,
    value_cache,
    w_out,
    w_up,
    w_down,
    ln_gain,
):
    zs, cs, xs, ys = (lax.axis_size(a) for a in ALL)
    members = xs * ys
    groups = zs * cs
    z = lax.axis_index("z")
    c = lax.axis_index("c")
    member = lax.axis_index(MLP)
    rows_dev, width = queries.shape
    requests, tree_len = tree_mask.shape[:2]
    group_rows = requests * tree_len
    pages_dev, page_len, _ = key_cache.shape
    tokens = group_rows * groups
    heads = width // HD
    half = width // cs
    chunk = half // zs
    block = tokens // members

    wide_q = jnp.broadcast_to(queries[None], (members,) + queries.shape)
    group_q = exchange(wide_q, MLP).reshape(group_rows, width)

    turn = (z + jnp.arange(zs, dtype=jnp.int32)) % zs
    own_turn, other_turn = c * zs + turn, (1 - c) * zs + turn

    def send(pieces):
        return [shift(p, d, zs) if d else p for d, p in enumerate(pieces)]

    k_dev = w_out.shape[0]
    wo = after(w_out, wide_q)
    wo_parts = send(cut(jnp.concatenate([own_turn, other_turn]), wo, wo, zs, chunk))
    wo_parts = jnp.concatenate(wo_parts, axis=1)

    def swap(w):
        return pair(lax.dynamic_slice_in_dim(w, (1 - c) * half, half, 1))

    def reshard(w, other):
        return send(cut(jnp.concatenate([own_turn, turn]), w, other, zs, chunk))

    def swap(w):
        return pair(lax.dynamic_slice_in_dim(w, (1 - c) * half, half, 1))

    up_w = after(w_up.T, wide_q)
    ups = reshard(up_w, swap(up_w))
    order = jnp.stack(
        [(c + e) % cs * zs + (z + d) % zs for d in range(zs) for e in range(cs)]
    ).astype(jnp.int32)
    gain_up = gain_products(order, ln_gain[None], up_w, chunk)

    page_ids = member * pages_dev + jnp.arange(pages_dev, dtype=jnp.int32)
    owners = jnp.any(page_table[:, :, None] == page_ids[None, None, :], axis=1)
    pool_mask = jnp.repeat(jnp.repeat(owners, page_len, axis=1), tree_len, axis=0).astype(F32)
    draft_pad = 16
    slot_ids = member * rows_dev + jnp.arange(draft_pad, dtype=jnp.int32)
    row_ids = jnp.arange(group_rows, dtype=jnp.int32)
    tree_cols = jnp.tile(tree_mask.reshape(group_rows, tree_len), (1, requests))
    live = jnp.repeat(tree_size, tree_len) > (row_ids % tree_len)
    tree_ok = (
        (tree_cols == 1)
        & live[None, :]
        & ((row_ids // tree_len)[:, None] == (row_ids // tree_len)[None, :])
    ).astype(F32)
    pick = (row_ids[:, None] == slot_ids[None, :]) & (
        jnp.arange(draft_pad, dtype=jnp.int32) < rows_dev
    )[None, :]
    draft_mask = jnp.dot(tree_ok, pick.astype(F32))
    pad = ((0, draft_pad - rows_dev), (0, 0))
    parts = attend(
        group_q,
        key_cache,
        value_cache,
        jnp.pad(keys_new, pad),
        jnp.pad(values_new, pad),
        jnp.concatenate([pool_mask, draft_mask], axis=1),
        heads // 7,
    )

    parts, ups[1], ups[3], wo_parts, gain_up = lax.optimization_barrier(
        (parts, ups[1], ups[3], wo_parts, gain_up)
    )
    down_other = swap(after(w_down, parts))

    res = after(resid, parts)
    res = jnp.stack(
        [
            lax.dynamic_slice_in_dim(res, c * half, half, 1),
            pair(lax.dynamic_slice_in_dim(res, (1 - c) * half, half, 1)),
        ]
    ).reshape(cs * rows_dev, half)
    res_parts = []
    for d in range(zs):
        part = lax.dynamic_slice_in_dim(res, ((z + d) % zs) * chunk, chunk, 1)
        res_parts.append(shift(part, d, zs) if d else part)
    res = jnp.concatenate(res_parts, axis=0)
    at = jnp.arange(block, dtype=jnp.int32)
    source = ((z - at // (cs * rows_dev)) % zs) * cs + (c + at // rows_dev) % cs
    order = at[:, None] == (source * rows_dev + at % rows_dev)[None, :]
    res = jnp.dot(order.astype(BF16), res, preferred_element_type=F32)

    parts = exchange(parts.reshape(members, rows_dev, parts.shape[1]), MLP)
    parts = parts.reshape(members, rows_dev, heads // 7, 8, HD).astype(F32)
    st = parts[:, :, :, 7]
    tops, highs, lows = st[..., 0:7], st[..., 8:15], st[..., 16:23]
    scale = jnp.exp(tops - jnp.max(tops, axis=0, keepdims=True))
    total = jnp.sum(scale * (highs + lows), axis=0)
    weighted = jnp.sum(scale[..., None] * parts[:, :, :, :7], axis=0)
    attended = (weighted / total[..., None]).astype(BF16).reshape(rows_dev, width)

    feats = attended.reshape(rows_dev, zs, cs, members, k_dev).transpose(1, 2, 3, 0, 4)
    feats = jnp.stack(
        [
            jnp.concatenate([feats[(to - d) % zs] for d in range(zs)], axis=3)
            for to in range(zs)
        ]
    ).reshape(groups * members, rows_dev, zs * k_dev)
    both = jnp.broadcast_to(
        jnp.concatenate([keys_new, values_new], axis=1)[None], (members, rows_dev, 2 * width)
    )
    feats, ups[2], down_other, res, both = lax.optimization_barrier(
        (feats, ups[2], down_other, res, both)
    )
    feats = exchange(feats, ALL)
    feats = (
        feats.reshape(groups, members, rows_dev, zs * k_dev)
        .transpose(1, 0, 2, 3)
        .reshape(tokens, zs * k_dev)
    )
    wo_own, wo_pair = wo_parts[0], wo_parts[1]
    sent = pair(jnp.dot(feats, wo_pair, preferred_element_type=F32).astype(BF16))
    part = jnp.dot(feats, wo_own, preferred_element_type=F32) + sent.astype(F32)
    part = part.astype(BF16).reshape(members, block, chunk)
    downs = reshard(*after((w_down, down_other), part))
    part = exchange(part, MLP)
    gain = lax.dynamic_slice_in_dim(ln_gain, c * half + z * chunk, chunk, 0)

    hidden, row = pl.pallas_call(
        hidden_kernel,
        out_shape=(
            jax.ShapeDtypeStruct((block, chunk), F32),
            jax.ShapeDtypeStruct((block, chunk + HD), BF16),
        ),
        compiler_params=params(),
    )(part, res, gain[None])
    rows = spread(row, MLP, members).reshape(tokens, chunk + HD)
    rows, downs = lax.optimization_barrier((rows, downs))

    both = exchange(after(both, rows), MLP)

    mine, theirs = up_project(rows, ups)
    theirs = pair(theirs)
    terms = []
    for d in range(zs):
        term = mine[d].astype(F32) + theirs[d].astype(F32)
        terms.append(shift(term.astype(BF16), -d, zs) if d else term)
    units = w_down.shape[0]
    act = pl.pallas_call(
        lambda *refs: act_kernel(width, units, zs, *refs),
        out_shape=jax.ShapeDtypeStruct((tokens, units), BF16),
        compiler_params=params(),
    )(*terms, gain_up)
    acts = [shift(act, d, zs) if d else act for d in range(zs)]
    down = down_project(acts, [pair(a) for a in acts], downs)
    down, both = lax.optimization_barrier((down, both))
    down = exchange(down.reshape(members, block, chunk), MLP)
    mixed = finish(down, hidden)
    mixed = exchange(mixed.reshape(groups, rows_dev, chunk), REQ)
    mixed = mixed.reshape(zs, cs, rows_dev, chunk).transpose(2, 1, 0, 3).reshape(rows_dev, width)

    valid = (accepted >= 0) & (dest_slot == member)[:, None]
    target = jnp.arange(requests, dtype=jnp.int32)[:, None] * tree_len + jnp.maximum(accepted, 0)
    chooser = jnp.any((target[:, :, None] == row_ids[None, None, :]) & valid[:, :, None], axis=0)
    both = both.reshape(group_rows, 2 * width)
    picked = jnp.dot(chooser.astype(BF16), both, preferred_element_type=F32).astype(BF16)
    return (mixed, picked[:, :width][None], picked[:, width:][None])


def solution(mesh):
    groups, members = mesh.devices.shape
    side = math.isqrt(members)
    fine = Mesh(mesh.devices.reshape(groups // 2, 2, side, side), ALL)
    rows = P(ALL, None)
    pages = P(ALL, None, None)
    in_specs = (
        rows,
        rows,
        rows,
        rows,
        P(REQ, None, None),
        P(REQ),
        P(REQ, None),
        P(REQ),
        P(REQ, None),
        pages,
        pages,
        rows,
        P(None, ALL),
        rows,
        P(),
    )
    return jax.shard_map(
        local, mesh=fine, in_specs=in_specs, out_specs=(rows, pages, pages), check_vma=False
    )
```

```python
import math

import jax
import jax.numpy as jnp
from jax import lax
from jax.experimental import pallas as pl
from jax.experimental.pallas import tpu as pltpu
from jax.sharding import Mesh, PartitionSpec as P

HD = 128
NEG = -(2.0**100)
F32 = jnp.float32
BF16 = jnp.bfloat16
ALL = ("z", "c", "x", "y")
REQ = ("z", "c")
MLP = ("x", "y")
DN = (((1,), (1,)), ((), ()))


def attend_kernel(heads, scaling, q, k, v, dk, dv, mask, out):
    rows = q.shape[0]
    keys = k.shape[0] * k.shape[1]
    kk = jnp.concatenate([k[...].reshape(keys, k.shape[2]), dk[...]], axis=0)
    vv = jnp.concatenate([v[...].reshape(keys, v.shape[2]), dv[...]], axis=0)
    m = mask[...]
    span = [slice(h * HD, (h + 1) * HD) for h in range(heads)]
    scores = [
        jnp.where(
            m > 0,
            lax.dot_general(q[:, cols], kk[:, cols], DN, preferred_element_type=F32) * scaling,
            NEG,
        )
        for cols in span
    ]
    tops = [jnp.max(s, axis=1, keepdims=True).astype(BF16).astype(F32) for s in scores]
    weights = [jnp.exp(s - top) * m for s, top in zip(scores, tops)]
    totals = [jnp.sum(p, axis=1, keepdims=True) for p in weights]
    lane = lax.broadcasted_iota(jnp.int32, (rows, HD), 1)
    stats = jnp.zeros((rows, HD), F32)
    for h, cols in enumerate(span):
        w = jnp.dot(weights[h].astype(BF16), vv[:, cols], preferred_element_type=F32)
        out[:, cols] = w.astype(BF16)
        high = totals[h].astype(BF16).astype(F32)
        stats = jnp.where(lane == h, tops[h], stats)
        stats = jnp.where(lane == 8 + h, high, stats)
        stats = jnp.where(lane == 16 + h, totals[h] - high, stats)
    out[:, heads * HD :] = stats.astype(BF16)


def attend(q, key_cache, value_cache, dk, dv, mask, steps):
    rows, width = q.shape
    pages, page_len, _ = key_cache.shape
    wide = width // steps
    heads = wide // HD
    col = lambda i: (0, i)
    col3 = lambda i: (0, 0, i)

    def body(*refs):
        attend_kernel(heads, 1.0 / math.sqrt(HD), *refs)

    return pl.pallas_call(
        body,
        grid=(steps,),
        in_specs=[
            pl.BlockSpec((rows, wide), col),
            pl.BlockSpec((pages, page_len, wide), col3),
            pl.BlockSpec((pages, page_len, wide), col3),
            pl.BlockSpec((dk.shape[0], wide), col),
            pl.BlockSpec((dv.shape[0], wide), col),
            pl.BlockSpec(mask.shape, lambda i: (0, 0)),
        ],
        out_specs=pl.BlockSpec((rows, wide + HD), col),
        out_shape=jax.ShapeDtypeStruct((rows, steps * (wide + HD)), BF16),
        compiler_params=pltpu.CompilerParams(vmem_limit_bytes=58 * 1024 * 1024),
        cost_estimate=pl.CostEstimate(
            flops=4 * rows * pages * page_len * width,
            bytes_accessed=4 * pages * page_len * width,
            transcendentals=rows * pages * page_len * width // HD,
        ),
    )(q, key_cache, value_cache, dk, dv, mask)


def pair(x):
    return lax.ppermute(x, "c", [(0, 1), (1, 0)])


def shift(x, step, size, axis="z"):
    return lax.ppermute(x, axis, [(i, (i + step) % size) for i in range(size)])


def after(x, first):
    return lax.optimization_barrier((x, first))[0]


def gain_kernel(place, gain, weight, out):
    high = gain[...].astype(BF16).astype(F32)
    row = lax.broadcasted_iota(jnp.int32, (8, gain.shape[1]), 0)
    both = jnp.where(row == 0, high, jnp.where(row == 1, gain[...] - high, 0.0)).astype(BF16)
    got = lax.dot_general(both, weight[...], DN, preferred_element_type=F32)
    out[0] = jnp.broadcast_to(got[0:1] + got[1:2], got.shape)


def hidden_kernel(parts, res, gain, hidden_out, row_out):
    hidden = res[...] + jnp.sum(parts[...].astype(F32), axis=0)
    hidden_out[...] = hidden
    rows, chunk = hidden.shape
    mean = jnp.mean(hidden, axis=1, keepdims=True)
    centered = hidden - mean
    dev = jnp.sum(centered * centered, axis=1, keepdims=True)
    row_out[:, :chunk] = (centered * gain[...]).astype(BF16)
    lane = lax.broadcasted_iota(jnp.int32, (rows, HD), 1)
    stats = jnp.zeros((rows, HD), F32)
    at = 0
    for value in (mean, dev):
        for _ in range(3):
            high = value.astype(BF16).astype(F32)
            stats = jnp.where(lane == at, high, stats)
            value = value - high
            at += 1
    row_out[:, chunk:] = stats.astype(BF16)


def fetch(sources, buffer, sems):
    copies = []
    for d, source in enumerate(sources):
        copies.append(pltpu.make_async_copy(source, buffer.at[d], sems.at[d]))
        copies[-1].start()
    return copies


def up_kernel(n, *refs):
    rows = refs[0]
    outs = refs[n + 1 : n + 3]
    buffer = refs[n + 3]
    copies = fetch(refs[1 : n + 1], buffer, refs[n + 4])
    chunk = buffer.shape[3]
    wide = outs[0].shape[2]
    g = rows[:, :chunk]
    st = rows[:, chunk:].astype(F32)
    lane = lax.broadcasted_iota(jnp.int32, st.shape, 1)
    st = jnp.where(lane < 6, st, 0.0)
    none = jnp.zeros_like(st)
    beside = [jnp.concatenate([none, pltpu.roll(st, by, 1)], axis=1) for by in (102, 96)]
    for d in range(n):
        copies[d].wait()
        for e in range(2):
            w = buffer[d, e]
            w = jnp.concatenate([w, jnp.zeros((wide - w.shape[0], chunk), BF16)], axis=0)
            got = lax.dot_general(g, w, DN, preferred_element_type=F32)
            outs[e][d] = (got + beside[e]).astype(BF16)


def act_kernel(width, units, n, *refs):
    terms = [refs[d][...].astype(F32) for d in range(n)]
    gain = refs[n]
    out = refs[n + 1]
    chunk = width // (2 * n)
    pre = terms[0]
    for d in range(1, n):
        pre = pre + terms[d]
    pre = pre[:, :units]
    means, devs = [], []
    for t in terms:
        for at in (units + 6, units):
            means.append(t[:, at : at + 1] + t[:, at + 1 : at + 2] + t[:, at + 2 : at + 3])
            devs.append(t[:, at + 3 : at + 4] + t[:, at + 4 : at + 5] + t[:, at + 5 : at + 6])
    mean = sum(means[1:], means[0]) / (2 * n)
    var = sum(devs[1:], devs[0])
    for k, value in enumerate(means):
        off = value - mean
        var = var + chunk * off * off
        pre = pre + off * gain[k, 0:1, :]
    out[...] = jnp.maximum(lax.rsqrt(var / width + 1e-05) * pre, 0.0).astype(BF16)


def down_kernel(n, *refs):
    buffer = refs[3 * n + 1]
    copies = fetch(refs[2 * n : 3 * n], buffer, refs[3 * n + 2])
    total = None
    for d in range(n):
        copies[d].wait()
        for e in range(2):
            term = jnp.dot(refs[e * n + d][...], buffer[d, e], preferred_element_type=F32)
            total = term if total is None else total + term
    refs[3 * n][...] = total.astype(BF16)


def finish_kernel(parts, hidden, out, total):
    step = pl.program_id(0)

    @pl.when(step == 0)
    def _():
        total[...] = hidden[...]

    total[...] += jnp.sum(parts[...].astype(F32), axis=0)

    @pl.when(step == pl.num_programs(0) - 1)
    def _():
        out[...] = total[...].astype(BF16)


def params(mib=32):
    return pltpu.CompilerParams(vmem_limit_bytes=mib * 1024 * 1024)


def cut_kernel(n, spots, a, b, *outs):
    for d in range(n):

        @pl.when(pl.program_id(0) == d)
        def _():
            outs[d][0] = a[...]
            outs[d][1] = b[...]


def cut(spots, a, b, n, chunk):
    rows = a.shape[0]
    whole = pl.BlockSpec((2, rows, chunk), lambda i, spots: (0, 0, 0))
    return pl.pallas_call(
        lambda *refs: cut_kernel(n, *refs),
        grid_spec=pltpu.PrefetchScalarGridSpec(
            num_scalar_prefetch=1,
            grid=(n,),
            in_specs=[
                pl.BlockSpec((rows, chunk), lambda i, spots: (0, spots[i])),
                pl.BlockSpec((rows, chunk), lambda i, spots: (0, spots[n + i])),
            ],
            out_specs=[whole] * n,
        ),
        out_shape=[jax.ShapeDtypeStruct((2, rows, chunk), BF16)] * n,
        compiler_params=params(),
    )(spots, a, b)


def gain_products(order, gain, weight, chunk):
    units = weight.shape[0]
    n = order.shape[0]
    return pl.pallas_call(
        gain_kernel,
        grid_spec=pltpu.PrefetchScalarGridSpec(
            num_scalar_prefetch=1,
            grid=(n,),
            in_specs=[
                pl.BlockSpec((1, chunk), lambda i, order: (0, order[i])),
                pl.BlockSpec((units, chunk), lambda i, order: (0, order[i])),
            ],
            out_specs=pl.BlockSpec((1, 8, units), lambda i, order: (i, 0, 0)),
        ),
        out_shape=jax.ShapeDtypeStruct((n, 8, units), F32),
        compiler_params=params(),
    )(order, gain, weight)


def weight_specs(weights):
    n = len(weights)
    return (
        [pl.BlockSpec(memory_space=pltpu.HBM)] * n,
        [pltpu.VMEM((n,) + weights[0].shape, BF16), pltpu.SemaphoreType.DMA((n,))],
    )


def up_project(rows, weights):
    n = len(weights)
    tokens = rows.shape[0]
    specs, scratch = weight_specs(weights)
    return pl.pallas_call(
        lambda *refs: up_kernel(n, *refs),
        in_specs=[pl.BlockSpec(memory_space=pltpu.VMEM)] + specs,
        out_shape=[jax.ShapeDtypeStruct((n, tokens, 256), BF16)] * 2,
        scratch_shapes=scratch,
        compiler_params=params(24),
    )(rows, *weights)


def down_project(own, other, weights):
    n = len(weights)
    specs, scratch = weight_specs(weights)
    return pl.pallas_call(
        lambda *refs: down_kernel(n, *refs),
        in_specs=[pl.BlockSpec(memory_space=pltpu.VMEM)] * (2 * n) + specs,
        out_shape=jax.ShapeDtypeStruct((own[0].shape[0], weights[0].shape[2]), BF16),
        scratch_shapes=scratch,
        compiler_params=params(24),
    )(*own, *other, *weights)


def finish(parts, hidden):
    count, block, chunk = parts.shape
    per = count // 4
    return pl.pallas_call(
        finish_kernel,
        grid=(4,),
        in_specs=[
            pl.BlockSpec((per, block, chunk), lambda i: (i, 0, 0)),
            pl.BlockSpec((block, chunk), lambda i: (0, 0)),
        ],
        out_specs=pl.BlockSpec((block, chunk), lambda i: (0, 0)),
        out_shape=jax.ShapeDtypeStruct((block, chunk), BF16),
        scratch_shapes=[pltpu.VMEM((block, chunk), F32)],
        compiler_params=params(),
    )(parts, hidden)


def spread(x, axes, count):
    return lax.all_to_all(
        jnp.broadcast_to(x[None], (count,) + x.shape), axes, split_axis=0, concat_axis=0
    )


def exchange(x, axes):
    return lax.all_to_all(x, axes, split_axis=0, concat_axis=0)


def local(
    queries,
    keys_new,
    values_new,
    resid,
    tree_mask,
    tree_size,
    accepted,
    dest_slot,
    page_table,
    key_cache,
    value_cache,
    w_out,
    w_up,
    w_down,
    ln_gain,
):
    zs, cs, xs, ys = (lax.axis_size(a) for a in ALL)
    members = xs * ys
    groups = zs * cs
    z = lax.axis_index("z")
    c = lax.axis_index("c")
    member = lax.axis_index(MLP)
    rows_dev, width = queries.shape
    requests, tree_len = tree_mask.shape[:2]
    group_rows = requests * tree_len
    pages_dev, page_len, _ = key_cache.shape
    tokens = group_rows * groups
    heads = width // HD
    half = width // cs
    chunk = half // zs
    block = tokens // members

    wide_q = jnp.broadcast_to(queries[None], (members,) + queries.shape)
    group_q = exchange(wide_q, MLP).reshape(group_rows, width)

    turn = (z + jnp.arange(zs, dtype=jnp.int32)) % zs
    own_turn, other_turn = c * zs + turn, (1 - c) * zs + turn

    def send(pieces):
        return [shift(p, d, zs) if d else p for d, p in enumerate(pieces)]

    k_dev = w_out.shape[0]

    def swap(w):
        return pair(lax.dynamic_slice_in_dim(w, (1 - c) * half, half, 1))

    def reshard(w, other):
        return cut(jnp.concatenate([own_turn, turn]), w, other, zs, chunk)

    def swap(w):
        return pair(lax.dynamic_slice_in_dim(w, (1 - c) * half, half, 1))

    up_w = after(w_up.T, wide_q)
    ups = send(reshard(up_w, swap(up_w)))

    page_ids = member * pages_dev + jnp.arange(pages_dev, dtype=jnp.int32)
    owners = jnp.any(page_table[:, :, None] == page_ids[None, None, :], axis=1)
    pool_mask = jnp.repeat(jnp.repeat(owners, page_len, axis=1), tree_len, axis=0).astype(F32)
    draft_pad = 16
    slot_ids = member * rows_dev + jnp.arange(draft_pad, dtype=jnp.int32)
    row_ids = jnp.arange(group_rows, dtype=jnp.int32)
    tree_cols = jnp.tile(tree_mask.reshape(group_rows, tree_len), (1, requests))
    live = jnp.repeat(tree_size, tree_len) > (row_ids % tree_len)
    tree_ok = (
        (tree_cols == 1)
        & live[None, :]
        & ((row_ids // tree_len)[:, None] == (row_ids // tree_len)[None, :])
    ).astype(F32)
    pick = (row_ids[:, None] == slot_ids[None, :]) & (
        jnp.arange(draft_pad, dtype=jnp.int32) < rows_dev
    )[None, :]
    draft_mask = jnp.dot(tree_ok, pick.astype(F32))
    pad = ((0, draft_pad - rows_dev), (0, 0))
    parts = attend(
        group_q,
        key_cache,
        value_cache,
        jnp.pad(keys_new, pad),
        jnp.pad(values_new, pad),
        jnp.concatenate([pool_mask, draft_mask], axis=1),
        heads // 7,
    )

    parts, ups[1], ups[3] = lax.optimization_barrier((parts, ups[1], ups[3]))

    wo = after(w_out, parts)
    wo_parts = send(cut(jnp.concatenate([own_turn, other_turn]), wo, wo, zs, chunk))
    wo_parts = jnp.concatenate(wo_parts, axis=1)
    down_other = swap(after(w_down, parts))

    res = after(resid, parts)
    res = jnp.stack(
        [
            lax.dynamic_slice_in_dim(res, c * half, half, 1),
            pair(lax.dynamic_slice_in_dim(res, (1 - c) * half, half, 1)),
        ]
    ).reshape(cs * rows_dev, half)
    res_parts = []
    for d in range(zs):
        part = lax.dynamic_slice_in_dim(res, ((z + d) % zs) * chunk, chunk, 1)
        res_parts.append(shift(part, d, zs) if d else part)
    res = jnp.concatenate(res_parts, axis=0)
    at = jnp.arange(block, dtype=jnp.int32)
    source = ((z - at // (cs * rows_dev)) % zs) * cs + (c + at // rows_dev) % cs
    order = at[:, None] == (source * rows_dev + at % rows_dev)[None, :]
    res = jnp.dot(order.astype(BF16), res, preferred_element_type=F32)

    parts = exchange(parts.reshape(members, rows_dev, parts.shape[1]), MLP)
    parts = parts.reshape(members, rows_dev, heads // 7, 8, HD).astype(F32)
    st = parts[:, :, :, 7]
    tops, highs, lows = st[..., 0:7], st[..., 8:15], st[..., 16:23]
    scale = jnp.exp(tops - jnp.max(tops, axis=0, keepdims=True))
    total = jnp.sum(scale * (highs + lows), axis=0)
    weighted = jnp.sum(scale[..., None] * parts[:, :, :, :7], axis=0)
    attended = (weighted / total[..., None]).astype(BF16).reshape(rows_dev, width)

    feats = attended.reshape(rows_dev, zs, cs, members, k_dev).transpose(1, 2, 3, 0, 4)
    feats = jnp.stack(
        [
            jnp.concatenate([feats[(to - d) % zs] for d in range(zs)], axis=3)
            for to in range(zs)
        ]
    ).reshape(groups * members, rows_dev, zs * k_dev)
    feats, ups[2], down_other, res = lax.optimization_barrier((feats, ups[2], down_other, res))
    downs = reshard(*after((w_down, down_other), feats))
    draft_k, draft_v = after((keys_new, values_new), feats)
    both = jnp.concatenate([draft_k, draft_v], axis=1)
    both = [shift(both, d, xs, "x") if d else both for d in range(xs)]
    feats = exchange(feats, ALL)
    feats = (
        feats.reshape(groups, members, rows_dev, zs * k_dev)
        .transpose(1, 0, 2, 3)
        .reshape(tokens, zs * k_dev)
    )
    wo_own, wo_pair = wo_parts[0], wo_parts[1]
    sent = pair(jnp.dot(feats, wo_pair, preferred_element_type=F32).astype(BF16))
    part = jnp.dot(feats, wo_own, preferred_element_type=F32) + sent.astype(F32)
    part = part.astype(BF16).reshape(members, block, chunk)
    part, downs = lax.optimization_barrier((part, downs))
    downs = send(downs)
    part = exchange(part, MLP)
    gain = lax.dynamic_slice_in_dim(ln_gain, c * half + z * chunk, chunk, 0)

    hidden, row = pl.pallas_call(
        hidden_kernel,
        out_shape=(
            jax.ShapeDtypeStruct((block, chunk), F32),
            jax.ShapeDtypeStruct((block, chunk + HD), BF16),
        ),
        compiler_params=params(),
    )(part, res, gain[None])
    row, downs[1], downs[3] = lax.optimization_barrier((row, downs[1], downs[3]))
    rows = spread(row, MLP, members).reshape(tokens, chunk + HD)

    order = jnp.stack(
        [(c + e) % cs * zs + (z + d) % zs for d in range(zs) for e in range(cs)]
    ).astype(jnp.int32)
    gain_up = gain_products(order, ln_gain[None], after(w_up.T, row), chunk)
    both = jnp.stack(both)
    rows, downs, gain_up, both = lax.optimization_barrier((rows, downs, gain_up, both))

    mine, theirs = up_project(rows, ups)
    theirs = pair(theirs)
    terms = []
    for d in range(zs):
        term = mine[d].astype(F32) + theirs[d].astype(F32)
        terms.append(shift(term.astype(BF16), -d, zs) if d else term)
    both = after(both, terms[1])
    both = jnp.stack([shift(both, d, ys, "y") if d else both for d in range(ys)])
    units = w_down.shape[0]
    act = pl.pallas_call(
        lambda *refs: act_kernel(width, units, zs, *refs),
        out_shape=jax.ShapeDtypeStruct((tokens, units), BF16),
        compiler_params=params(),
    )(*terms, gain_up)
    acts = [shift(act, d, zs) if d else act for d in range(zs)]
    down = down_project(acts, [pair(a) for a in acts], downs)
    down = exchange(down.reshape(members, block, chunk), MLP)
    mixed = finish(down, hidden)
    mixed = exchange(mixed.reshape(groups, rows_dev, chunk), REQ)
    mixed = mixed.reshape(zs, cs, rows_dev, chunk).transpose(2, 1, 0, 3).reshape(rows_dev, width)

    valid = (accepted >= 0) & (dest_slot == member)[:, None]
    target = jnp.arange(requests, dtype=jnp.int32)[:, None] * tree_len + jnp.maximum(accepted, 0)
    x, y = lax.axis_index("x"), lax.axis_index("y")
    at = jnp.arange(group_rows, dtype=jnp.int32)
    near = at // rows_dev
    slots = (((x - near % xs) % xs) * ys + (y - near // xs) % ys) * rows_dev + at % rows_dev
    chooser = jnp.any((target[:, :, None] == slots[None, None, :]) & valid[:, :, None], axis=0)
    both = both.reshape(group_rows, 2 * width)
    picked = jnp.dot(chooser.astype(BF16), both, preferred_element_type=F32).astype(BF16)
    return (mixed, picked[:, :width][None], picked[:, width:][None])


def solution(mesh):
    groups, members = mesh.devices.shape
    side = math.isqrt(members)
    fine = Mesh(mesh.devices.reshape(groups // 2, 2, side, side), ALL)
    rows = P(ALL, None)
    pages = P(ALL, None, None)
    in_specs = (
        rows,
        rows,
        rows,
        rows,
        P(REQ, None, None),
        P(REQ),
        P(REQ, None),
        P(REQ),
        P(REQ, None),
        pages,
        pages,
        rows,
        P(None, ALL),
        rows,
        P(),
    )
    return jax.shard_map(
        local, mesh=fine, in_specs=in_specs, out_specs=(rows, pages, pages), check_vma=False
    )
```

```python
import math

import jax
import jax.numpy as jnp
from jax import lax
from jax.experimental import pallas as pl
from jax.experimental.pallas import tpu as pltpu
from jax.sharding import Mesh, PartitionSpec as P

HD = 128
NEG = -(2.0**100)
F32 = jnp.float32
BF16 = jnp.bfloat16
ALL = ("z", "c", "x", "y")
REQ = ("z", "c")
MLP = ("x", "y")
DN = (((1,), (1,)), ((), ()))


def attend_kernel(heads, scaling, q, k, v, dk, dv, mask, out):
    rows = q.shape[0]
    keys = k.shape[0] * k.shape[1]
    kk = jnp.concatenate([k[...].reshape(keys, k.shape[2]), dk[...]], axis=0)
    vv = jnp.concatenate([v[...].reshape(keys, v.shape[2]), dv[...]], axis=0)
    m = mask[...]
    span = [slice(h * HD, (h + 1) * HD) for h in range(heads)]
    scores = [
        jnp.where(
            m > 0,
            lax.dot_general(q[:, cols], kk[:, cols], DN, preferred_element_type=F32) * scaling,
            NEG,
        )
        for cols in span
    ]
    tops = [jnp.max(s, axis=1, keepdims=True).astype(BF16).astype(F32) for s in scores]
    weights = [jnp.exp(s - top) * m for s, top in zip(scores, tops)]
    totals = [jnp.sum(p, axis=1, keepdims=True) for p in weights]
    lane = lax.broadcasted_iota(jnp.int32, (rows, HD), 1)
    stats = jnp.zeros((rows, HD), F32)
    for h, cols in enumerate(span):
        w = jnp.dot(weights[h].astype(BF16), vv[:, cols], preferred_element_type=F32)
        out[:, cols] = w.astype(BF16)
        high = totals[h].astype(BF16).astype(F32)
        stats = jnp.where(lane == h, tops[h], stats)
        stats = jnp.where(lane == 8 + h, high, stats)
        stats = jnp.where(lane == 16 + h, totals[h] - high, stats)
    out[:, heads * HD :] = stats.astype(BF16)


def attend(q, key_cache, value_cache, dk, dv, mask, steps):
    rows, width = q.shape
    pages, page_len, _ = key_cache.shape
    wide = width // steps
    heads = wide // HD
    col = lambda i: (0, i)
    col3 = lambda i: (0, 0, i)

    def body(*refs):
        attend_kernel(heads, 1.0 / math.sqrt(HD), *refs)

    return pl.pallas_call(
        body,
        grid=(steps,),
        in_specs=[
            pl.BlockSpec((rows, wide), col),
            pl.BlockSpec((pages, page_len, wide), col3),
            pl.BlockSpec((pages, page_len, wide), col3),
            pl.BlockSpec((dk.shape[0], wide), col),
            pl.BlockSpec((dv.shape[0], wide), col),
            pl.BlockSpec(mask.shape, lambda i: (0, 0)),
        ],
        out_specs=pl.BlockSpec((rows, wide + HD), col),
        out_shape=jax.ShapeDtypeStruct((rows, steps * (wide + HD)), BF16),
        compiler_params=pltpu.CompilerParams(vmem_limit_bytes=58 * 1024 * 1024),
        cost_estimate=pl.CostEstimate(
            flops=4 * rows * pages * page_len * width,
            bytes_accessed=4 * pages * page_len * width,
            transcendentals=rows * pages * page_len * width // HD,
        ),
    )(q, key_cache, value_cache, dk, dv, mask)


def pair(x):
    return lax.ppermute(x, "c", [(0, 1), (1, 0)])


def shift(x, step, size):
    return lax.ppermute(x, "z", [(i, (i + step) % size) for i in range(size)])


def after(x, first):
    return lax.optimization_barrier((x, first))[0]


def gain_kernel(place, gain, weight, out):
    high = gain[...].astype(BF16).astype(F32)
    row = lax.broadcasted_iota(jnp.int32, (8, gain.shape[1]), 0)
    both = jnp.where(row == 0, high, jnp.where(row == 1, gain[...] - high, 0.0)).astype(BF16)
    got = lax.dot_general(both, weight[...], DN, preferred_element_type=F32)
    out[0] = jnp.broadcast_to(got[0:1] + got[1:2], got.shape)


def hidden_kernel(parts, res, gain, hidden_out, row_out):
    hidden = res[...] + jnp.sum(parts[...].astype(F32), axis=0)
    hidden_out[...] = hidden
    rows, chunk = hidden.shape
    mean = jnp.mean(hidden, axis=1, keepdims=True)
    centered = hidden - mean
    dev = jnp.sum(centered * centered, axis=1, keepdims=True)
    row_out[:, :chunk] = (centered * gain[...]).astype(BF16)
    lane = lax.broadcasted_iota(jnp.int32, (rows, HD), 1)
    stats = jnp.zeros((rows, HD), F32)
    at = 0
    for value in (mean, dev):
        for _ in range(3):
            high = value.astype(BF16).astype(F32)
            stats = jnp.where(lane == at, high, stats)
            value = value - high
            at += 1
    row_out[:, chunk:] = stats.astype(BF16)


def fetch(sources, buffer, sems):
    copies = []
    for d, source in enumerate(sources):
        copies.append(pltpu.make_async_copy(source, buffer.at[d], sems.at[d]))
        copies[-1].start()
    return copies


def up_kernel(n, *refs):
    rows = refs[0]
    outs = refs[n + 1 : n + 3]
    buffer = refs[n + 3]
    copies = fetch(refs[1 : n + 1], buffer, refs[n + 4])
    chunk = buffer.shape[3]
    wide = outs[0].shape[2]
    g = rows[:, :chunk]
    st = rows[:, chunk:].astype(F32)
    lane = lax.broadcasted_iota(jnp.int32, st.shape, 1)
    st = jnp.where(lane < 6, st, 0.0)
    none = jnp.zeros_like(st)
    beside = [jnp.concatenate([none, pltpu.roll(st, by, 1)], axis=1) for by in (102, 96)]
    for d in range(n):
        copies[d].wait()
        for e in range(2):
            w = buffer[d, e]
            w = jnp.concatenate([w, jnp.zeros((wide - w.shape[0], chunk), BF16)], axis=0)
            got = lax.dot_general(g, w, DN, preferred_element_type=F32)
            outs[e][d] = (got + beside[e]).astype(BF16)


def act_kernel(width, units, n, *refs):
    terms = [refs[d][...].astype(F32) for d in range(n)]
    gain = refs[n]
    out = refs[n + 1]
    chunk = width // (2 * n)
    pre = terms[0]
    for d in range(1, n):
        pre = pre + terms[d]
    pre = pre[:, :units]
    means, devs = [], []
    for t in terms:
        for at in (units + 6, units):
            means.append(t[:, at : at + 1] + t[:, at + 1 : at + 2] + t[:, at + 2 : at + 3])
            devs.append(t[:, at + 3 : at + 4] + t[:, at + 4 : at + 5] + t[:, at + 5 : at + 6])
    mean = sum(means[1:], means[0]) / (2 * n)
    var = sum(devs[1:], devs[0])
    for k, value in enumerate(means):
        off = value - mean
        var = var + chunk * off * off
        pre = pre + off * gain[k, 0:1, :]
    out[...] = jnp.maximum(lax.rsqrt(var / width + 1e-05) * pre, 0.0).astype(BF16)


def down_kernel(n, *refs):
    buffer = refs[3 * n + 1]
    copies = fetch(refs[2 * n : 3 * n], buffer, refs[3 * n + 2])
    total = None
    for d in range(n):
        copies[d].wait()
        for e in range(2):
            term = jnp.dot(refs[e * n + d][...], buffer[d, e], preferred_element_type=F32)
            total = term if total is None else total + term
    refs[3 * n][...] = total.astype(BF16)


def finish_kernel(parts, hidden, out, total):
    step = pl.program_id(0)

    @pl.when(step == 0)
    def _():
        total[...] = hidden[...]

    total[...] += jnp.sum(parts[...].astype(F32), axis=0)

    @pl.when(step == pl.num_programs(0) - 1)
    def _():
        out[...] = total[...].astype(BF16)


def params(mib=32):
    return pltpu.CompilerParams(vmem_limit_bytes=mib * 1024 * 1024)


def cut_kernel(n, spots, a, b, *outs):
    for d in range(n):

        @pl.when(pl.program_id(0) == d)
        def _():
            outs[d][0] = a[...]
            outs[d][1] = b[...]


def cut(spots, a, b, n, chunk):
    rows = a.shape[0]
    whole = pl.BlockSpec((2, rows, chunk), lambda i, spots: (0, 0, 0))
    return pl.pallas_call(
        lambda *refs: cut_kernel(n, *refs),
        grid_spec=pltpu.PrefetchScalarGridSpec(
            num_scalar_prefetch=1,
            grid=(n,),
            in_specs=[
                pl.BlockSpec((rows, chunk), lambda i, spots: (0, spots[i])),
                pl.BlockSpec((rows, chunk), lambda i, spots: (0, spots[n + i])),
            ],
            out_specs=[whole] * n,
        ),
        out_shape=[jax.ShapeDtypeStruct((2, rows, chunk), BF16)] * n,
        compiler_params=params(),
    )(spots, a, b)


def gain_products(order, gain, weight, chunk):
    units = weight.shape[0]
    n = order.shape[0]
    return pl.pallas_call(
        gain_kernel,
        grid_spec=pltpu.PrefetchScalarGridSpec(
            num_scalar_prefetch=1,
            grid=(n,),
            in_specs=[
                pl.BlockSpec((1, chunk), lambda i, order: (0, order[i])),
                pl.BlockSpec((units, chunk), lambda i, order: (0, order[i])),
            ],
            out_specs=pl.BlockSpec((1, 8, units), lambda i, order: (i, 0, 0)),
        ),
        out_shape=jax.ShapeDtypeStruct((n, 8, units), F32),
        compiler_params=params(),
    )(order, gain, weight)


def weight_specs(weights):
    n = len(weights)
    return (
        [pl.BlockSpec(memory_space=pltpu.HBM)] * n,
        [pltpu.VMEM((n,) + weights[0].shape, BF16), pltpu.SemaphoreType.DMA((n,))],
    )


def up_project(rows, weights):
    n = len(weights)
    tokens = rows.shape[0]
    specs, scratch = weight_specs(weights)
    return pl.pallas_call(
        lambda *refs: up_kernel(n, *refs),
        in_specs=[pl.BlockSpec(memory_space=pltpu.VMEM)] + specs,
        out_shape=[jax.ShapeDtypeStruct((n, tokens, 256), BF16)] * 2,
        scratch_shapes=scratch,
        compiler_params=params(24),
    )(rows, *weights)


def down_project(own, other, weights):
    n = len(weights)
    specs, scratch = weight_specs(weights)
    return pl.pallas_call(
        lambda *refs: down_kernel(n, *refs),
        in_specs=[pl.BlockSpec(memory_space=pltpu.VMEM)] * (2 * n) + specs,
        out_shape=jax.ShapeDtypeStruct((own[0].shape[0], weights[0].shape[2]), BF16),
        scratch_shapes=scratch,
        compiler_params=params(24),
    )(*own, *other, *weights)


def finish(parts, hidden):
    count, block, chunk = parts.shape
    per = count // 4
    return pl.pallas_call(
        finish_kernel,
        grid=(4,),
        in_specs=[
            pl.BlockSpec((per, block, chunk), lambda i: (i, 0, 0)),
            pl.BlockSpec((block, chunk), lambda i: (0, 0)),
        ],
        out_specs=pl.BlockSpec((block, chunk), lambda i: (0, 0)),
        out_shape=jax.ShapeDtypeStruct((block, chunk), BF16),
        scratch_shapes=[pltpu.VMEM((block, chunk), F32)],
        compiler_params=params(),
    )(parts, hidden)


def spread(x, axes, count):
    return lax.all_to_all(
        jnp.broadcast_to(x[None], (count,) + x.shape), axes, split_axis=0, concat_axis=0
    )


def exchange(x, axes):
    return lax.all_to_all(x, axes, split_axis=0, concat_axis=0)


def local(
    queries,
    keys_new,
    values_new,
    resid,
    tree_mask,
    tree_size,
    accepted,
    dest_slot,
    page_table,
    key_cache,
    value_cache,
    w_out,
    w_up,
    w_down,
    ln_gain,
):
    zs, cs, xs, ys = (lax.axis_size(a) for a in ALL)
    members = xs * ys
    groups = zs * cs
    z = lax.axis_index("z")
    c = lax.axis_index("c")
    member = lax.axis_index(MLP)
    rows_dev, width = queries.shape
    requests, tree_len = tree_mask.shape[:2]
    group_rows = requests * tree_len
    pages_dev, page_len, _ = key_cache.shape
    tokens = group_rows * groups
    heads = width // HD
    half = width // cs
    chunk = half // zs
    block = tokens // members

    wide_q = jnp.broadcast_to(queries[None], (members,) + queries.shape)
    group_q = exchange(wide_q, MLP).reshape(group_rows, width)

    turn = (z + jnp.arange(zs, dtype=jnp.int32)) % zs
    own_turn, other_turn = c * zs + turn, (1 - c) * zs + turn

    def send(pieces):
        return [shift(p, d, zs) if d else p for d, p in enumerate(pieces)]

    k_dev = w_out.shape[0]

    def swap(w):
        return pair(lax.dynamic_slice_in_dim(w, (1 - c) * half, half, 1))

    def reshard(w, other):
        return cut(jnp.concatenate([own_turn, turn]), w, other, zs, chunk)

    def swap(w):
        return pair(lax.dynamic_slice_in_dim(w, (1 - c) * half, half, 1))

    up_w = after(w_up.T, wide_q)
    ups = send(reshard(up_w, swap(up_w)))

    res = after(resid, wide_q)
    res = jnp.stack(
        [
            lax.dynamic_slice_in_dim(res, c * half, half, 1),
            pair(lax.dynamic_slice_in_dim(res, (1 - c) * half, half, 1)),
        ]
    ).reshape(cs * rows_dev, half)
    res_parts = []
    for d in range(zs):
        part = lax.dynamic_slice_in_dim(res, ((z + d) % zs) * chunk, chunk, 1)
        res_parts.append(shift(part, d, zs) if d else part)
    res = jnp.concatenate(res_parts, axis=0)
    at = jnp.arange(block, dtype=jnp.int32)
    source = ((z - at // (cs * rows_dev)) % zs) * cs + (c + at // rows_dev) % cs
    order = at[:, None] == (source * rows_dev + at % rows_dev)[None, :]
    res = jnp.dot(order.astype(BF16), res, preferred_element_type=F32)

    page_ids = member * pages_dev + jnp.arange(pages_dev, dtype=jnp.int32)
    owners = jnp.any(page_table[:, :, None] == page_ids[None, None, :], axis=1)
    pool_mask = jnp.repeat(jnp.repeat(owners, page_len, axis=1), tree_len, axis=0).astype(F32)
    draft_pad = 16
    slot_ids = member * rows_dev + jnp.arange(draft_pad, dtype=jnp.int32)
    row_ids = jnp.arange(group_rows, dtype=jnp.int32)
    tree_cols = jnp.tile(tree_mask.reshape(group_rows, tree_len), (1, requests))
    live = jnp.repeat(tree_size, tree_len) > (row_ids % tree_len)
    tree_ok = (
        (tree_cols == 1)
        & live[None, :]
        & ((row_ids // tree_len)[:, None] == (row_ids // tree_len)[None, :])
    ).astype(F32)
    pick = (row_ids[:, None] == slot_ids[None, :]) & (
        jnp.arange(draft_pad, dtype=jnp.int32) < rows_dev
    )[None, :]
    draft_mask = jnp.dot(tree_ok, pick.astype(F32))
    pad = ((0, draft_pad - rows_dev), (0, 0))
    parts = attend(
        group_q,
        key_cache,
        value_cache,
        jnp.pad(keys_new, pad),
        jnp.pad(values_new, pad),
        jnp.concatenate([pool_mask, draft_mask], axis=1),
        heads // 7,
    )

    parts, ups[1], ups[3], res = lax.optimization_barrier((parts, ups[1], ups[3], res))

    wo = after(w_out, parts)
    wo_parts = send(cut(jnp.concatenate([own_turn, other_turn]), wo, wo, zs, chunk))
    wo_parts = jnp.concatenate(wo_parts, axis=1)
    down_other = swap(after(w_down, parts))

    parts = exchange(parts.reshape(members, rows_dev, parts.shape[1]), MLP)
    parts = parts.reshape(members, rows_dev, heads // 7, 8, HD).astype(F32)
    st = parts[:, :, :, 7]
    tops, highs, lows = st[..., 0:7], st[..., 8:15], st[..., 16:23]
    scale = jnp.exp(tops - jnp.max(tops, axis=0, keepdims=True))
    total = jnp.sum(scale * (highs + lows), axis=0)
    weighted = jnp.sum(scale[..., None] * parts[:, :, :, :7], axis=0)
    attended = (weighted / total[..., None]).astype(BF16).reshape(rows_dev, width)

    feats = attended.reshape(rows_dev, zs, cs, members, k_dev).transpose(1, 2, 3, 0, 4)
    feats = jnp.stack(
        [
            jnp.concatenate([feats[(to - d) % zs] for d in range(zs)], axis=3)
            for to in range(zs)
        ]
    ).reshape(groups * members, rows_dev, zs * k_dev)
    feats, ups[2], down_other, wo_parts = lax.optimization_barrier(
        (feats, ups[2], down_other, wo_parts)
    )
    downs = reshard(*after((w_down, down_other), feats))
    feats, downs = lax.optimization_barrier((exchange(feats, ALL), downs))
    downs = send(downs)
    feats = (
        feats.reshape(groups, members, rows_dev, zs * k_dev)
        .transpose(1, 0, 2, 3)
        .reshape(tokens, zs * k_dev)
    )
    wo_own, wo_pair = wo_parts[0], wo_parts[1]
    sent = pair(jnp.dot(feats, wo_pair, preferred_element_type=F32).astype(BF16))
    part = jnp.dot(feats, wo_own, preferred_element_type=F32) + sent.astype(F32)
    part = part.astype(BF16).reshape(members, block, chunk)
    part = exchange(part, MLP)
    gain = lax.dynamic_slice_in_dim(ln_gain, c * half + z * chunk, chunk, 0)

    hidden, row = pl.pallas_call(
        hidden_kernel,
        out_shape=(
            jax.ShapeDtypeStruct((block, chunk), F32),
            jax.ShapeDtypeStruct((block, chunk + HD), BF16),
        ),
        compiler_params=params(),
    )(part, res, gain[None])
    rows = spread(row, MLP, members).reshape(tokens, chunk + HD)

    order = jnp.stack(
        [(c + e) % cs * zs + (z + d) % zs for d in range(zs) for e in range(cs)]
    ).astype(jnp.int32)
    gain_up = gain_products(order, ln_gain[None], after(w_up.T, row), chunk)
    draft_k, draft_v = after((keys_new, values_new), row)
    both = jnp.broadcast_to(
        jnp.concatenate([draft_k, draft_v], axis=1)[None], (members, rows_dev, 2 * width)
    )
    rows, gain_up, both, downs = lax.optimization_barrier((rows, gain_up, both, downs))

    both = exchange(after(both, rows), MLP)

    mine, theirs = up_project(rows, ups)
    theirs = pair(theirs)
    terms = []
    for d in range(zs):
        term = mine[d].astype(F32) + theirs[d].astype(F32)
        terms.append(shift(term.astype(BF16), -d, zs) if d else term)
    units = w_down.shape[0]
    act = pl.pallas_call(
        lambda *refs: act_kernel(width, units, zs, *refs),
        out_shape=jax.ShapeDtypeStruct((tokens, units), BF16),
        compiler_params=params(),
    )(*terms, gain_up)
    acts = [shift(act, d, zs) if d else act for d in range(zs)]
    down = down_project(acts, [pair(a) for a in acts], downs)
    down, both = lax.optimization_barrier((down, both))
    down = exchange(down.reshape(members, block, chunk), MLP)
    mixed = finish(down, hidden)
    mixed = exchange(mixed.reshape(groups, rows_dev, chunk), REQ)
    mixed = mixed.reshape(zs, cs, rows_dev, chunk).transpose(2, 1, 0, 3).reshape(rows_dev, width)

    valid = (accepted >= 0) & (dest_slot == member)[:, None]
    target = jnp.arange(requests, dtype=jnp.int32)[:, None] * tree_len + jnp.maximum(accepted, 0)
    chooser = jnp.any((target[:, :, None] == row_ids[None, None, :]) & valid[:, :, None], axis=0)
    both = both.reshape(group_rows, 2 * width)
    picked = jnp.dot(chooser.astype(BF16), both, preferred_element_type=F32).astype(BF16)
    return (mixed, picked[:, :width][None], picked[:, width:][None])


def solution(mesh):
    groups, members = mesh.devices.shape
    side = math.isqrt(members)
    fine = Mesh(mesh.devices.reshape(groups // 2, 2, side, side), ALL)
    rows = P(ALL, None)
    pages = P(ALL, None, None)
    in_specs = (
        rows,
        rows,
        rows,
        rows,
        P(REQ, None, None),
        P(REQ),
        P(REQ, None),
        P(REQ),
        P(REQ, None),
        pages,
        pages,
        rows,
        P(None, ALL),
        rows,
        P(),
    )
    return jax.shard_map(
        local, mesh=fine, in_specs=in_specs, out_specs=(rows, pages, pages), check_vma=False
    )
```

```python
import math

import jax
import jax.numpy as jnp
from jax import lax
from jax.experimental import pallas as pl
from jax.experimental.pallas import tpu as pltpu
from jax.sharding import Mesh, PartitionSpec as P

HD = 128
NEG = -(2.0**100)
F32 = jnp.float32
BF16 = jnp.bfloat16
ALL = ("z", "c", "x", "y")
REQ = ("z", "c")
MLP = ("x", "y")
CHIPS = ("z", "x", "y")
DN = (((1,), (1,)), ((), ()))


def attend_kernel(heads, scaling, q, k, v, dk, dv, mask, out):
    rows = q.shape[0]
    keys = k.shape[0] * k.shape[1]
    kk = jnp.concatenate([k[...].reshape(keys, k.shape[2]), dk[...]], axis=0)
    vv = jnp.concatenate([v[...].reshape(keys, v.shape[2]), dv[...]], axis=0)
    m = mask[...]
    span = [slice(h * HD, (h + 1) * HD) for h in range(heads)]
    scores = [
        jnp.where(
            m > 0,
            lax.dot_general(q[:, cols], kk[:, cols], DN, preferred_element_type=F32) * scaling,
            NEG,
        )
        for cols in span
    ]
    tops = [jnp.max(s, axis=1, keepdims=True).astype(BF16).astype(F32) for s in scores]
    weights = [jnp.exp(s - top) * m for s, top in zip(scores, tops)]
    totals = [jnp.sum(p, axis=1, keepdims=True) for p in weights]
    lane = lax.broadcasted_iota(jnp.int32, (rows, HD), 1)
    stats = jnp.zeros((rows, HD), F32)
    for h, cols in enumerate(span):
        w = jnp.dot(weights[h].astype(BF16), vv[:, cols], preferred_element_type=F32)
        out[:, cols] = w.astype(BF16)
        high = totals[h].astype(BF16).astype(F32)
        stats = jnp.where(lane == h, tops[h], stats)
        stats = jnp.where(lane == 8 + h, high, stats)
        stats = jnp.where(lane == 16 + h, totals[h] - high, stats)
    out[:, heads * HD :] = stats.astype(BF16)


def attend(q, key_cache, value_cache, dk, dv, mask, steps):
    rows, width = q.shape
    pages, page_len, _ = key_cache.shape
    wide = width // steps
    heads = wide // HD
    col = lambda i: (0, i)
    col3 = lambda i: (0, 0, i)

    def body(*refs):
        attend_kernel(heads, 1.0 / math.sqrt(HD), *refs)

    return pl.pallas_call(
        body,
        grid=(steps,),
        in_specs=[
            pl.BlockSpec((rows, wide), col),
            pl.BlockSpec((pages, page_len, wide), col3),
            pl.BlockSpec((pages, page_len, wide), col3),
            pl.BlockSpec((dk.shape[0], wide), col),
            pl.BlockSpec((dv.shape[0], wide), col),
            pl.BlockSpec(mask.shape, lambda i: (0, 0)),
        ],
        out_specs=pl.BlockSpec((rows, wide + HD), col),
        out_shape=jax.ShapeDtypeStruct((rows, steps * (wide + HD)), BF16),
        compiler_params=pltpu.CompilerParams(vmem_limit_bytes=58 * 1024 * 1024),
        cost_estimate=pl.CostEstimate(
            flops=4 * rows * pages * page_len * width,
            bytes_accessed=4 * pages * page_len * width,
            transcendentals=rows * pages * page_len * width // HD,
        ),
    )(q, key_cache, value_cache, dk, dv, mask)


def pair(x):
    return lax.ppermute(x, "c", [(0, 1), (1, 0)])


def shift(x, step, size, axis="z"):
    return lax.ppermute(x, axis, [(i, (i + step) % size) for i in range(size)])


def after(x, first):
    return lax.optimization_barrier((x, first))[0]


def gain_kernel(gain, own, other, out):
    high = gain[...].astype(BF16).astype(F32)
    row = lax.broadcasted_iota(jnp.int32, (8, gain.shape[1]), 0)
    low = gain[...] - high
    both = jnp.where(row == 0, high, jnp.where(row == 1, low, 0.0)).astype(BF16)
    for e, w in enumerate((own, other)):
        out[e] = lax.dot_general(both, w[...], DN, preferred_element_type=F32)


def hidden_kernel(parts, res, gain, hidden_out, row_out):
    hidden = res[...] + jnp.sum(parts[...].astype(F32), axis=0)
    hidden_out[...] = hidden
    rows, chunk = hidden.shape
    mean = jnp.mean(hidden, axis=1, keepdims=True)
    centered = hidden - mean
    dev = jnp.sum(centered * centered, axis=1, keepdims=True)
    row_out[:, :chunk] = (centered * gain[...]).astype(BF16)
    lane = lax.broadcasted_iota(jnp.int32, (rows, HD), 1)
    stats = jnp.zeros((rows, HD), F32)
    at = 0
    for value in (mean, dev):
        for _ in range(3):
            high = value.astype(BF16).astype(F32)
            stats = jnp.where(lane == at, high, stats)
            value = value - high
            at += 1
    row_out[:, chunk:] = stats.astype(BF16)


def up_kernel(place, rows, own, other, gain_own, gain_other, mine, theirs, stats_out):
    step = pl.program_id(0)
    chunk = own.shape[1]
    g = rows[0, :, :chunk]
    st = rows[0, :, chunk:].astype(F32)
    mean = st[:, 0:1] + st[:, 1:2] + st[:, 2:3]
    dev = st[:, 3:4] + st[:, 4:5] + st[:, 5:6]
    lane = lax.broadcasted_iota(jnp.int32, st.shape, 1)
    stats = jnp.where(lane == step, mean, 0.0) + jnp.where(lane == 8, dev, 0.0)

    @pl.when(step == 0)
    def _():
        mine[...] = jnp.zeros_like(mine)
        theirs[...] = jnp.zeros_like(theirs)
        stats_out[...] = jnp.zeros_like(stats_out)

    stats_out[...] += stats
    for w, gw, out in ((own, gain_own, mine), (other, gain_other, theirs)):
        term = lax.dot_general(g, w[...], DN, preferred_element_type=F32)
        out[...] += term + mean * (gw[0, 0:1, :] + gw[0, 1:2, :])


def act_kernel(width, mine, theirs, stats, stats_pair, gain_own, gain_pair, out):
    n = gain_own.shape[0]
    a = stats[...]
    b = stats_pair[...]
    lane = lax.broadcasted_iota(jnp.int32, a.shape, 1)
    chunk = width // (2 * n)
    mean = (
        jnp.sum(jnp.where(lane < n, a, 0.0), axis=1, keepdims=True)
        + jnp.sum(jnp.where(lane < n, b, 0.0), axis=1, keepdims=True)
    ) / (2 * n)

    def spread_of(v):
        part = jnp.where(lane < n, chunk * jnp.square(v - mean), jnp.where(lane == 8, v, 0.0))
        return jnp.sum(part, axis=1, keepdims=True)

    inv = lax.rsqrt((spread_of(a) + spread_of(b)) / width + 1e-05)
    gw = jnp.zeros((1, out.shape[1]), F32)
    for k in range(n):
        for ref in (gain_own, gain_pair):
            gw = gw + ref[k, 0:1, :] + ref[k, 1:2, :]
    pre = inv * (mine[...] + theirs[...] - mean * gw)
    out[...] = jnp.maximum(pre, 0.0).astype(BF16)


def down_kernel(place, act, act_pair, own, other, out):
    out[0] = (
        jnp.dot(act[...], own[...], preferred_element_type=F32)
        + jnp.dot(act_pair[...], other[...], preferred_element_type=F32)
    ).astype(BF16)


def finish_kernel(parts, hidden, out, total):
    step = pl.program_id(0)

    @pl.when(step == 0)
    def _():
        total[...] = hidden[...]

    total[...] += jnp.sum(parts[...].astype(F32), axis=0)

    @pl.when(step == pl.num_programs(0) - 1)
    def _():
        out[...] = total[...].astype(BF16)


def params():
    return pltpu.CompilerParams(vmem_limit_bytes=32 * 1024 * 1024)


def own_spec(units, chunk, n):
    return pl.BlockSpec((units, chunk), lambda i, place: (0, place[0] * n + i))


def other_spec(units, chunk):
    return pl.BlockSpec((units, chunk), lambda i, place: (0, i))


def gain_products(place, gain, own, other, n, chunk):
    units = own.shape[0]

    def body(place, gain, own, other, out):
        gain_kernel(gain, own, other, out.at[0])

    return pl.pallas_call(
        body,
        grid_spec=pltpu.PrefetchScalarGridSpec(
            num_scalar_prefetch=1,
            grid=(n,),
            in_specs=[
                pl.BlockSpec((1, chunk), lambda i, place: (0, place[0] * n + i)),
                own_spec(units, chunk, n),
                other_spec(units, chunk),
            ],
            out_specs=pl.BlockSpec((1, 2, 8, units), lambda i, place: (i, 0, 0, 0)),
        ),
        out_shape=jax.ShapeDtypeStruct((n, 2, 8, units), F32),
        compiler_params=params(),
    )(place, gain, own, other)


def up_project(place, rows, own, other, gain_own, gain_other):
    n, tokens, wide = rows.shape
    units = own.shape[0]
    chunk = wide - HD
    fixed = lambda i, place: (0, 0)
    turn = lambda i, place: (i, 0, 0)
    return pl.pallas_call(
        up_kernel,
        grid_spec=pltpu.PrefetchScalarGridSpec(
            num_scalar_prefetch=1,
            grid=(n,),
            in_specs=[
                pl.BlockSpec((1, tokens, wide), turn),
                own_spec(units, chunk, n),
                other_spec(units, chunk),
                pl.BlockSpec((1, 8, units), turn),
                pl.BlockSpec((1, 8, units), turn),
            ],
            out_specs=[
                pl.BlockSpec((tokens, units), fixed),
                pl.BlockSpec((tokens, units), fixed),
                pl.BlockSpec((tokens, HD), fixed),
            ],
        ),
        out_shape=(
            jax.ShapeDtypeStruct((tokens, units), F32),
            jax.ShapeDtypeStruct((tokens, units), F32),
            jax.ShapeDtypeStruct((tokens, HD), F32),
        ),
        compiler_params=params(),
    )(place, rows, own, other, gain_own, gain_other)


def down_project(place, act, act_pair, own, other, n, chunk):
    tokens, units = act.shape
    fixed = lambda i, place: (0, 0)
    return pl.pallas_call(
        down_kernel,
        grid_spec=pltpu.PrefetchScalarGridSpec(
            num_scalar_prefetch=1,
            grid=(n,),
            in_specs=[
                pl.BlockSpec((tokens, units), fixed),
                pl.BlockSpec((tokens, units), fixed),
                own_spec(units, chunk, n),
                other_spec(units, chunk),
            ],
            out_specs=pl.BlockSpec((1, tokens, chunk), lambda i, place: (i, 0, 0)),
        ),
        out_shape=jax.ShapeDtypeStruct((n, tokens, chunk), BF16),
        compiler_params=params(),
    )(place, act, act_pair, own, other)


def finish(parts, hidden):
    count, block, chunk = parts.shape
    per = count // 4
    return pl.pallas_call(
        finish_kernel,
        grid=(4,),
        in_specs=[
            pl.BlockSpec((per, block, chunk), lambda i: (i, 0, 0)),
            pl.BlockSpec((block, chunk), lambda i: (0, 0)),
        ],
        out_specs=pl.BlockSpec((block, chunk), lambda i: (0, 0)),
        out_shape=jax.ShapeDtypeStruct((block, chunk), BF16),
        scratch_shapes=[pltpu.VMEM((block, chunk), F32)],
        compiler_params=params(),
    )(parts, hidden)


def spread(x, axes, count):
    return lax.all_to_all(
        jnp.broadcast_to(x[None], (count,) + x.shape), axes, split_axis=0, concat_axis=0
    )


def exchange(x, axes):
    return lax.all_to_all(x, axes, split_axis=0, concat_axis=0)


def local(
    queries,
    keys_new,
    values_new,
    resid,
    tree_mask,
    tree_size,
    accepted,
    dest_slot,
    page_table,
    key_cache,
    value_cache,
    w_out,
    w_up,
    w_down,
    ln_gain,
):
    zs, cs, xs, ys = (lax.axis_size(a) for a in ALL)
    members = xs * ys
    groups = zs * cs
    z = lax.axis_index("z")
    c = lax.axis_index("c")
    member = lax.axis_index(MLP)
    rows_dev, width = queries.shape
    requests, tree_len = tree_mask.shape[:2]
    group_rows = requests * tree_len
    pages_dev, page_len, _ = key_cache.shape
    tokens = group_rows * groups
    heads = width // HD
    half = width // cs
    chunk = half // zs
    block = tokens // members

    wide_q = jnp.broadcast_to(queries[None], (members,) + queries.shape)
    group_q = exchange(wide_q, MLP).reshape(group_rows, width)

    def piece(w, core, d):
        return lax.dynamic_slice_in_dim(w, core * half + ((z + d) % zs) * chunk, chunk, 1)

    k_dev = w_out.shape[0]
    wo = after(w_out, group_q)
    wo_parts = []
    for d in range(zs):
        part = jnp.stack([piece(wo, c, d), piece(wo, 1 - c, d)])
        wo_parts.append(shift(part, d, zs) if d else part)
    wo_parts = jnp.concatenate(wo_parts, axis=1)

    both = after(jnp.concatenate([keys_new, values_new], axis=1), wide_q)
    both = jnp.stack([shift(both, d, xs, "x") if d else both for d in range(xs)])

    page_ids = member * pages_dev + jnp.arange(pages_dev, dtype=jnp.int32)
    owners = jnp.any(page_table[:, :, None] == page_ids[None, None, :], axis=1)
    pool_mask = jnp.repeat(jnp.repeat(owners, page_len, axis=1), tree_len, axis=0).astype(F32)
    draft_pad = 16
    slot_ids = member * rows_dev + jnp.arange(draft_pad, dtype=jnp.int32)
    row_ids = jnp.arange(group_rows, dtype=jnp.int32)
    tree_cols = jnp.tile(tree_mask.reshape(group_rows, tree_len), (1, requests))
    live = jnp.repeat(tree_size, tree_len) > (row_ids % tree_len)
    tree_ok = (
        (tree_cols == 1)
        & live[None, :]
        & ((row_ids // tree_len)[:, None] == (row_ids // tree_len)[None, :])
    ).astype(F32)
    pick = (row_ids[:, None] == slot_ids[None, :]) & (
        jnp.arange(draft_pad, dtype=jnp.int32) < rows_dev
    )[None, :]
    draft_mask = jnp.dot(tree_ok, pick.astype(F32))
    pad = ((0, draft_pad - rows_dev), (0, 0))
    parts = attend(
        group_q,
        key_cache,
        value_cache,
        jnp.pad(keys_new, pad),
        jnp.pad(values_new, pad),
        jnp.concatenate([pool_mask, draft_mask], axis=1),
        heads // 7,
    )

    parts, both = lax.optimization_barrier((parts, both))

    res = after(resid, parts)
    res = jnp.stack(
        [
            lax.dynamic_slice_in_dim(res, c * half, half, 1),
            pair(lax.dynamic_slice_in_dim(res, (1 - c) * half, half, 1)),
        ]
    ).reshape(cs * rows_dev, half)
    res_parts = []
    for d in range(zs):
        part = lax.dynamic_slice_in_dim(res, ((z + d) % zs) * chunk, chunk, 1)
        res_parts.append(shift(part, d, zs) if d else part)
    res = jnp.concatenate(res_parts, axis=0)
    at = jnp.arange(block, dtype=jnp.int32)
    source = ((z - at // (cs * rows_dev)) % zs) * cs + (c + at // rows_dev) % cs
    order = at[:, None] == (source * rows_dev + at % rows_dev)[None, :]
    res = jnp.dot(order.astype(BF16), res, preferred_element_type=F32)

    parts = exchange(parts.reshape(members, rows_dev, parts.shape[1]), MLP)
    parts = parts.reshape(members, rows_dev, heads // 7, 8, HD).astype(F32)
    st = parts[:, :, :, 7]
    tops, highs, lows = st[..., 0:7], st[..., 8:15], st[..., 16:23]
    scale = jnp.exp(tops - jnp.max(tops, axis=0, keepdims=True))
    total = jnp.sum(scale * (highs + lows), axis=0)
    weighted = jnp.sum(scale[..., None] * parts[:, :, :, :7], axis=0)
    attended = (weighted / total[..., None]).astype(BF16).reshape(rows_dev, width)

    feats = attended.reshape(rows_dev, zs, cs, members, k_dev).transpose(1, 2, 3, 0, 4)
    feats = jnp.stack(
        [
            jnp.concatenate([feats[(to - d) % zs] for d in range(zs)], axis=3)
            for to in range(zs)
        ]
    ).reshape(groups * members, rows_dev, zs * k_dev)
    feats = exchange(feats, ALL)
    feats = (
        feats.reshape(groups, members, rows_dev, zs * k_dev)
        .transpose(1, 0, 2, 3)
        .reshape(tokens, zs * k_dev)
    )
    wo_own, wo_pair = wo_parts[0], wo_parts[1]
    sent = pair(jnp.dot(feats, wo_pair, preferred_element_type=F32).astype(BF16))
    part = jnp.dot(feats, wo_own, preferred_element_type=F32) + sent.astype(F32)
    part = exchange(part.astype(BF16).reshape(members, block, chunk), MLP)
    gain = lax.dynamic_slice_in_dim(ln_gain, c * half + z * chunk, chunk, 0)

    hidden, row = pl.pallas_call(
        hidden_kernel,
        out_shape=(
            jax.ShapeDtypeStruct((block, chunk), F32),
            jax.ShapeDtypeStruct((block, chunk + HD), BF16),
        ),
        compiler_params=params(),
    )(part, res, gain[None])

    place = c.reshape(1).astype(jnp.int32)
    up_w = w_up.T
    up_other = pair(lax.dynamic_slice_in_dim(after(up_w, row), (1 - c) * half, half, 1))
    down_other = pair(lax.dynamic_slice_in_dim(after(w_down, row), (1 - c) * half, half, 1))
    gw = gain_products(place, ln_gain[None], up_w, up_other, zs, chunk)
    gain_own = gw[:, 0]
    gain_other = gw[:, 1]
    gain_pair = pair(gain_other)

    both = after(both, row)
    both = jnp.stack([shift(both, d, ys, "y") if d else both for d in range(ys)])
    rows = spread(row, CHIPS, zs * members).reshape(zs, tokens, chunk + HD)
    rows, both = lax.optimization_barrier((rows, both))
    mine, theirs, stats = up_project(place, rows, up_w, up_other, gain_own, gain_other)
    act = pl.pallas_call(
        lambda *refs: act_kernel(width, *refs),
        out_shape=jax.ShapeDtypeStruct(mine.shape, BF16),
        compiler_params=params(),
    )(mine, pair(theirs), stats, pair(stats), gain_own, gain_pair)
    down = down_project(place, act, pair(act), w_down, down_other, zs, chunk)
    down = exchange(down.reshape(zs * members, block, chunk), CHIPS)
    mixed = finish(down, hidden)
    mixed = exchange(mixed.reshape(groups, rows_dev, chunk), REQ)
    mixed = mixed.reshape(zs, cs, rows_dev, chunk).transpose(2, 1, 0, 3).reshape(rows_dev, width)

    valid = (accepted >= 0) & (dest_slot == member)[:, None]
    target = jnp.arange(requests, dtype=jnp.int32)[:, None] * tree_len + jnp.maximum(accepted, 0)
    x, y = lax.axis_index("x"), lax.axis_index("y")
    at = jnp.arange(group_rows, dtype=jnp.int32)
    near = at // rows_dev
    slots = (((x - near % xs) % xs) * ys + (y - near // xs) % ys) * rows_dev + at % rows_dev
    chooser = jnp.any((target[:, :, None] == slots[None, None, :]) & valid[:, :, None], axis=0)
    both = both.reshape(group_rows, 2 * width)
    picked = jnp.dot(chooser.astype(BF16), both, preferred_element_type=F32).astype(BF16)
    return (mixed, picked[:, :width][None], picked[:, width:][None])


def solution(mesh):
    groups, members = mesh.devices.shape
    side = math.isqrt(members)
    fine = Mesh(mesh.devices.reshape(groups // 2, 2, side, side), ALL)
    rows = P(ALL, None)
    pages = P(ALL, None, None)
    in_specs = (
        rows,
        rows,
        rows,
        rows,
        P(REQ, None, None),
        P(REQ),
        P(REQ, None),
        P(REQ),
        P(REQ, None),
        pages,
        pages,
        rows,
        P(None, ALL),
        rows,
        P(),
    )
    return jax.shard_map(
        local, mesh=fine, in_specs=in_specs, out_specs=(rows, pages, pages), check_vma=False
    )
```

```python
import math

import jax
import jax.numpy as jnp
from jax import lax
from jax.experimental import pallas as pl
from jax.experimental.pallas import tpu as pltpu
from jax.sharding import Mesh, PartitionSpec as P

HD = 128
NEG = -(2.0**100)
F32 = jnp.float32
BF16 = jnp.bfloat16
ALL = ("z", "c", "x", "y")
REQ = ("z", "c")
MLP = ("x", "y")
CHIPS = ("z", "x", "y")
DN = (((1,), (1,)), ((), ()))


def attend_kernel(heads, scaling, q, k, v, dk, dv, mask, out):
    rows = q.shape[0]
    keys = k.shape[0] * k.shape[1]
    kk = jnp.concatenate([k[...].reshape(keys, k.shape[2]), dk[...]], axis=0)
    vv = jnp.concatenate([v[...].reshape(keys, v.shape[2]), dv[...]], axis=0)
    m = mask[...]
    span = [slice(h * HD, (h + 1) * HD) for h in range(heads)]
    scores = [
        jnp.where(
            m > 0,
            lax.dot_general(q[:, cols], kk[:, cols], DN, preferred_element_type=F32) * scaling,
            NEG,
        )
        for cols in span
    ]
    tops = [jnp.max(s, axis=1, keepdims=True).astype(BF16).astype(F32) for s in scores]
    weights = [jnp.exp(s - top) * m for s, top in zip(scores, tops)]
    totals = [jnp.sum(p, axis=1, keepdims=True) for p in weights]
    lane = lax.broadcasted_iota(jnp.int32, (rows, HD), 1)
    stats = jnp.zeros((rows, HD), F32)
    for h, cols in enumerate(span):
        w = jnp.dot(weights[h].astype(BF16), vv[:, cols], preferred_element_type=F32)
        out[:, cols] = w.astype(BF16)
        high = totals[h].astype(BF16).astype(F32)
        stats = jnp.where(lane == h, tops[h], stats)
        stats = jnp.where(lane == 8 + h, high, stats)
        stats = jnp.where(lane == 16 + h, totals[h] - high, stats)
    out[:, heads * HD :] = stats.astype(BF16)


def attend(q, key_cache, value_cache, dk, dv, mask, steps):
    rows, width = q.shape
    pages, page_len, _ = key_cache.shape
    wide = width // steps
    heads = wide // HD
    col = lambda i: (0, i)
    col3 = lambda i: (0, 0, i)

    def body(*refs):
        attend_kernel(heads, 1.0 / math.sqrt(HD), *refs)

    return pl.pallas_call(
        body,
        grid=(steps,),
        in_specs=[
            pl.BlockSpec((rows, wide), col),
            pl.BlockSpec((pages, page_len, wide), col3),
            pl.BlockSpec((pages, page_len, wide), col3),
            pl.BlockSpec((dk.shape[0], wide), col),
            pl.BlockSpec((dv.shape[0], wide), col),
            pl.BlockSpec(mask.shape, lambda i: (0, 0)),
        ],
        out_specs=pl.BlockSpec((rows, wide + HD), col),
        out_shape=jax.ShapeDtypeStruct((rows, steps * (wide + HD)), BF16),
        compiler_params=pltpu.CompilerParams(vmem_limit_bytes=58 * 1024 * 1024),
        cost_estimate=pl.CostEstimate(
            flops=4 * rows * pages * page_len * width,
            bytes_accessed=4 * pages * page_len * width,
            transcendentals=rows * pages * page_len * width // HD,
        ),
    )(q, key_cache, value_cache, dk, dv, mask)


def pair(x):
    return lax.ppermute(x, "c", [(0, 1), (1, 0)])


def shift(x, step, size, axis="z"):
    return lax.ppermute(x, axis, [(i, (i + step) % size) for i in range(size)])


def after(x, first):
    return lax.optimization_barrier((x, first))[0]


def gain_kernel(gain, own, other, out):
    high = gain[...].astype(BF16).astype(F32)
    row = lax.broadcasted_iota(jnp.int32, (8, gain.shape[1]), 0)
    low = gain[...] - high
    both = jnp.where(row == 0, high, jnp.where(row == 1, low, 0.0)).astype(BF16)
    for e, w in enumerate((own, other)):
        out[e] = lax.dot_general(both, w[...], DN, preferred_element_type=F32)


def hidden_kernel(parts, res, gain, hidden_out, row_out):
    hidden = res[...] + jnp.sum(parts[...].astype(F32), axis=0)
    hidden_out[...] = hidden
    rows, chunk = hidden.shape
    mean = jnp.mean(hidden, axis=1, keepdims=True)
    centered = hidden - mean
    dev = jnp.sum(centered * centered, axis=1, keepdims=True)
    row_out[:, :chunk] = (centered * gain[...]).astype(BF16)
    lane = lax.broadcasted_iota(jnp.int32, (rows, HD), 1)
    stats = jnp.zeros((rows, HD), F32)
    at = 0
    for value in (mean, dev):
        for _ in range(3):
            high = value.astype(BF16).astype(F32)
            stats = jnp.where(lane == at, high, stats)
            value = value - high
            at += 1
    row_out[:, chunk:] = stats.astype(BF16)


def up_kernel(place, rows, own, other, gain_own, gain_other, mine, theirs, stats_out):
    step = pl.program_id(0)
    chunk = own.shape[1]
    g = rows[0, :, :chunk]
    st = rows[0, :, chunk:].astype(F32)
    mean = st[:, 0:1] + st[:, 1:2] + st[:, 2:3]
    dev = st[:, 3:4] + st[:, 4:5] + st[:, 5:6]
    lane = lax.broadcasted_iota(jnp.int32, st.shape, 1)
    stats = jnp.where(lane == step, mean, 0.0) + jnp.where(lane == 8, dev, 0.0)

    @pl.when(step == 0)
    def _():
        mine[...] = jnp.zeros_like(mine)
        theirs[...] = jnp.zeros_like(theirs)
        stats_out[...] = jnp.zeros_like(stats_out)

    stats_out[...] += stats
    for w, gw, out in ((own, gain_own, mine), (other, gain_other, theirs)):
        term = lax.dot_general(g, w[...], DN, preferred_element_type=F32)
        out[...] += term + mean * (gw[0, 0:1, :] + gw[0, 1:2, :])


def act_kernel(width, mine, theirs, stats, stats_pair, gain_own, gain_pair, out):
    n = gain_own.shape[0]
    a = stats[...]
    b = stats_pair[...]
    lane = lax.broadcasted_iota(jnp.int32, a.shape, 1)
    chunk = width // (2 * n)
    mean = (
        jnp.sum(jnp.where(lane < n, a, 0.0), axis=1, keepdims=True)
        + jnp.sum(jnp.where(lane < n, b, 0.0), axis=1, keepdims=True)
    ) / (2 * n)

    def spread_of(v):
        part = jnp.where(lane < n, chunk * jnp.square(v - mean), jnp.where(lane == 8, v, 0.0))
        return jnp.sum(part, axis=1, keepdims=True)

    inv = lax.rsqrt((spread_of(a) + spread_of(b)) / width + 1e-05)
    gw = jnp.zeros((1, out.shape[1]), F32)
    for k in range(n):
        for ref in (gain_own, gain_pair):
            gw = gw + ref[k, 0:1, :] + ref[k, 1:2, :]
    pre = inv * (mine[...] + theirs[...] - mean * gw)
    out[...] = jnp.maximum(pre, 0.0).astype(BF16)


def down_kernel(place, act, act_pair, own, other, out):
    out[0] = (
        jnp.dot(act[...], own[...], preferred_element_type=F32)
        + jnp.dot(act_pair[...], other[...], preferred_element_type=F32)
    ).astype(BF16)


def finish_kernel(parts, hidden, out, total):
    step = pl.program_id(0)

    @pl.when(step == 0)
    def _():
        total[...] = hidden[...]

    total[...] += jnp.sum(parts[...].astype(F32), axis=0)

    @pl.when(step == pl.num_programs(0) - 1)
    def _():
        out[...] = total[...].astype(BF16)


def params():
    return pltpu.CompilerParams(vmem_limit_bytes=32 * 1024 * 1024)


def own_spec(units, chunk, n):
    return pl.BlockSpec((units, chunk), lambda i, place: (0, place[0] * n + i))


def other_spec(units, chunk):
    return pl.BlockSpec((units, chunk), lambda i, place: (0, i))


def gain_products(place, gain, own, other, n, chunk):
    units = own.shape[0]

    def body(place, gain, own, other, out):
        gain_kernel(gain, own, other, out.at[0])

    return pl.pallas_call(
        body,
        grid_spec=pltpu.PrefetchScalarGridSpec(
            num_scalar_prefetch=1,
            grid=(n,),
            in_specs=[
                pl.BlockSpec((1, chunk), lambda i, place: (0, place[0] * n + i)),
                own_spec(units, chunk, n),
                other_spec(units, chunk),
            ],
            out_specs=pl.BlockSpec((1, 2, 8, units), lambda i, place: (i, 0, 0, 0)),
        ),
        out_shape=jax.ShapeDtypeStruct((n, 2, 8, units), F32),
        compiler_params=params(),
    )(place, gain, own, other)


def up_project(place, rows, own, other, gain_own, gain_other):
    n, tokens, wide = rows.shape
    units = own.shape[0]
    chunk = wide - HD
    fixed = lambda i, place: (0, 0)
    turn = lambda i, place: (i, 0, 0)
    return pl.pallas_call(
        up_kernel,
        grid_spec=pltpu.PrefetchScalarGridSpec(
            num_scalar_prefetch=1,
            grid=(n,),
            in_specs=[
                pl.BlockSpec((1, tokens, wide), turn),
                own_spec(units, chunk, n),
                other_spec(units, chunk),
                pl.BlockSpec((1, 8, units), turn),
                pl.BlockSpec((1, 8, units), turn),
            ],
            out_specs=[
                pl.BlockSpec((tokens, units), fixed),
                pl.BlockSpec((tokens, units), fixed),
                pl.BlockSpec((tokens, HD), fixed),
            ],
        ),
        out_shape=(
            jax.ShapeDtypeStruct((tokens, units), F32),
            jax.ShapeDtypeStruct((tokens, units), F32),
            jax.ShapeDtypeStruct((tokens, HD), F32),
        ),
        compiler_params=params(),
    )(place, rows, own, other, gain_own, gain_other)


def down_project(place, act, act_pair, own, other, n, chunk):
    tokens, units = act.shape
    fixed = lambda i, place: (0, 0)
    return pl.pallas_call(
        down_kernel,
        grid_spec=pltpu.PrefetchScalarGridSpec(
            num_scalar_prefetch=1,
            grid=(n,),
            in_specs=[
                pl.BlockSpec((tokens, units), fixed),
                pl.BlockSpec((tokens, units), fixed),
                own_spec(units, chunk, n),
                other_spec(units, chunk),
            ],
            out_specs=pl.BlockSpec((1, tokens, chunk), lambda i, place: (i, 0, 0)),
        ),
        out_shape=jax.ShapeDtypeStruct((n, tokens, chunk), BF16),
        compiler_params=params(),
    )(place, act, act_pair, own, other)


def finish(parts, hidden):
    count, block, chunk = parts.shape
    per = count // 4
    return pl.pallas_call(
        finish_kernel,
        grid=(4,),
        in_specs=[
            pl.BlockSpec((per, block, chunk), lambda i: (i, 0, 0)),
            pl.BlockSpec((block, chunk), lambda i: (0, 0)),
        ],
        out_specs=pl.BlockSpec((block, chunk), lambda i: (0, 0)),
        out_shape=jax.ShapeDtypeStruct((block, chunk), BF16),
        scratch_shapes=[pltpu.VMEM((block, chunk), F32)],
        compiler_params=params(),
    )(parts, hidden)


def spread(x, axes, count):
    return lax.all_to_all(
        jnp.broadcast_to(x[None], (count,) + x.shape), axes, split_axis=0, concat_axis=0
    )


def exchange(x, axes):
    return lax.all_to_all(x, axes, split_axis=0, concat_axis=0)


def local(
    queries,
    keys_new,
    values_new,
    resid,
    tree_mask,
    tree_size,
    accepted,
    dest_slot,
    page_table,
    key_cache,
    value_cache,
    w_out,
    w_up,
    w_down,
    ln_gain,
):
    zs, cs, xs, ys = (lax.axis_size(a) for a in ALL)
    members = xs * ys
    groups = zs * cs
    z = lax.axis_index("z")
    c = lax.axis_index("c")
    member = lax.axis_index(MLP)
    rows_dev, width = queries.shape
    requests, tree_len = tree_mask.shape[:2]
    group_rows = requests * tree_len
    pages_dev, page_len, _ = key_cache.shape
    tokens = group_rows * groups
    heads = width // HD
    half = width // cs
    chunk = half // zs
    block = tokens // members

    wide_q = jnp.broadcast_to(queries[None], (members,) + queries.shape)
    group_q = exchange(wide_q, MLP).reshape(group_rows, width)

    def piece(w, core, d):
        return lax.dynamic_slice_in_dim(w, core * half + ((z + d) % zs) * chunk, chunk, 1)

    k_dev = w_out.shape[0]
    wo = after(w_out, group_q)
    wo_parts = []
    for d in range(zs):
        part = jnp.stack([piece(wo, c, d), piece(wo, 1 - c, d)])
        wo_parts.append(shift(part, d, zs) if d else part)
    wo_parts = jnp.concatenate(wo_parts, axis=1)

    both = after(jnp.concatenate([keys_new, values_new], axis=1), wide_q)
    both = jnp.stack([shift(both, d, xs, "x") if d else both for d in range(xs)])

    page_ids = member * pages_dev + jnp.arange(pages_dev, dtype=jnp.int32)
    owners = jnp.any(page_table[:, :, None] == page_ids[None, None, :], axis=1)
    pool_mask = jnp.repeat(jnp.repeat(owners, page_len, axis=1), tree_len, axis=0).astype(F32)
    draft_pad = 16
    slot_ids = member * rows_dev + jnp.arange(draft_pad, dtype=jnp.int32)
    row_ids = jnp.arange(group_rows, dtype=jnp.int32)
    tree_cols = jnp.tile(tree_mask.reshape(group_rows, tree_len), (1, requests))
    live = jnp.repeat(tree_size, tree_len) > (row_ids % tree_len)
    tree_ok = (
        (tree_cols == 1)
        & live[None, :]
        & ((row_ids // tree_len)[:, None] == (row_ids // tree_len)[None, :])
    ).astype(F32)
    pick = (row_ids[:, None] == slot_ids[None, :]) & (
        jnp.arange(draft_pad, dtype=jnp.int32) < rows_dev
    )[None, :]
    draft_mask = jnp.dot(tree_ok, pick.astype(F32))
    pad = ((0, draft_pad - rows_dev), (0, 0))
    parts = attend(
        group_q,
        key_cache,
        value_cache,
        jnp.pad(keys_new, pad),
        jnp.pad(values_new, pad),
        jnp.concatenate([pool_mask, draft_mask], axis=1),
        heads // 7,
    )

    parts, both = lax.optimization_barrier((parts, both))

    res = after(resid, parts)
    res = jnp.stack(
        [
            lax.dynamic_slice_in_dim(res, c * half, half, 1),
            pair(lax.dynamic_slice_in_dim(res, (1 - c) * half, half, 1)),
        ]
    ).reshape(cs * rows_dev, half)
    res_parts = []
    for d in range(zs):
        part = lax.dynamic_slice_in_dim(res, ((z + d) % zs) * chunk, chunk, 1)
        res_parts.append(shift(part, d, zs) if d else part)
    res = jnp.concatenate(res_parts, axis=0)
    at = jnp.arange(block, dtype=jnp.int32)
    source = ((z - at // (cs * rows_dev)) % zs) * cs + (c + at // rows_dev) % cs
    order = at[:, None] == (source * rows_dev + at % rows_dev)[None, :]
    res = jnp.dot(order.astype(BF16), res, preferred_element_type=F32)

    sent_parts = parts
    parts = exchange(parts.reshape(members, rows_dev, parts.shape[1]), MLP)
    parts = parts.reshape(members, rows_dev, heads // 7, 8, HD).astype(F32)
    st = parts[:, :, :, 7]
    tops, highs, lows = st[..., 0:7], st[..., 8:15], st[..., 16:23]
    scale = jnp.exp(tops - jnp.max(tops, axis=0, keepdims=True))
    total = jnp.sum(scale * (highs + lows), axis=0)
    weighted = jnp.sum(scale[..., None] * parts[:, :, :, :7], axis=0)
    attended = (weighted / total[..., None]).astype(BF16).reshape(rows_dev, width)

    feats = attended.reshape(rows_dev, zs, cs, members, k_dev).transpose(1, 2, 3, 0, 4)
    feats = jnp.stack(
        [
            jnp.concatenate([feats[(to - d) % zs] for d in range(zs)], axis=3)
            for to in range(zs)
        ]
    ).reshape(groups * members, rows_dev, zs * k_dev)
    far = shift(after(both, sent_parts), ys // 2, ys, "y")
    feats, far = lax.optimization_barrier((feats, far))
    both = after(both, feats)
    both = [far if d == ys // 2 else shift(both, d, ys, "y") if d else both for d in range(ys)]
    feats, both = lax.optimization_barrier((exchange(feats, ALL), both))
    feats = (
        feats.reshape(groups, members, rows_dev, zs * k_dev)
        .transpose(1, 0, 2, 3)
        .reshape(tokens, zs * k_dev)
    )
    wo_own, wo_pair = wo_parts[0], wo_parts[1]
    sent = pair(jnp.dot(feats, wo_pair, preferred_element_type=F32).astype(BF16))
    part = jnp.dot(feats, wo_own, preferred_element_type=F32) + sent.astype(F32)
    part = exchange(part.astype(BF16).reshape(members, block, chunk), MLP)
    gain = lax.dynamic_slice_in_dim(ln_gain, c * half + z * chunk, chunk, 0)

    hidden, row = pl.pallas_call(
        hidden_kernel,
        out_shape=(
            jax.ShapeDtypeStruct((block, chunk), F32),
            jax.ShapeDtypeStruct((block, chunk + HD), BF16),
        ),
        compiler_params=params(),
    )(part, res, gain[None])

    place = c.reshape(1).astype(jnp.int32)
    up_w = w_up.T
    up_other = pair(lax.dynamic_slice_in_dim(after(up_w, row), (1 - c) * half, half, 1))
    down_other = pair(lax.dynamic_slice_in_dim(after(w_down, row), (1 - c) * half, half, 1))
    gw = gain_products(place, ln_gain[None], up_w, up_other, zs, chunk)
    gain_own = gw[:, 0]
    gain_other = gw[:, 1]
    gain_pair = pair(gain_other)

    rows = spread(row, CHIPS, zs * members).reshape(zs, tokens, chunk + HD)
    mine, theirs, stats = up_project(place, rows, up_w, up_other, gain_own, gain_other)
    act = pl.pallas_call(
        lambda *refs: act_kernel(width, *refs),
        out_shape=jax.ShapeDtypeStruct(mine.shape, BF16),
        compiler_params=params(),
    )(mine, pair(theirs), stats, pair(stats), gain_own, gain_pair)
    down = down_project(place, act, pair(act), w_down, down_other, zs, chunk)
    down = exchange(down.reshape(zs * members, block, chunk), CHIPS)
    mixed = finish(down, hidden)
    mixed = exchange(mixed.reshape(groups, rows_dev, chunk), REQ)
    mixed = mixed.reshape(zs, cs, rows_dev, chunk).transpose(2, 1, 0, 3).reshape(rows_dev, width)

    valid = (accepted >= 0) & (dest_slot == member)[:, None]
    target = jnp.arange(requests, dtype=jnp.int32)[:, None] * tree_len + jnp.maximum(accepted, 0)
    x, y = lax.axis_index("x"), lax.axis_index("y")
    at = jnp.arange(group_rows, dtype=jnp.int32)
    near = at // rows_dev
    slots = (((x - near % xs) % xs) * ys + (y - near // xs) % ys) * rows_dev + at % rows_dev
    chooser = jnp.any((target[:, :, None] == slots[None, None, :]) & valid[:, :, None], axis=0)
    both = jnp.stack(both).reshape(group_rows, 2 * width)
    picked = jnp.dot(chooser.astype(BF16), both, preferred_element_type=F32).astype(BF16)
    return (mixed, picked[:, :width][None], picked[:, width:][None])


def solution(mesh):
    groups, members = mesh.devices.shape
    side = math.isqrt(members)
    fine = Mesh(mesh.devices.reshape(groups // 2, 2, side, side), ALL)
    rows = P(ALL, None)
    pages = P(ALL, None, None)
    in_specs = (
        rows,
        rows,
        rows,
        rows,
        P(REQ, None, None),
        P(REQ),
        P(REQ, None),
        P(REQ),
        P(REQ, None),
        pages,
        pages,
        rows,
        P(None, ALL),
        rows,
        P(),
    )
    return jax.shard_map(
        local, mesh=fine, in_specs=in_specs, out_specs=(rows, pages, pages), check_vma=False
    )
```

```python
import math

import jax
import jax.numpy as jnp
from jax import lax
from jax.experimental import pallas as pl
from jax.experimental.pallas import tpu as pltpu
from jax.sharding import Mesh, PartitionSpec as P

HD = 128
NEG = -(2.0**100)
F32 = jnp.float32
BF16 = jnp.bfloat16
ALL = ("z", "c", "x", "y")
REQ = ("z", "c")
MLP = ("x", "y")
CHIPS = ("z", "x", "y")
DN = (((1,), (1,)), ((), ()))


def attend_kernel(heads, scaling, q, k, v, dk, dv, mask, out):
    rows = q.shape[0]
    keys = k.shape[0] * k.shape[1]
    kk = jnp.concatenate([k[...].reshape(keys, k.shape[2]), dk[...]], axis=0)
    vv = jnp.concatenate([v[...].reshape(keys, v.shape[2]), dv[...]], axis=0)
    m = mask[...]
    span = [slice(h * HD, (h + 1) * HD) for h in range(heads)]
    scores = [
        jnp.where(
            m > 0,
            lax.dot_general(q[:, cols], kk[:, cols], DN, preferred_element_type=F32) * scaling,
            NEG,
        )
        for cols in span
    ]
    tops = [jnp.max(s, axis=1, keepdims=True).astype(BF16).astype(F32) for s in scores]
    weights = [jnp.exp(s - top) * m for s, top in zip(scores, tops)]
    totals = [jnp.sum(p, axis=1, keepdims=True) for p in weights]
    lane = lax.broadcasted_iota(jnp.int32, (rows, HD), 1)
    stats = jnp.zeros((rows, HD), F32)
    for h, cols in enumerate(span):
        w = jnp.dot(weights[h].astype(BF16), vv[:, cols], preferred_element_type=F32)
        out[:, cols] = w.astype(BF16)
        high = totals[h].astype(BF16).astype(F32)
        stats = jnp.where(lane == h, tops[h], stats)
        stats = jnp.where(lane == 8 + h, high, stats)
        stats = jnp.where(lane == 16 + h, totals[h] - high, stats)
    out[:, heads * HD :] = stats.astype(BF16)


def attend(q, key_cache, value_cache, dk, dv, mask, steps):
    rows, width = q.shape
    pages, page_len, _ = key_cache.shape
    wide = width // steps
    heads = wide // HD
    col = lambda i: (0, i)
    col3 = lambda i: (0, 0, i)

    def body(*refs):
        attend_kernel(heads, 1.0 / math.sqrt(HD), *refs)

    return pl.pallas_call(
        body,
        grid=(steps,),
        in_specs=[
            pl.BlockSpec((rows, wide), col),
            pl.BlockSpec((pages, page_len, wide), col3),
            pl.BlockSpec((pages, page_len, wide), col3),
            pl.BlockSpec((dk.shape[0], wide), col),
            pl.BlockSpec((dv.shape[0], wide), col),
            pl.BlockSpec(mask.shape, lambda i: (0, 0)),
        ],
        out_specs=pl.BlockSpec((rows, wide + HD), col),
        out_shape=jax.ShapeDtypeStruct((rows, steps * (wide + HD)), BF16),
        compiler_params=pltpu.CompilerParams(vmem_limit_bytes=58 * 1024 * 1024),
        cost_estimate=pl.CostEstimate(
            flops=4 * rows * pages * page_len * width,
            bytes_accessed=4 * pages * page_len * width,
            transcendentals=rows * pages * page_len * width // HD,
        ),
    )(q, key_cache, value_cache, dk, dv, mask)


def pair(x):
    return lax.ppermute(x, "c", [(0, 1), (1, 0)])


def shift(x, step, size, axis="z"):
    return lax.ppermute(x, axis, [(i, (i + step) % size) for i in range(size)])


def after(x, first):
    return lax.optimization_barrier((x, first))[0]


def gain_kernel(gain, own, other, out):
    high = gain[...].astype(BF16).astype(F32)
    row = lax.broadcasted_iota(jnp.int32, (8, gain.shape[1]), 0)
    low = gain[...] - high
    both = jnp.where(row == 0, high, jnp.where(row == 1, low, 0.0)).astype(BF16)
    for e, w in enumerate((own, other)):
        out[e] = lax.dot_general(both, w[...], DN, preferred_element_type=F32)


def hidden_kernel(parts, res, gain, hidden_out, row_out):
    hidden = res[...] + jnp.sum(parts[...].astype(F32), axis=0)
    hidden_out[...] = hidden
    rows, chunk = hidden.shape
    mean = jnp.mean(hidden, axis=1, keepdims=True)
    centered = hidden - mean
    dev = jnp.sum(centered * centered, axis=1, keepdims=True)
    row_out[:, :chunk] = (centered * gain[...]).astype(BF16)
    lane = lax.broadcasted_iota(jnp.int32, (rows, HD), 1)
    stats = jnp.zeros((rows, HD), F32)
    at = 0
    for value in (mean, dev):
        for _ in range(3):
            high = value.astype(BF16).astype(F32)
            stats = jnp.where(lane == at, high, stats)
            value = value - high
            at += 1
    row_out[:, chunk:] = stats.astype(BF16)


def up_kernel(place, rows, own, other, gain_own, gain_other, mine, theirs, stats_out):
    step = pl.program_id(0)
    chunk = own.shape[1]
    g = rows[0, :, :chunk]
    st = rows[0, :, chunk:].astype(F32)
    mean = st[:, 0:1] + st[:, 1:2] + st[:, 2:3]
    dev = st[:, 3:4] + st[:, 4:5] + st[:, 5:6]
    lane = lax.broadcasted_iota(jnp.int32, st.shape, 1)
    stats = jnp.where(lane == step, mean, 0.0) + jnp.where(lane == 8, dev, 0.0)

    @pl.when(step == 0)
    def _():
        mine[...] = jnp.zeros_like(mine)
        theirs[...] = jnp.zeros_like(theirs)
        stats_out[...] = jnp.zeros_like(stats_out)

    stats_out[...] += stats
    for w, gw, out in ((own, gain_own, mine), (other, gain_other, theirs)):
        term = lax.dot_general(g, w[...], DN, preferred_element_type=F32)
        out[...] += term + mean * (gw[0, 0:1, :] + gw[0, 1:2, :])


def act_kernel(width, mine, theirs, stats, stats_pair, gain_own, gain_pair, out):
    n = gain_own.shape[0]
    a = stats[...]
    b = stats_pair[...]
    lane = lax.broadcasted_iota(jnp.int32, a.shape, 1)
    chunk = width // (2 * n)
    mean = (
        jnp.sum(jnp.where(lane < n, a, 0.0), axis=1, keepdims=True)
        + jnp.sum(jnp.where(lane < n, b, 0.0), axis=1, keepdims=True)
    ) / (2 * n)

    def spread_of(v):
        part = jnp.where(lane < n, chunk * jnp.square(v - mean), jnp.where(lane == 8, v, 0.0))
        return jnp.sum(part, axis=1, keepdims=True)

    inv = lax.rsqrt((spread_of(a) + spread_of(b)) / width + 1e-05)
    gw = jnp.zeros((1, out.shape[1]), F32)
    for k in range(n):
        for ref in (gain_own, gain_pair):
            gw = gw + ref[k, 0:1, :] + ref[k, 1:2, :]
    pre = inv * (mine[...] + theirs[...] - mean * gw)
    out[...] = jnp.maximum(pre, 0.0).astype(BF16)


def down_kernel(place, act, act_pair, own, other, out):
    out[0] = (
        jnp.dot(act[...], own[...], preferred_element_type=F32)
        + jnp.dot(act_pair[...], other[...], preferred_element_type=F32)
    ).astype(BF16)


def finish_kernel(parts, hidden, out, total):
    step = pl.program_id(0)

    @pl.when(step == 0)
    def _():
        total[...] = hidden[...]

    total[...] += jnp.sum(parts[...].astype(F32), axis=0)

    @pl.when(step == pl.num_programs(0) - 1)
    def _():
        out[...] = total[...].astype(BF16)


def params():
    return pltpu.CompilerParams(vmem_limit_bytes=32 * 1024 * 1024)


def own_spec(units, chunk, n):
    return pl.BlockSpec((units, chunk), lambda i, place: (0, place[0] * n + i))


def other_spec(units, chunk):
    return pl.BlockSpec((units, chunk), lambda i, place: (0, i))


def gain_products(place, gain, own, other, n, chunk):
    units = own.shape[0]

    def body(place, gain, own, other, out):
        gain_kernel(gain, own, other, out.at[0])

    return pl.pallas_call(
        body,
        grid_spec=pltpu.PrefetchScalarGridSpec(
            num_scalar_prefetch=1,
            grid=(n,),
            in_specs=[
                pl.BlockSpec((1, chunk), lambda i, place: (0, place[0] * n + i)),
                own_spec(units, chunk, n),
                other_spec(units, chunk),
            ],
            out_specs=pl.BlockSpec((1, 2, 8, units), lambda i, place: (i, 0, 0, 0)),
        ),
        out_shape=jax.ShapeDtypeStruct((n, 2, 8, units), F32),
        compiler_params=params(),
    )(place, gain, own, other)


def up_project(place, rows, own, other, gain_own, gain_other):
    n, tokens, wide = rows.shape
    units = own.shape[0]
    chunk = wide - HD
    fixed = lambda i, place: (0, 0)
    turn = lambda i, place: (i, 0, 0)
    return pl.pallas_call(
        up_kernel,
        grid_spec=pltpu.PrefetchScalarGridSpec(
            num_scalar_prefetch=1,
            grid=(n,),
            in_specs=[
                pl.BlockSpec((1, tokens, wide), turn),
                own_spec(units, chunk, n),
                other_spec(units, chunk),
                pl.BlockSpec((1, 8, units), turn),
                pl.BlockSpec((1, 8, units), turn),
            ],
            out_specs=[
                pl.BlockSpec((tokens, units), fixed),
                pl.BlockSpec((tokens, units), fixed),
                pl.BlockSpec((tokens, HD), fixed),
            ],
        ),
        out_shape=(
            jax.ShapeDtypeStruct((tokens, units), F32),
            jax.ShapeDtypeStruct((tokens, units), F32),
            jax.ShapeDtypeStruct((tokens, HD), F32),
        ),
        compiler_params=params(),
    )(place, rows, own, other, gain_own, gain_other)


def down_project(place, act, act_pair, own, other, n, chunk):
    tokens, units = act.shape
    fixed = lambda i, place: (0, 0)
    return pl.pallas_call(
        down_kernel,
        grid_spec=pltpu.PrefetchScalarGridSpec(
            num_scalar_prefetch=1,
            grid=(n,),
            in_specs=[
                pl.BlockSpec((tokens, units), fixed),
                pl.BlockSpec((tokens, units), fixed),
                own_spec(units, chunk, n),
                other_spec(units, chunk),
            ],
            out_specs=pl.BlockSpec((1, tokens, chunk), lambda i, place: (i, 0, 0)),
        ),
        out_shape=jax.ShapeDtypeStruct((n, tokens, chunk), BF16),
        compiler_params=params(),
    )(place, act, act_pair, own, other)


def finish(parts, hidden):
    count, block, chunk = parts.shape
    per = count // 4
    return pl.pallas_call(
        finish_kernel,
        grid=(4,),
        in_specs=[
            pl.BlockSpec((per, block, chunk), lambda i: (i, 0, 0)),
            pl.BlockSpec((block, chunk), lambda i: (0, 0)),
        ],
        out_specs=pl.BlockSpec((block, chunk), lambda i: (0, 0)),
        out_shape=jax.ShapeDtypeStruct((block, chunk), BF16),
        scratch_shapes=[pltpu.VMEM((block, chunk), F32)],
        compiler_params=params(),
    )(parts, hidden)


def spread(x, axes, count):
    return lax.all_to_all(
        jnp.broadcast_to(x[None], (count,) + x.shape), axes, split_axis=0, concat_axis=0
    )


def exchange(x, axes):
    return lax.all_to_all(x, axes, split_axis=0, concat_axis=0)


def local(
    queries,
    keys_new,
    values_new,
    resid,
    tree_mask,
    tree_size,
    accepted,
    dest_slot,
    page_table,
    key_cache,
    value_cache,
    w_out,
    w_up,
    w_down,
    ln_gain,
):
    zs, cs, xs, ys = (lax.axis_size(a) for a in ALL)
    members = xs * ys
    groups = zs * cs
    z = lax.axis_index("z")
    c = lax.axis_index("c")
    member = lax.axis_index(MLP)
    rows_dev, width = queries.shape
    requests, tree_len = tree_mask.shape[:2]
    group_rows = requests * tree_len
    pages_dev, page_len, _ = key_cache.shape
    tokens = group_rows * groups
    heads = width // HD
    half = width // cs
    chunk = half // zs
    block = tokens // members

    wide_q = jnp.broadcast_to(queries[None], (members,) + queries.shape)
    group_q = exchange(wide_q, MLP).reshape(group_rows, width)

    def piece(w, core, d):
        return lax.dynamic_slice_in_dim(w, core * half + ((z + d) % zs) * chunk, chunk, 1)

    k_dev = w_out.shape[0]
    wo = after(w_out, group_q)
    wo_parts = []
    for d in range(zs):
        part = jnp.stack([piece(wo, c, d), piece(wo, 1 - c, d)])
        wo_parts.append(shift(part, d, zs) if d else part)
    wo_parts = jnp.concatenate(wo_parts, axis=1)

    both = after(jnp.concatenate([keys_new, values_new], axis=1), wide_q)
    both = jnp.stack([shift(both, d, xs, "x") if d else both for d in range(xs)])

    page_ids = member * pages_dev + jnp.arange(pages_dev, dtype=jnp.int32)
    owners = jnp.any(page_table[:, :, None] == page_ids[None, None, :], axis=1)
    pool_mask = jnp.repeat(jnp.repeat(owners, page_len, axis=1), tree_len, axis=0).astype(F32)
    draft_pad = 16
    slot_ids = member * rows_dev + jnp.arange(draft_pad, dtype=jnp.int32)
    row_ids = jnp.arange(group_rows, dtype=jnp.int32)
    tree_cols = jnp.tile(tree_mask.reshape(group_rows, tree_len), (1, requests))
    live = jnp.repeat(tree_size, tree_len) > (row_ids % tree_len)
    tree_ok = (
        (tree_cols == 1)
        & live[None, :]
        & ((row_ids // tree_len)[:, None] == (row_ids // tree_len)[None, :])
    ).astype(F32)
    pick = (row_ids[:, None] == slot_ids[None, :]) & (
        jnp.arange(draft_pad, dtype=jnp.int32) < rows_dev
    )[None, :]
    draft_mask = jnp.dot(tree_ok, pick.astype(F32))
    pad = ((0, draft_pad - rows_dev), (0, 0))
    parts = attend(
        group_q,
        key_cache,
        value_cache,
        jnp.pad(keys_new, pad),
        jnp.pad(values_new, pad),
        jnp.concatenate([pool_mask, draft_mask], axis=1),
        heads // 7,
    )

    far = shift(both, ys // 2, ys, "y")
    parts, both, far = lax.optimization_barrier((parts, both, far))
    both = [far if d == ys // 2 else shift(both, d, ys, "y") if d else both for d in range(ys)]

    res = after(resid, parts)
    res = jnp.stack(
        [
            lax.dynamic_slice_in_dim(res, c * half, half, 1),
            pair(lax.dynamic_slice_in_dim(res, (1 - c) * half, half, 1)),
        ]
    ).reshape(cs * rows_dev, half)
    res_parts = []
    for d in range(zs):
        part = lax.dynamic_slice_in_dim(res, ((z + d) % zs) * chunk, chunk, 1)
        res_parts.append(shift(part, d, zs) if d else part)
    res = jnp.concatenate(res_parts, axis=0)
    at = jnp.arange(block, dtype=jnp.int32)
    source = ((z - at // (cs * rows_dev)) % zs) * cs + (c + at // rows_dev) % cs
    order = at[:, None] == (source * rows_dev + at % rows_dev)[None, :]
    res = jnp.dot(order.astype(BF16), res, preferred_element_type=F32)

    parts = exchange(parts.reshape(members, rows_dev, parts.shape[1]), MLP)
    parts = parts.reshape(members, rows_dev, heads // 7, 8, HD).astype(F32)
    st = parts[:, :, :, 7]
    tops, highs, lows = st[..., 0:7], st[..., 8:15], st[..., 16:23]
    scale = jnp.exp(tops - jnp.max(tops, axis=0, keepdims=True))
    total = jnp.sum(scale * (highs + lows), axis=0)
    weighted = jnp.sum(scale[..., None] * parts[:, :, :, :7], axis=0)
    attended = (weighted / total[..., None]).astype(BF16).reshape(rows_dev, width)

    feats = attended.reshape(rows_dev, zs, cs, members, k_dev).transpose(1, 2, 3, 0, 4)
    feats = jnp.stack(
        [
            jnp.concatenate([feats[(to - d) % zs] for d in range(zs)], axis=3)
            for to in range(zs)
        ]
    ).reshape(groups * members, rows_dev, zs * k_dev)
    feats, both = lax.optimization_barrier((feats, both))
    feats = exchange(feats, ALL)
    feats = (
        feats.reshape(groups, members, rows_dev, zs * k_dev)
        .transpose(1, 0, 2, 3)
        .reshape(tokens, zs * k_dev)
    )
    wo_own, wo_pair = wo_parts[0], wo_parts[1]
    sent = pair(jnp.dot(feats, wo_pair, preferred_element_type=F32).astype(BF16))
    part = jnp.dot(feats, wo_own, preferred_element_type=F32) + sent.astype(F32)
    part = exchange(part.astype(BF16).reshape(members, block, chunk), MLP)
    gain = lax.dynamic_slice_in_dim(ln_gain, c * half + z * chunk, chunk, 0)

    hidden, row = pl.pallas_call(
        hidden_kernel,
        out_shape=(
            jax.ShapeDtypeStruct((block, chunk), F32),
            jax.ShapeDtypeStruct((block, chunk + HD), BF16),
        ),
        compiler_params=params(),
    )(part, res, gain[None])

    place = c.reshape(1).astype(jnp.int32)
    up_w = w_up.T
    up_other = pair(lax.dynamic_slice_in_dim(after(up_w, row), (1 - c) * half, half, 1))
    down_other = pair(lax.dynamic_slice_in_dim(after(w_down, row), (1 - c) * half, half, 1))
    gw = gain_products(place, ln_gain[None], up_w, up_other, zs, chunk)
    gain_own = gw[:, 0]
    gain_other = gw[:, 1]
    gain_pair = pair(gain_other)

    rows = spread(row, CHIPS, zs * members).reshape(zs, tokens, chunk + HD)
    mine, theirs, stats = up_project(place, rows, up_w, up_other, gain_own, gain_other)
    act = pl.pallas_call(
        lambda *refs: act_kernel(width, *refs),
        out_shape=jax.ShapeDtypeStruct(mine.shape, BF16),
        compiler_params=params(),
    )(mine, pair(theirs), stats, pair(stats), gain_own, gain_pair)
    down = down_project(place, act, pair(act), w_down, down_other, zs, chunk)
    down = exchange(down.reshape(zs * members, block, chunk), CHIPS)
    mixed = finish(down, hidden)
    mixed = exchange(mixed.reshape(groups, rows_dev, chunk), REQ)
    mixed = mixed.reshape(zs, cs, rows_dev, chunk).transpose(2, 1, 0, 3).reshape(rows_dev, width)

    valid = (accepted >= 0) & (dest_slot == member)[:, None]
    target = jnp.arange(requests, dtype=jnp.int32)[:, None] * tree_len + jnp.maximum(accepted, 0)
    x, y = lax.axis_index("x"), lax.axis_index("y")
    at = jnp.arange(group_rows, dtype=jnp.int32)
    near = at // rows_dev
    slots = (((x - near % xs) % xs) * ys + (y - near // xs) % ys) * rows_dev + at % rows_dev
    chooser = jnp.any((target[:, :, None] == slots[None, None, :]) & valid[:, :, None], axis=0)
    both = jnp.stack(both).reshape(group_rows, 2 * width)
    picked = jnp.dot(chooser.astype(BF16), both, preferred_element_type=F32).astype(BF16)
    return (mixed, picked[:, :width][None], picked[:, width:][None])


def solution(mesh):
    groups, members = mesh.devices.shape
    side = math.isqrt(members)
    fine = Mesh(mesh.devices.reshape(groups // 2, 2, side, side), ALL)
    rows = P(ALL, None)
    pages = P(ALL, None, None)
    in_specs = (
        rows,
        rows,
        rows,
        rows,
        P(REQ, None, None),
        P(REQ),
        P(REQ, None),
        P(REQ),
        P(REQ, None),
        pages,
        pages,
        rows,
        P(None, ALL),
        rows,
        P(),
    )
    return jax.shard_map(
        local, mesh=fine, in_specs=in_specs, out_specs=(rows, pages, pages), check_vma=False
    )
```
